32 devices in a mesh: section: 2 (over core), expert: 16 (over z, y, x).
Axes of the slice: x: 2, y: 2, z: 4, core: 2. Of those that a mesh axis runs over, the one named last changes fastest.
Arguments:
- layer_in: bfloat16 [2, 2048, 5120], P('section', 'expert'), may hold values from -50 to 50
- memory: bfloat16 [2, 128, 2, 5120], P('section', 'expert'), may hold values from -80 to 80
- cotangent: bfloat16 [2, 2048, 5120], P('section', 'expert'), may hold values from -6 to 6
- norm_gain: float32 [2, 5120], P('section'), may hold values from 0.5 to 1.5
- attn_gain: float32 [2, 5120], P('section'), may hold values from 0.5 to 1.5
- expert_in: bfloat16 [2, 5120, 10240], P('section', None, 'expert'), may hold values from -0.078125 to 0.078125
- expert_out: bfloat16 [2, 10240, 5120], P('section', 'expert'), may hold values from -0.0625 to 0.0625
- slot_index: int32 [2, 2048], P('section', 'expert'), may hold values from -1 to 7, as said below
- gate_prob: float32 [2, 2048], P('section', 'expert'), may hold values from 0.2 to 1
Outputs:
- layer_out: bfloat16 [2, 2048, 5120], P('section', 'expert')
- arriving: bfloat16 [2, 2048, 5120], P('section', 'expert')
- grad_memory: float32 [2, 128, 2, 5120], P('section', 'expert')
The draws below stay inside these ranges and needn't reach their ends.
Inputs may be any that keep to these rules, and one draw needn't show every extreme that they name: `slot_index`: within each aligned block of 128 tokens of a layer the slots used are 0 to that block's count minus 1, each once; counts lie between 8 // 3 (at least 1) and 8, and every layer has a block with all 8 slots used.
All inputs are finite; a program needn't handle non-finite values.
Results may differ from the reference program's by a relative error of at most 0.0049.
The reference program's roundings to bfloat16 on the way (of `queries`, `residual`, `normed`, `capacity` and `hidden`) count: a program that leaves them out, or rounds other values in their place, can miss the bound.
Values may be sent and summed in bfloat16 or wider, within the bound.
No kernel may reach another device: no remote copies, remote signals or barrier semaphores. Data moves between devices by JAX's collectives and lax.ppermute only.
A program may use at most 128 MiB of HBM per device.

```python
import jax
import jax.numpy as jnp
from jax import lax

D = 5120
HD = 128
FFW = 10240
TOK_DEV = 128
MEM = 128
CAP = 8
LAYERS = 2
TOKENS = 2048


def draw_memory(key, part):
    key = jax.random.fold_in(key, 11)
    key_draw = jax.random.fold_in(key, 3)
    value_draw = jax.random.fold_in(key, 4)
    keys = jnp.clip(jax.random.normal(key_draw, (LAYERS, MEM, D), jnp.float32), -4.0, 4.0)
    values = jnp.clip(jax.random.normal(value_draw, (LAYERS, MEM, D), jnp.float32), -4.0, 4.0)
    return jnp.stack([keys, values], axis=2).astype(jnp.bfloat16)


def draw_layer_in(key, part):
    key = jax.random.fold_in(key, 23)
    base = jnp.clip(jax.random.normal(key, (LAYERS, TOKENS, D), jnp.float32), -5.0, 5.0)
    return base.astype(jnp.bfloat16)


def draw_slot_index(key, part):
    key = jax.random.fold_in(key, 37)
    groups = TOKENS // TOK_DEV
    count_key, full_key, order_key = jax.random.split(key, 3)
    counts = jax.random.randint(count_key, (LAYERS, groups), max(CAP // 3, 1), CAP + 1)
    full_at = jax.random.randint(full_key, (LAYERS,), 0, groups)
    counts = jnp.where(jnp.arange(groups, dtype=jnp.int32)[None, :] == full_at[:, None], CAP, counts)
    order_keys = jax.random.split(order_key, LAYERS * groups)
    ranks = jax.vmap(lambda single: jax.random.permutation(single, TOK_DEV))(order_keys)
    ranks = ranks.reshape(LAYERS, groups, TOK_DEV).astype(jnp.int32)
    chosen = jnp.where(ranks < counts[:, :, None], ranks, -1)
    return chosen.reshape(LAYERS, TOKENS).astype(jnp.int32)


def steps_of(rng, shape, cuts, low, top_value):
    def one(axis_at, shards_of):
        heights = jax.random.uniform(jax.random.fold_in(jax.random.fold_in(rng, 6), axis_at), (shards_of,), jnp.float32, low / len(cuts), top_value / len(cuts))
        return jnp.repeat(jnp.exp(heights), shape[axis_at] // shards_of).reshape((-1,) + (1,) * (len(shape) - axis_at - 1))

    factor_of = one(*cuts[0])
    for cut in cuts[1:]:
        factor_of = factor_of * one(*cut)
    return factor_of


def bell_draw(stream_key, dims, scale, bound, pieces=(), held_as=jnp.bfloat16):
    values = jax.random.normal(stream_key, dims, jnp.float32) * scale
    if len(pieces) > 0:
        values = steps_of(stream_key, dims, pieces, -0.22, 0.18) * values
    return jnp.clip(values, min=-bound, max=bound).astype(held_as)


def setup_inputs(seed: int = 0) -> dict:
    key_list = jax.random.split(jax.random.key(seed), 10)
    layer_in = draw_layer_in(jax.random.fold_in(key_list[9], 71), 0)
    memory = draw_memory(jax.random.fold_in(key_list[9], 71), 0)
    cotangent = bell_draw(key_list[2], (LAYERS, TOKENS, D), 1.0, 6.0, ((0, 2), (1, 16)))
    norm_gain = jnp.clip(1.0 + 0.1 * jax.random.normal(key_list[3], (LAYERS, D), jnp.float32), 0.5, 1.5)
    attn_gain = jnp.clip(1.0 + 0.1 * jax.random.normal(key_list[4], (LAYERS, D), jnp.float32), 0.5, 1.5)
    expert_in = bell_draw(key_list[5], (LAYERS, D, FFW), D ** -0.5, 0.078125, ((0, 2), (2, 16)))
    expert_out = bell_draw(key_list[6], (LAYERS, FFW, D), FFW ** -0.5, 0.0625, ((0, 2), (1, 16)))
    slot_index = draw_slot_index(jax.random.fold_in(key_list[9], 71), 0)
    gate_prob = jnp.clip(0.2 + 0.8 * jax.random.uniform(key_list[8], (LAYERS, TOKENS), jnp.float32) ** steps_of(key_list[8], (LAYERS, TOKENS), ((0, 2), (1, 16)), -0.2, 0.2), 0.2, 1.0)
    return dict(layer_in=layer_in, memory=memory, cotangent=cotangent, norm_gain=norm_gain, attn_gain=attn_gain, expert_in=expert_in, expert_out=expert_out, slot_index=slot_index, gate_prob=gate_prob)


def rms_scale(values, scale_row):
    return values * lax.rsqrt(lax.optimization_barrier(jnp.mean(values * values, axis=-1, keepdims=True)) + 1e-06) * scale_row

def attend_grad(queries, keys, values, upstream):
    query_rows = queries.shape[0]
    source_rows = keys.shape[0]
    per_head_queries = queries.reshape(query_rows, -1, HD)
    per_head_keys = keys.reshape(source_rows, -1, HD)
    per_head_values = values.reshape(source_rows, -1, HD)
    incoming_head_gradient = upstream.reshape(query_rows, -1, HD)
    scaling_factor = HD ** (-0.5)
    attention_scores = jnp.einsum('ksu,lsu->skl', per_head_queries, per_head_keys, preferred_element_type=jnp.float32) * scaling_factor
    highest = lax.optimization_barrier(jnp.max(attention_scores, axis=-1, keepdims=True))
    weights = jnp.exp(attention_scores - highest)
    weights = weights / lax.optimization_barrier(jnp.sum(weights, axis=-1, keepdims=True))
    rounded_down = weights.astype(jnp.bfloat16)
    expert_mixture = jnp.einsum('cif,fcv->icv', rounded_down, per_head_values, preferred_element_type=jnp.float32)
    value_gradient_rows = jnp.einsum('yfg,fyb->gyb', rounded_down, incoming_head_gradient, preferred_element_type=jnp.float32)
    probability_gradient = jnp.einsum('ksu,lsu->skl', incoming_head_gradient, per_head_values, preferred_element_type=jnp.float32)
    dscore = weights * (probability_gradient - lax.optimization_barrier(jnp.sum(probability_gradient * weights, axis=-1, keepdims=True))) * scaling_factor
    upper_limit = dscore.astype(jnp.bfloat16)
    lower_limit = (dscore - upper_limit.astype(jnp.float32)).astype(jnp.bfloat16)
    key_gradient_rows = jnp.einsum('yfg,fyb->gyb', upper_limit, per_head_queries, preferred_element_type=jnp.float32)
    key_gradient_rows = key_gradient_rows + jnp.einsum('yfg,fyb->gyb', lower_limit, per_head_queries, preferred_element_type=jnp.float32)
    stacked = jnp.stack([key_gradient_rows.reshape(source_rows, -1), value_gradient_rows.reshape(source_rows, -1)], axis=1)
    return (expert_mixture.reshape(query_rows, -1), stacked)

def reference(layer_in, memory, cotangent, norm_gain, attn_gain, expert_in, expert_out, slot_index, gate_prob):
    groups = TOKENS // TOK_DEV
    produced = []
    grads = []
    for section_number in range(LAYERS):
        current = layer_in[section_number].astype(jnp.float32)
        if section_number >= LAYERS // 2:
            queries = rms_scale(current, attn_gain[section_number]).astype(jnp.bfloat16)
            expert_mixture, grad_part = attend_grad(queries, memory[section_number, :, 0], memory[section_number, :, 1], cotangent[section_number])
            grads.append(grad_part)
            residual = (current + expert_mixture).astype(jnp.bfloat16)
        else:
            grads.append(jnp.zeros((MEM, 2, D), jnp.float32))
            residual = layer_in[section_number]
        normed = rms_scale(residual.astype(jnp.float32), norm_gain[section_number]).astype(jnp.bfloat16)
        onehot = slot_index[section_number].reshape(groups, 1, TOK_DEV) == jnp.arange(CAP, dtype=jnp.int32).reshape(1, CAP, 1)
        capacity = jnp.einsum('gct,gtd->gcd', onehot.astype(jnp.bfloat16), normed.reshape(groups, TOK_DEV, D), preferred_element_type=jnp.float32)
        capacity = capacity.astype(jnp.bfloat16).reshape(groups * CAP, D)
        hidden = jax.nn.gelu(jnp.dot(capacity, expert_in[section_number], preferred_element_type=jnp.float32)).astype(jnp.bfloat16)
        computed = jnp.dot(hidden, expert_out[section_number], preferred_element_type=jnp.float32)
        combined = jnp.einsum('gct,gcd->gtd', onehot.astype(jnp.float32), computed.reshape(groups, CAP, D), precision=lax.Precision.HIGHEST).reshape(TOKENS, D)
        produced.append((residual.astype(jnp.float32) + gate_prob[section_number][:, None] * combined).astype(jnp.bfloat16))
    layer_out = jnp.stack(produced)
    arriving = jnp.concatenate([jnp.zeros_like(layer_out[:1]), layer_out[:-1]], axis=0)
    return (layer_out, arriving, jnp.stack(grads))
```

```python
import functools

import jax
import jax.numpy as jnp
from jax import lax
from jax.experimental import pallas as pl
from jax.experimental.pallas import tpu as pltpu
from jax.sharding import PartitionSpec as P

HD = 128
CAP = 8


def passed_along(block, axis, distance):
    devices = range(lax.axis_size(axis))
    route = [(i - distance, i) for i in devices if i - distance in devices]
    return lax.ppermute(block, axis, route)


def swapped(block):
    sections = lax.axis_size("section")
    return lax.ppermute(block, "section", [(i, (i + sections // 2) % sections) for i in range(sections)])


def partner(position, distance, size):
    return position ^ distance if size & (size - 1) == 0 else (position + distance) % size


class Grid:
    def __init__(self, size):
        a = 4 if size % 4 == 0 else 1
        c = 2 if (size // a) % 2 == 0 else 1
        self.sizes = (a, size // a // c, c)
        self.size = size

    def shift(self, block, by, back=False):
        sizes = self.sizes
        route = []
        for index in range(self.size):
            at = (index // (sizes[1] * sizes[2]), index // sizes[2] % sizes[1], index % sizes[2])
            to = [partner(p, d, n) for p, d, n in zip(at, by, sizes)]
            route.append((index, (to[0] * sizes[1] + to[1]) * sizes[2] + to[2]))
        if back:
            route = [(target, source) for source, target in route]
        return lax.ppermute(block, "expert", route)

    def offsets(self):
        _, nb, nc = self.sizes
        return [(b, c) for b in range(nb) for c in range(nc)]

    def heights(self, rows):
        na = self.sizes[0]
        half = rows * (na - na // 2)
        listed = []
        for b, c in self.offsets():
            listed += [half, na * rows - half] if b and c else [na * rows]
        return listed

    def types(self):
        listed = []
        for b, c in self.offsets():
            listed += [jnp.bfloat16] * 2 if b and c else [jnp.float32]
        return listed

    def gather(self, block):
        na, nb, nc = self.sizes
        rows = block.shape[0]
        own = [block] + [self.shift(block, (s, 0, 0)) for s in range(1, na)]
        own = jnp.concatenate(own, axis=0)
        half = rows * (na - na // 2)
        pieces = {(0, 0): [own]}
        for b in range(1, nb):
            pieces[b, 0] = [self.shift(own, (0, b, 0))]
        for c in range(1, nc):
            pieces[0, c] = [self.shift(own, (0, 0, c))]
        for b in range(1, nb):
            for c in range(1, nc):
                first = self.shift(pieces[b, 0][0][:half], (0, 0, c))
                second = self.shift(pieces[0, c][0][half:], (0, b, 0))
                pieces[b, c] = [first, second]
        return sum((pieces[k] for k in self.offsets()), [])

    def scatter(self, pieces, rows, after=(None, None, None)):
        na, nb, nc = self.sizes
        half = rows * (na - na // 2)
        held, at = {}, 0
        for k in self.offsets():
            count = 2 if k[0] and k[1] else 1
            held[k] = pieces[at : at + count]
            at += count
        arrived = []
        for b in range(1, nb):
            more = [self.shift(held[b, c][0], (0, 0, c), back=True) for c in range(1, nc)]
            arrived.append((held[b, 0][0], more, 0, (0, b, 0)))
        for c in range(1, nc):
            more = [self.shift(held[b, c][1], (0, b, 0), back=True) for b in range(1, nb)]
            arrived.append((held[0, c][0], more, half, (0, 0, c)))
        arrived = [
            self.shift(add_half(piece, more, start, after[0]), by, back=True)
            for piece, more, start, by in arrived
        ]
        blocks = add_blocks(held[0, 0][0], arrived, rows, after[1])
        more = [self.shift(blocks[s], (s, 0, 0), back=True) for s in range(1, na)]
        return add_last(blocks[0], more, after[2])


def compiler_params():
    return pltpu.CompilerParams(vmem_limit_bytes=24 * 2**20)


def in_vmem(count):
    return [pl.BlockSpec(memory_space=pltpu.VMEM)] * count


ANYWHERE = pl.BlockSpec(memory_space=pl.ANY)
LAST = (((1,), (1,)), ((), ()))
PLAIN = (((1,), (0,)), ((), ()))


def dot(left, right, dims=PLAIN):
    return lax.dot_general(left, right, dims, preferred_element_type=jnp.float32)


def local_kernel(kernel, name, outs, args, after=None, flops=0, scalars=0, **more):
    args = list(args)
    in_specs = [pl.BlockSpec(memory_space=pltpu.SMEM)] * scalars + in_vmem(len(args) - scalars)
    count = len(args)
    body = kernel
    if after is not None:
        args.append(after)
        in_specs.append(ANYWHERE)

        def body(*refs):
            kernel(*refs[:count], *refs[count + 1 :])

    moved = sum(x.size * x.dtype.itemsize for x in args[:count]) + sum(
        x.size * x.dtype.itemsize for x in outs
    )
    return pl.pallas_call(
        body,
        out_shape=tuple(outs),
        in_specs=in_specs,
        out_specs=tuple(in_vmem(len(outs))),
        compiler_params=compiler_params(),
        cost_estimate=pl.CostEstimate(flops=flops, bytes_accessed=moved, transcendentals=0),
        name=name,
        **more,
    )(*args)


def add_half(piece, more, start, after):
    rows = more[0].shape[0]

    def add(whole, terms):
        there = whole[start : start + rows]
        for term in terms:
            there = there + term.astype(jnp.float32)
        parts = [whole[:start], there, whole[start + rows :]]
        return jnp.concatenate([p for p in parts if p.shape[0]], axis=0).astype(jnp.bfloat16)

    if rows % 16:
        return add(piece, more)

    def kernel(piece_ref, *refs):
        refs[-1][...] = add(piece_ref[...], [r[...] for r in refs[:-1]])

    one = jax.ShapeDtypeStruct(piece.shape, jnp.bfloat16)
    return local_kernel(kernel, "add_half", [one], [piece, *more], after)[0]


def add_blocks(piece, more, rows, after):
    count = piece.shape[0] // rows
    types = [jnp.float32] + [jnp.bfloat16] * (count - 1)

    def add(whole, terms):
        for term in terms:
            whole = whole + term.astype(jnp.float32)
        return [whole[s * rows : (s + 1) * rows].astype(t) for s, t in enumerate(types)]

    if rows % 8:
        return add(piece, more)

    def kernel(*refs):
        terms = [r[...] for r in refs[: 1 + len(more)]]
        for ref, block in zip(refs[1 + len(more) :], add(terms[0], terms[1:])):
            ref[...] = block

    outs = [jax.ShapeDtypeStruct((rows, piece.shape[1]), t) for t in types]
    return local_kernel(kernel, "add_blocks", outs, [piece, *more], after)


def add_last(block, more, after):
    def kernel(block_ref, *refs):
        total = block_ref[...]
        for ref in refs[:-1]:
            total = total + ref[...].astype(jnp.float32)
        refs[-1][...] = total

    one = jax.ShapeDtypeStruct(block.shape, jnp.float32)
    return local_kernel(kernel, "add_last", [one], [block, *more], after)[0]


def head_loop(heads, some_heads):
    few = next(u for u in (5, 4, 2, 1) if heads % u == 0)

    def step(g, carry):
        numbers = [g * few + u for u in range(few)]
        some_heads(numbers, [pl.ds(pl.multiple_of(h * HD, HD), HD) for h in numbers])
        return carry

    lax.fori_loop(0, heads // few, step, 0)


def beside(columns, width):
    return [pl.ds(pl.multiple_of(width + c.start, HD), HD) for c in columns]


def stacked(refs, columns):
    return [jnp.concatenate([r[:, c] for r in refs], axis=0) for c in columns]


def make_queries(x, gain):
    tokens, width = x.shape
    half = width // 2

    def kernel(x_ref, gain_ref, *q_refs):
        x = x_ref[...].astype(jnp.float32)
        inverse = lax.rsqrt(jnp.mean(x * x, axis=-1, keepdims=True) + 1e-06)
        for at, ref in zip((0, half), q_refs):
            x = x_ref[:, at : at + half].astype(jnp.float32)
            ref[...] = (x * inverse * gain_ref[:, at : at + half]).astype(jnp.bfloat16)

    one = jax.ShapeDtypeStruct((tokens, half), jnp.bfloat16)
    return local_kernel(kernel, "queries", [one, one], [x, gain])


def attend(q, pieces):
    tokens, width = q.shape
    heads = width // HD
    rows = sum(p.shape[0] for p in pieces)
    count = len(pieces)

    def kernel(q_ref, *refs):
        kv_refs, (mixed_ref, p_ref) = refs[:count], refs[count:]

        def some_heads(numbers, columns):
            keys = stacked(kv_refs, columns)
            values = stacked(kv_refs, beside(columns, width))
            scores = [dot(k, q_ref[:, c], LAST) * HD**-0.5 for k, c in zip(keys, columns)]
            e = [jnp.exp(s - jnp.max(s, axis=0, keepdims=True)) for s in scores]
            w = [x * (1.0 / jnp.sum(x, axis=0, keepdims=True)) for x in e]
            mixed = [dot(x.astype(jnp.bfloat16).T, v) for x, v in zip(w, values)]
            for h, c, x, m in zip(numbers, columns, w, mixed):
                p_ref[h] = x
                mixed_ref[:, c] = m.astype(jnp.bfloat16)

        head_loop(heads, some_heads)

    outs = [
        jax.ShapeDtypeStruct((tokens, width), jnp.bfloat16),
        jax.ShapeDtypeStruct((heads, rows, tokens), jnp.float32),
    ]
    return local_kernel(kernel, "attend", outs, [q, *pieces], flops=4 * tokens * rows * width)


def gradient(q, cot, p, pieces, heights, types, after):
    tokens, width = q.shape
    heads, rows, _ = p.shape
    count = len(pieces)

    def kernel(q_ref, cot_ref, p_ref, *refs):
        kv_refs, out_refs = refs[:count], refs[count:]

        def some_heads(numbers, columns):
            values = stacked(kv_refs, beside(columns, width))
            q = [q_ref[:, c] for c in columns]
            cot = [cot_ref[:, c] for c in columns]
            w = [p_ref[h] for h in numbers]
            dp = [dot(v, c, LAST) for v, c in zip(values, cot)]
            ds = [
                x * (d - jnp.sum(d * x, axis=0, keepdims=True)) * HD**-0.5 for d, x in zip(dp, w)
            ]
            upper = [x.astype(jnp.bfloat16) for x in ds]
            lower = [(x - u.astype(jnp.float32)).astype(jnp.bfloat16) for x, u in zip(ds, upper)]
            dk = [
                dot(jnp.concatenate([u, v], axis=1), jnp.concatenate([x, x], axis=0))
                for u, v, x in zip(upper, lower, q)
            ]
            dv = [dot(x.astype(jnp.bfloat16), c) for x, c in zip(w, cot)]
            for there, grads in ((columns, dk), (beside(columns, width), dv)):
                for c, g in zip(there, grads):
                    at = 0
                    for ref in out_refs:
                        ref[:, c] = g[at : at + ref.shape[0]].astype(ref.dtype)
                        at += ref.shape[0]

        head_loop(heads, some_heads)

    outs = [jax.ShapeDtypeStruct((n, 2 * width), t) for n, t in zip(heights, types)]
    return local_kernel(
        kernel, "gradient", outs, [q, cot, p, *pieces], after, flops=10 * tokens * rows * width
    )


def settle(flag, x, first, second, norm_gain, slots):
    tokens, width = x.shape
    half = width // 2

    def kernel(flag, x_ref, first_ref, second_ref, norm_ref, slot_ref, res_ref, cap_ref):
        onehot = slot_ref[...] == lax.broadcasted_iota(jnp.int32, (CAP, tokens), 0)
        onehot = jnp.where(onehot, 1.0, 0.0).astype(jnp.bfloat16)
        attends = jnp.full((tokens, 1), flag[0], jnp.int32) == 1
        chosen = []
        for at, ref in ((0, first_ref), (half, second_ref)):
            mixed = jnp.where(attends, ref[...].astype(jnp.float32), 0.0)
            res = (x_ref[:, at : at + half].astype(jnp.float32) + mixed).astype(jnp.bfloat16)
            res_ref[:, at : at + half] = res
            chosen.append(dot(onehot, res))
        squares = sum(jnp.sum(c * c, axis=-1, keepdims=True) for c in chosen)
        inverse = lax.rsqrt(squares / width + 1e-06)
        for at, c in zip((0, half), chosen):
            rows = (c * inverse * norm_ref[:, at : at + half]).astype(jnp.bfloat16)
            cap_ref[:, at : at + half] = rows

    outs = [
        jax.ShapeDtypeStruct((tokens, width), jnp.bfloat16),
        jax.ShapeDtypeStruct((CAP, width), jnp.bfloat16),
    ]
    return local_kernel(
        kernel, "settle", outs, [flag, x, first, second, norm_gain, slots], scalars=1
    )


def expert(w1, w2, pieces, heights, types, after):
    width, units = w1.shape
    rows = sum(heights)
    count = len(pieces)
    steps = next(s for s in (4, 2, 1) if width % (s * 128) == 0)
    step = width // steps

    def kernel(w1_any, w2_any, _, *refs):
        in_refs, out_refs = refs[:count], refs[count : count + len(heights)]
        w1_ref, w2_ref, sems = refs[count + len(heights) :]
        parts = [slice(i * step, (i + 1) * step) for i in range(steps)]
        copies = [
            pltpu.make_async_copy(w1_any.at[c, :], w1_ref.at[c, :], sems.at[0, i])
            for i, c in enumerate(parts)
        ]
        later = [
            pltpu.make_async_copy(w2_any.at[:, c], w2_ref.at[:, c], sems.at[1, i])
            for i, c in enumerate(parts)
        ]
        for copy in copies + later:
            copy.start()
        hidden = jnp.zeros((rows, units), jnp.float32)
        for copy, c in zip(copies, parts):
            x = jnp.concatenate([r[:, c] for r in in_refs], axis=0)
            copy.wait()
            hidden = hidden + dot(x, w1_ref[c, :])
        hidden = jax.nn.gelu(hidden).astype(jnp.bfloat16)
        for copy, c in zip(later, parts):
            copy.wait()
            y = dot(hidden, w2_ref[:, c])
            at = 0
            for ref in out_refs:
                ref[:, c] = y[at : at + ref.shape[0]].astype(ref.dtype)
                at += ref.shape[0]

    return pl.pallas_call(
        kernel,
        out_shape=tuple(jax.ShapeDtypeStruct((n, width), t) for n, t in zip(heights, types)),
        in_specs=[ANYWHERE] * 3 + in_vmem(count),
        out_specs=tuple(in_vmem(len(heights))),
        scratch_shapes=[
            pltpu.VMEM((width, units), w1.dtype),
            pltpu.VMEM((units, width), w2.dtype),
            pltpu.SemaphoreType.DMA((2, steps)),
        ],
        compiler_params=pltpu.CompilerParams(vmem_limit_bytes=48 * 2**20),
        cost_estimate=pl.CostEstimate(
            flops=4 * rows * width * units, bytes_accessed=4 * width * units, transcendentals=0
        ),
        name="expert",
    )(w1, w2, after, *pieces)


def finish(own, before):
    one = jax.ShapeDtypeStruct(own[0].shape, jnp.bfloat16)
    tokens, width = one.shape
    step = next(s for s in (1280, 1024, 512, 256, 128) if width % s == 0)

    def kernel(*refs):
        for res_ref, back_ref, gate_ref, out_ref in (refs[0:3] + refs[6:7], refs[3:6] + refs[7:8]):
            gate = jnp.broadcast_to(gate_ref[0:1], (CAP, tokens)).T[:, 0:1]
            slots = lax.broadcasted_iota(jnp.int32, (CAP, tokens), 0).astype(jnp.float32)
            onehot = jnp.where(gate_ref[1:2] == slots, 1.0, 0.0).T
            onehot = jnp.concatenate([onehot] * 3, axis=1).astype(jnp.bfloat16)
            for at in range(0, width, step):
                columns = slice(at, at + step)
                back = back_ref[:, columns]
                high = back.astype(jnp.bfloat16).astype(jnp.float32)
                middle = (back - high).astype(jnp.bfloat16).astype(jnp.float32)
                parts = jnp.concatenate([high, middle, back - high - middle], axis=0)
                moved = dot(onehot, parts.astype(jnp.bfloat16))
                res = res_ref[:, columns].astype(jnp.float32)
                out_ref[:, columns] = (res + gate * moved).astype(jnp.bfloat16)

    return local_kernel(
        kernel, "finish", [one, one], [*own, *before], flops=100 * tokens * width
    )


def local(
    layer_in, memory, cotangent, norm_gain, attn_gain, expert_in, expert_out, slot_index, gate_prob
):
    sections = lax.axis_size("section")
    decoder = lax.axis_index("section") >= sections // 2
    flag = decoder.astype(jnp.int32).reshape(1)
    grid = Grid(lax.axis_size("expert"))
    own_rows, _, width = memory[0].shape
    half = width // 2
    heights, types = grid.heights(own_rows), grid.types()
    narrow = any(n % 16 for n in heights)

    def shared(first, second):
        return jnp.where(decoder, second, swapped(first))

    stash = shared(
        memory[0, :, :, :half].reshape(own_rows, width),
        memory[0, :, :, half:].reshape(own_rows, width),
    )
    pieces = grid.gather(stash)
    queries = shared(*make_queries(layer_in[0], attn_gain))
    upstream = shared(cotangent[0, :, :half], cotangent[0, :, half:])
    if narrow:
        pieces = [jnp.concatenate(pieces, axis=0)]
    mixed, weights = attend(queries, pieces)
    residual, capacity = settle(flag, layer_in[0], swapped(mixed), mixed, norm_gain, slot_index)
    gathered = grid.gather(capacity)
    gates = jnp.concatenate([gate_prob, slot_index.astype(jnp.float32)], axis=0)
    residual_before = passed_along(residual, "section", 1)
    gates_before = passed_along(gates, "section", 1)
    computed = expert(
        expert_in[0], expert_out[0], gathered, grid.heights(CAP), types, residual_before
    )
    returned = grid.scatter(computed, CAP)
    returned_before = passed_along(returned, "section", 1)
    output, arriving = finish(
        (residual, returned, gates), (residual_before, returned_before, gates_before)
    )
    if narrow:
        whole = [sum(heights)], [jnp.float32]
        (whole,) = gradient(queries, upstream, weights, pieces, *whole, capacity)
        parts, at = [], 0
        for n, t in zip(heights, types):
            parts.append(whole[at : at + n].astype(t))
            at += n
    else:
        parts = gradient(queries, upstream, weights, pieces, heights, types, capacity)
    total_grad = grid.scatter(parts, own_rows, (gathered[-1], computed[0], returned))
    first = swapped(total_grad).reshape(own_rows, 2, half)
    total_grad = jnp.concatenate([first, total_grad.reshape(own_rows, 2, half)], axis=2)
    total_grad = jnp.where(decoder, total_grad, 0.0)
    return (output[None], arriving[None], total_grad[None])


def solution(mesh):
    placed = (
        P("section", "expert", None),
        P("section", "expert", None, None),
        P("section", "expert", None),
        P("section", None),
        P("section", None),
        P("section", None, "expert"),
        P("section", "expert", None),
        P("section", "expert"),
        P("section", "expert"),
    )
    return jax.shard_map(
        local,
        mesh=mesh,
        in_specs=placed,
        out_specs=(
            P("section", "expert", None),
            P("section", "expert", None),
            P("section", "expert", None, None),
        ),
        check_vma=False,
    )
```

```python
import functools

import jax
import jax.numpy as jnp
from jax import lax
from jax.experimental import pallas as pl
from jax.experimental.pallas import tpu as pltpu
from jax.sharding import PartitionSpec as P

HD = 128
CAP = 8


def passed_along(block, axis, distance):
    devices = range(lax.axis_size(axis))
    route = [(i - distance, i) for i in devices if i - distance in devices]
    return lax.ppermute(block, axis, route)


def swapped(block):
    sections = lax.axis_size("section")
    return lax.ppermute(block, "section", [(i, (i + sections // 2) % sections) for i in range(sections)])


def to_decoder(block):
    apart = lax.axis_size("section") // 2
    return lax.ppermute(block, "section", [(i, i + apart) for i in range(apart)])


def partner(position, distance, size):
    return position ^ distance if size & (size - 1) == 0 else (position + distance) % size


class Grid:
    def __init__(self, size):
        side = 2 if size % 4 == 0 else 1
        self.sizes = (size // side**2, side, side)
        self.size = size

    def shift(self, block, by, back=False):
        sizes = self.sizes
        route = []
        for index in range(self.size):
            at = (index // (sizes[1] * sizes[2]), index // sizes[2] % sizes[1], index % sizes[2])
            to = [partner(p, d, n) for p, d, n in zip(at, by, sizes)]
            route.append((index, (to[0] * sizes[1] + to[1]) * sizes[2] + to[2]))
        if back:
            route = [(target, source) for source, target in route]
        return lax.ppermute(block, "expert", route)

    def offsets(self):
        _, nb, nc = self.sizes
        return [(b, c) for b in range(nb) for c in range(nc)]

    def heights(self, rows):
        na = self.sizes[0]
        half = rows * (na - na // 2)
        listed = []
        for b, c in self.offsets():
            listed += [half, na * rows - half] if b and c else [na * rows]
        return listed

    def types(self):
        listed = []
        for b, c in self.offsets():
            listed += [jnp.bfloat16] * 2 if b and c else [jnp.float32]
        return listed

    def line(self, block):
        return join([block] + [self.shift(block, (s, 0, 0)) for s in range(1, self.sizes[0])])

    def plane(self, blocks):
        return [blocks[0]] + [
            self.shift(block, (0, b, c)) for block, (b, c) in zip(blocks[1:], self.offsets()[1:])
        ]

    def gather(self, block, after):
        na, nb, nc = self.sizes
        own = self.line(block)
        half = block.shape[0] * (na - na // 2)
        pieces = {(0, 0): [own]}
        for b in range(1, nb):
            pieces[b, 0] = [self.shift(own, (0, b, 0))]
        for c in range(1, nc):
            pieces[0, c] = [self.shift(own, (0, 0, c))]
        for b in range(1, nb):
            for c in range(1, nc):
                first, second = halves_of(pieces[b, 0][0], pieces[0, c][0], half, after)
                first, second = self.shift(first, (0, 0, c)), self.shift(second, (0, b, 0))
                pieces[b, c] = [first, second]
        return sum((pieces[k] for k in self.offsets()), [])

    def scatter(self, pieces, rows, first=()):
        na, nb, nc = self.sizes
        half = rows * (na - na // 2)
        held, at = {}, 0
        for k in self.offsets():
            count = 2 if k[0] and k[1] else 1
            held[k] = pieces[at : at + count]
            at += count
        arrived = []
        for b in range(1, nb):
            more = [self.shift(held[b, c][0], (0, 0, c), back=True) for c in range(1, nc)]
            arrived.append((held[b, 0][0], more, 0, (0, b, 0)))
        for c in range(1, nc):
            more = [self.shift(held[b, c][1], (0, b, 0), back=True) for b in range(1, nb)]
            arrived.append((held[0, c][0], more, half, (0, 0, c)))
        arrived = [
            (add_half(piece, more, start, first), by) for piece, more, start, by in arrived
        ]
        halves = [piece for piece, _ in arrived]
        arrived = [self.shift(piece, by, back=True) for piece, by in arrived]
        after = yield halves
        blocks = add_blocks(held[0, 0][0], arrived, rows, after)
        yield self.last(blocks)

    def last(self, blocks):
        more = [self.shift(blocks[s], (s, 0, 0), back=True) for s in range(1, self.sizes[0])]
        return add_last(blocks[0], more)


def compiler_params():
    return pltpu.CompilerParams(vmem_limit_bytes=20 * 2**20)


def in_vmem(count):
    return [pl.BlockSpec(memory_space=pltpu.VMEM)] * count


ANYWHERE = pl.BlockSpec(memory_space=pl.ANY)
LAST = (((1,), (1,)), ((), ()))
PLAIN = (((1,), (0,)), ((), ()))


def dot(left, right, dims=PLAIN):
    return lax.dot_general(left, right, dims, preferred_element_type=jnp.float32)


def local_kernel(kernel, name, outs, args, after=(), flops=0, scalars=0, **more):
    args = list(args)
    in_specs = [pl.BlockSpec(memory_space=pltpu.SMEM)] * scalars + in_vmem(len(args) - scalars)
    count = len(args)
    body = kernel
    if after:
        args += after
        in_specs += [ANYWHERE] * len(after)

        def body(*refs):
            kernel(*refs[:count], *refs[count + len(after) :])

    moved = sum(x.size * x.dtype.itemsize for x in args[:count]) + sum(
        x.size * x.dtype.itemsize for x in outs
    )
    return pl.pallas_call(
        body,
        out_shape=tuple(outs),
        in_specs=in_specs,
        out_specs=tuple(in_vmem(len(outs))),
        compiler_params=compiler_params(),
        cost_estimate=pl.CostEstimate(flops=flops, bytes_accessed=moved, transcendentals=0),
        name=name,
        **more,
    )(*args)


def join(blocks):
    if blocks[0].shape[0] % 8:
        return jnp.concatenate(blocks, axis=0)

    def kernel(*refs):
        rows = jnp.concatenate([r[...].astype(jnp.float32) for r in refs[:-1]], axis=0)
        refs[-1][...] = rows.astype(jnp.bfloat16)

    one = jax.ShapeDtypeStruct((len(blocks) * blocks[0].shape[0], blocks[0].shape[1]), jnp.bfloat16)
    return local_kernel(kernel, "join", [one], blocks)[0]


def halves_of(first, second, half, after):
    if half % 16:
        return first[:half], second[half:]

    def kernel(first_ref, second_ref, upper_ref, lower_ref):
        upper_ref[...] = first_ref[:half]
        lower_ref[...] = second_ref[half:]

    width = first.shape[1]
    outs = [
        jax.ShapeDtypeStruct((half, width), first.dtype),
        jax.ShapeDtypeStruct((second.shape[0] - half, width), first.dtype),
    ]
    return local_kernel(kernel, "halves", outs, [first, second], after)


def add_half(piece, more, start, after):
    rows = more[0].shape[0]

    def add(whole, terms):
        there = whole[start : start + rows]
        for term in terms:
            there = there + term.astype(jnp.float32)
        parts = [whole[:start], there, whole[start + rows :]]
        return jnp.concatenate([p for p in parts if p.shape[0]], axis=0).astype(jnp.bfloat16)

    if rows % 16:
        return add(piece, more)

    def kernel(piece_ref, *refs):
        refs[-1][...] = add(piece_ref[...], [r[...] for r in refs[:-1]])

    one = jax.ShapeDtypeStruct(piece.shape, jnp.bfloat16)
    return local_kernel(kernel, "add_half", [one], [piece, *more], after)[0]


def add_blocks(piece, more, rows, after):
    count = piece.shape[0] // rows
    types = [jnp.float32] + [jnp.bfloat16] * (count - 1)

    def add(whole, terms):
        for term in terms:
            whole = whole + term.astype(jnp.float32)
        return [whole[s * rows : (s + 1) * rows].astype(t) for s, t in enumerate(types)]

    if rows % 8:
        return add(piece, more)

    def kernel(*refs):
        terms = [r[...] for r in refs[: 1 + len(more)]]
        for ref, block in zip(refs[1 + len(more) :], add(terms[0], terms[1:])):
            ref[...] = block

    outs = [jax.ShapeDtypeStruct((rows, piece.shape[1]), t) for t in types]
    return local_kernel(kernel, "add_blocks", outs, [piece, *more], after)


def add_last(block, more):
    def kernel(block_ref, *refs):
        total = block_ref[...]
        for ref in refs[:-1]:
            total = total + ref[...].astype(jnp.float32)
        refs[-1][...] = total

    one = jax.ShapeDtypeStruct(block.shape, jnp.float32)
    return local_kernel(kernel, "add_last", [one], [block, *more])[0]


class Place:
    def __init__(self, section, sections, index, shares):
        self.args = [section.reshape(1), index.reshape(1)]
        self.sections, self.shares = sections, shares

    def decodes(self, refs):
        return refs[0][0] >= self.sections // 2

    def columns(self, refs, k, width, start=0):
        share = jnp.bitwise_xor(lax.rem(refs[1][0], self.shares), k)
        return pl.ds(pl.multiple_of(start + share * width, HD), width)


def spread_stash(place, first, second):
    rows, width = first.shape
    part = width // 2 // place.shares

    def kernel(*refs):
        (first_ref, second_ref), out_refs = refs[2:4], refs[4:]
        for at in (0, 1):
            for k, ref in enumerate(out_refs):
                columns = place.columns(refs, k, part, at * (width // 2))
                one = first_ref[:, columns].astype(jnp.float32)
                two = second_ref[:, columns].astype(jnp.float32)
                mine = jnp.where(jnp.full((rows, 1), refs[0][0]) >= place.sections // 2, two, one)
                ref[:, at * part : (at + 1) * part] = mine.astype(jnp.bfloat16)

    outs = [jax.ShapeDtypeStruct((rows, 2 * part), jnp.bfloat16)] * place.shares
    return local_kernel(kernel, "spread_stash", outs, [*place.args, first, second], scalars=2)


def prepare(place, x, gain, cot, gate, slots, after):
    tokens, width = x.shape
    half = width // 2
    part = half // place.shares

    def kernel(*refs):
        x_ref, gain_ref, cot_ref, gate_ref, slot_ref = refs[2:7]
        copy_ref, q_refs, cot_refs, gates_ref = refs[7], refs[8:10], refs[10:12], refs[12]
        copy_ref[...] = x_ref[...]
        gates_ref[0:1] = gate_ref[...]
        gates_ref[1:2] = slot_ref[...].astype(jnp.float32)
        x = x_ref[...].astype(jnp.float32)
        inverse = lax.rsqrt(jnp.mean(x * x, axis=-1, keepdims=True) + 1e-06)
        for at, q_ref, part_ref in zip((0, half), q_refs, cot_refs):
            for k in range(place.shares):
                columns = place.columns(refs, k, part, at)
                x = x_ref[:, columns].astype(jnp.float32)
                q_ref[k] = (x * inverse * gain_ref[:, columns]).astype(jnp.bfloat16)
                part_ref[k] = cot_ref[:, columns]

    one = jax.ShapeDtypeStruct((place.shares, tokens, part), jnp.bfloat16)
    outs = [
        jax.ShapeDtypeStruct((tokens, width), x.dtype),
        *[one] * 4,
        jax.ShapeDtypeStruct((2, tokens), jnp.float32),
    ]
    args = [*place.args, x, gain, cot, gate, slots]
    return local_kernel(kernel, "prepare", outs, args, after, scalars=2)


def pick(place, first, second):
    def kernel(*refs):
        (first_ref, second_ref), out_refs = refs[2:4], refs[4:]

        @pl.when(place.decodes(refs))
        def _():
            for k, ref in enumerate(out_refs):
                ref[...] = second_ref[k]

        @pl.when(jnp.logical_not(place.decodes(refs)))
        def _():
            for k, ref in enumerate(out_refs):
                ref[...] = first_ref[k]

    outs = [jax.ShapeDtypeStruct(first.shape[1:], first.dtype)] * first.shape[0]
    return local_kernel(kernel, "pick", outs, [*place.args, first, second], scalars=2)


def pile(blocks):
    def kernel(*refs):
        for k, ref in enumerate(refs[:-1]):
            refs[-1][k] = ref[...]

    one = jax.ShapeDtypeStruct((len(blocks), *blocks[0].shape), blocks[0].dtype)
    return local_kernel(kernel, "pile", [one], blocks)[0]


def attend(stash, queries, after):
    tokens, width = queries[0].shape
    heads = width // HD
    rows = stash.shape[0]
    count = len(queries)

    def kernel(stash_ref, *refs):
        q_refs, mixed_refs, p_ref = refs[:count], refs[count : 2 * count], refs[2 * count]
        for h in range(heads):
            c = slice(h * HD, (h + 1) * HD)
            keys, values = stash_ref[:, c], stash_ref[:, width + h * HD : width + (h + 1) * HD]
            scores = [dot(keys, ref[:, c], LAST) * HD**-0.5 for ref in q_refs]
            e = [jnp.exp(s - jnp.max(s, axis=0, keepdims=True)) for s in scores]
            w = [x * (1.0 / jnp.sum(x, axis=0, keepdims=True)) for x in e]
            mixed = [dot(x.astype(jnp.bfloat16).T, values) for x in w]
            for k, (x, m) in enumerate(zip(w, mixed)):
                p_ref[h, k] = x
                mixed_refs[k][:, c] = m.astype(jnp.bfloat16)

    outs = [jax.ShapeDtypeStruct((tokens, width), jnp.bfloat16)] * count
    outs.append(jax.ShapeDtypeStruct((heads, count, rows, tokens), jnp.float32))
    *mixed, weights = local_kernel(
        kernel, "attend", outs, [stash, *queries], after, flops=4 * count * tokens * rows * width
    )
    return mixed, weights


def gradient(stash, queries, cots, p, blocks, after):
    tokens, width = queries[0].shape
    heads, count, rows, _ = p.shape
    height = rows // blocks

    def kernel(stash_ref, p_ref, *refs):
        q_refs, cot_refs, out_refs = refs[:count], refs[count : 2 * count], refs[2 * count :]
        for h in range(heads):
            c = slice(h * HD, (h + 1) * HD)
            there = slice(width + h * HD, width + (h + 1) * HD)
            values = stash_ref[:, there]
            q = [ref[:, c] for ref in q_refs]
            cot = [ref[:, c] for ref in cot_refs]
            w = [p_ref[h, k] for k in range(count)]
            dp = [dot(values, x, LAST) for x in cot]
            ds = [
                x * (d - jnp.sum(d * x, axis=0, keepdims=True)) * HD**-0.5 for d, x in zip(dp, w)
            ]
            upper = [x.astype(jnp.bfloat16) for x in ds]
            lower = [(x - u.astype(jnp.float32)).astype(jnp.bfloat16) for x, u in zip(ds, upper)]
            dk = sum(
                dot(jnp.concatenate([u, v], axis=1), jnp.concatenate([x, x], axis=0))
                for u, v, x in zip(upper, lower, q)
            )
            dv = sum(dot(x.astype(jnp.bfloat16), y) for x, y in zip(w, cot))
            for columns, grad in ((c, dk), (there, dv)):
                for s, ref in enumerate(out_refs):
                    ref[:, columns] = grad[s * height : (s + 1) * height].astype(ref.dtype)

    types = [jnp.float32] + [jnp.bfloat16] * (blocks - 1)
    outs = [jax.ShapeDtypeStruct((height, 2 * width), t) for t in types]
    return local_kernel(
        kernel, "gradient", outs, [stash, p, *queries, *cots], after,
        flops=10 * count * tokens * rows * width,
    )


def settle(place, x, first, second, norm_gain, gates):
    tokens, width = x.shape
    shares, _, part = first.shape

    def kernel(*refs):
        x_ref, first_ref, second_ref, norm_ref, gate_ref, res_ref, cap_ref, sel_ref = refs[2:]
        slots = lax.broadcasted_iota(jnp.int32, (CAP, tokens), 0).astype(jnp.float32)
        onehot = jnp.where(gate_ref[1:2] == slots, 1.0, 0.0).astype(jnp.bfloat16)
        attends = jnp.full((tokens, 1), refs[0][0]) >= place.sections // 2
        squares = jnp.zeros((CAP, 1), jnp.float32)
        for at, ref in ((0, first_ref), (width // 2, second_ref)):
            for k in range(shares):
                columns = place.columns(refs, k, part, at)
                mixed = jnp.where(attends, ref[k].astype(jnp.float32), 0.0)
                res = (x_ref[:, columns].astype(jnp.float32) + mixed).astype(jnp.bfloat16)
                res_ref[:, columns] = res
                chosen = dot(onehot, res)
                sel_ref[:, columns] = chosen
                squares = squares + jnp.sum(chosen * chosen, axis=-1, keepdims=True)
        inverse = lax.rsqrt(squares / width + 1e-06)
        cap_ref[...] = (sel_ref[...] * inverse * norm_ref[...]).astype(jnp.bfloat16)

    outs = [
        jax.ShapeDtypeStruct((tokens, width), jnp.bfloat16),
        jax.ShapeDtypeStruct((CAP, width), jnp.bfloat16),
    ]
    return local_kernel(
        kernel, "settle", outs, [*place.args, x, first, second, norm_gain, gates], scalars=2,
        scratch_shapes=[pltpu.VMEM((CAP, width), jnp.float32)],
    )


def add_line(blocks, rows, after):
    count = blocks[0].shape[0] // rows

    def add(terms):
        total = sum((t.astype(jnp.float32) for t in terms[1:]), terms[0])
        return [total[k * rows : (k + 1) * rows] for k in range(count)]

    if rows % 8:
        return add(blocks)

    def kernel(*refs):
        for ref, block in zip(refs[len(blocks) :], add([r[...] for r in refs[: len(blocks)]])):
            ref[...] = block

    outs = [jax.ShapeDtypeStruct((rows, blocks[0].shape[1]), jnp.float32)] * count
    return local_kernel(kernel, "add_line", outs, blocks, after)


def lay_out(place, first, second):
    shares, rows, part = first.shape
    part = part // 2
    half = shares * part

    def kernel(*refs):
        first_ref, second_ref, out_ref = refs[2:]
        decodes = jnp.full((rows, 1), refs[0][0]) >= place.sections // 2
        for at in (0, 1):
            for side, ref in ((0, first_ref), (half, second_ref)):
                for k in range(shares):
                    columns = place.columns(refs, k, part, at * 2 * half + side)
                    block = ref[k, :, at * part : (at + 1) * part]
                    out_ref[:, columns] = jnp.where(decodes, block, 0.0)

    one = jax.ShapeDtypeStruct((rows, 4 * half), jnp.float32)
    return local_kernel(kernel, "lay_out", [one], [*place.args, first, second], scalars=2)[0]


def expert(w1, w2, pieces, heights, types, after):
    width, units = w1.shape
    rows = sum(heights)
    count = len(pieces)
    steps = next(s for s in (4, 2, 1) if width % (s * 128) == 0)
    step = width // steps

    def kernel(w1_ref, w2_ref, *refs):
        in_refs, out_refs = refs[:count], refs[count:]
        parts = [slice(i * step, (i + 1) * step) for i in range(steps)]
        hidden = jnp.zeros((rows, units), jnp.float32)
        for c in parts:
            hidden = hidden + dot(jnp.concatenate([r[:, c] for r in in_refs], axis=0), w1_ref[c, :])
        hidden = jax.nn.gelu(hidden).astype(jnp.bfloat16)
        for c in parts:
            y = dot(hidden, w2_ref[:, c])
            at = 0
            for ref in out_refs:
                ref[:, c] = y[at : at + ref.shape[0]].astype(ref.dtype)
                at += ref.shape[0]

    outs = [jax.ShapeDtypeStruct((n, width), t) for n, t in zip(heights, types)]
    return local_kernel(
        kernel, "expert", outs, [w1, w2, *pieces], after, flops=4 * rows * width * units
    )


def finish(res, back, gates, after=()):
    one = jax.ShapeDtypeStruct(res.shape, jnp.bfloat16)
    tokens, width = res.shape
    step = next(s for s in (1280, 1024, 512, 256, 128) if width % s == 0)

    def kernel(res_ref, back_ref, gate_ref, out_ref):
        gate = jnp.broadcast_to(gate_ref[0:1], (CAP, tokens)).T[:, 0:1]
        slots = lax.broadcasted_iota(jnp.int32, (CAP, tokens), 0).astype(jnp.float32)
        onehot = jnp.where(gate_ref[1:2] == slots, 1.0, 0.0).T
        onehot = jnp.concatenate([onehot] * 3, axis=1).astype(jnp.bfloat16)
        for at in range(0, width, step):
            columns = slice(at, at + step)
            back = back_ref[:, columns]
            high = back.astype(jnp.bfloat16).astype(jnp.float32)
            middle = (back - high).astype(jnp.bfloat16).astype(jnp.float32)
            parts = jnp.concatenate([high, middle, back - high - middle], axis=0)
            moved = dot(onehot, parts.astype(jnp.bfloat16))
            here = res_ref[:, columns].astype(jnp.float32)
            out_ref[:, columns] = (here + gate * moved).astype(jnp.bfloat16)

    return local_kernel(
        kernel, "finish", [one], [res, back, gates], after, flops=50 * tokens * width
    )[0]


def local(
    layer_in, memory, cotangent, norm_gain, attn_gain, expert_in, expert_out, slot_index, gate_prob
):
    sections = lax.axis_size("section")
    section, index = lax.axis_index("section"), lax.axis_index("expert")
    grid = Grid(lax.axis_size("expert"))
    lines = grid.sizes[0]
    place = Place(section, sections, index, grid.size // lines)
    own_rows, _, width = memory[0].shape
    half = width // 2

    first = swapped(memory[0, :, :, :half].reshape(own_rows, width))
    second = memory[0, :, :, half:].reshape(own_rows, width)
    shares = join(grid.plane(spread_stash(place, first, second)))
    stash = grid.line(shares)
    current, q_first, q_second, cot_first, cot_second, gates = prepare(
        place, layer_in[0], attn_gain, cotangent[0], gate_prob, slot_index, [shares]
    )
    queries = grid.plane(pick(place, swapped(q_first), q_second))
    cots = pick(place, swapped(cot_first), cot_second)

    gates_before = passed_along(gates, "section", 1)
    early = [cots[0], gates_before]
    if sections == 2:
        residual_before = passed_along(current, "section", 1)
        early.append(residual_before)
    mixed, weights = attend(stash, queries, early)
    mixed = pile(grid.plane(mixed))
    residual, capacity = settle(place, current, to_decoder(mixed), mixed, norm_gain, gates)
    if sections != 2:
        residual_before = passed_along(residual, "section", 1)
    grads = gradient(stash, queries, grid.plane(cots), weights, lines, [capacity])
    gathered = grid.gather(capacity, [grads[0]])
    computed = expert(
        expert_in[0], expert_out[0], gathered, grid.heights(CAP), grid.types(), [residual_before]
    )
    results = grid.scatter(computed, CAP)
    sent = next(results)
    grads = [grads[0]] + [grid.shift(grads[s], (s, 0, 0), back=True) for s in range(1, lines)]
    grads = pile(grid.plane(add_line(grads, own_rows, sent)))
    returned = results.send([])
    returned_before = passed_along(returned, "section", 1)
    output = finish(residual, returned, gates)
    arriving = finish(residual_before, returned_before, gates_before)
    total_grad = lay_out(place, to_decoder(grads), grads).reshape(own_rows, 2, width)
    return (output[None], arriving[None], total_grad[None])


def solution(mesh):
    placed = (
        P("section", "expert", None),
        P("section", "expert", None, None),
        P("section", "expert", None),
        P("section", None),
        P("section", None),
        P("section", None, "expert"),
        P("section", "expert", None),
        P("section", "expert"),
        P("section", "expert"),
    )
    return jax.shard_map(
        local,
        mesh=mesh,
        in_specs=placed,
        out_specs=(
            P("section", "expert", None),
            P("section", "expert", None),
            P("section", "expert", None, None),
        ),
        check_vma=False,
    )
```

```python
import functools

import jax
import jax.numpy as jnp
from jax import lax
from jax.experimental import pallas as pl
from jax.experimental.pallas import tpu as pltpu
from jax.sharding import PartitionSpec as P

HD = 128
CAP = 8


def passed_along(block, axis, distance):
    devices = range(lax.axis_size(axis))
    route = [(i - distance, i) for i in devices if i - distance in devices]
    return lax.ppermute(block, axis, route)


def swapped(block):
    sections = lax.axis_size("section")
    return lax.ppermute(block, "section", [(i, (i + sections // 2) % sections) for i in range(sections)])


def to_decoder(block):
    apart = lax.axis_size("section") // 2
    return lax.ppermute(block, "section", [(i, i + apart) for i in range(apart)])


def partner(position, distance, size):
    return position ^ distance if size & (size - 1) == 0 else (position + distance) % size


class Grid:
    def __init__(self, size):
        a = 4 if size % 4 == 0 else 1
        c = 2 if (size // a) % 2 == 0 else 1
        self.sizes = (a, size // a // c, c)
        self.size = size

    def shift(self, block, by, back=False):
        sizes = self.sizes
        route = []
        for index in range(self.size):
            at = (index // (sizes[1] * sizes[2]), index // sizes[2] % sizes[1], index % sizes[2])
            to = [partner(p, d, n) for p, d, n in zip(at, by, sizes)]
            route.append((index, (to[0] * sizes[1] + to[1]) * sizes[2] + to[2]))
        if back:
            route = [(target, source) for source, target in route]
        return lax.ppermute(block, "expert", route)

    def offsets(self):
        _, nb, nc = self.sizes
        return [(b, c) for b in range(nb) for c in range(nc)]

    def heights(self, rows):
        na = self.sizes[0]
        half = rows * (na - na // 2)
        listed = []
        for b, c in self.offsets():
            listed += [half, na * rows - half] if b and c else [na * rows]
        return listed

    def types(self):
        listed = []
        for b, c in self.offsets():
            listed += [jnp.bfloat16] * 2 if b and c else [jnp.float32]
        return listed

    def gather(self, block):
        na, nb, nc = self.sizes
        rows = block.shape[0]
        own = join([block] + [self.shift(block, (s, 0, 0)) for s in range(1, na)])
        half = rows * (na - na // 2)
        pieces = {(0, 0): [own]}
        for b in range(1, nb):
            pieces[b, 0] = [self.shift(own, (0, b, 0))]
        for c in range(1, nc):
            pieces[0, c] = [self.shift(own, (0, 0, c))]
        for b in range(1, nb):
            for c in range(1, nc):
                first = self.shift(pieces[b, 0][0][:half], (0, 0, c))
                second = self.shift(pieces[0, c][0][half:], (0, b, 0))
                pieces[b, c] = [first, second]
        return sum((pieces[k] for k in self.offsets()), [])

    def scatter(self, pieces, rows, after=()):
        na, nb, nc = self.sizes
        half = rows * (na - na // 2)
        held, at = {}, 0
        for k in self.offsets():
            count = 2 if k[0] and k[1] else 1
            held[k] = pieces[at : at + count]
            at += count
        arrived = []
        for b in range(1, nb):
            more = [self.shift(held[b, c][0], (0, 0, c), back=True) for c in range(1, nc)]
            arrived.append((held[b, 0][0], more, 0, (0, b, 0)))
        for c in range(1, nc):
            more = [self.shift(held[b, c][1], (0, b, 0), back=True) for b in range(1, nb)]
            arrived.append((held[0, c][0], more, half, (0, 0, c)))
        halves = [add_half(piece, more, start, after) for piece, more, start, _ in arrived]
        arrived = [self.shift(piece, by, back=True) for piece, (*_, by) in zip(halves, arrived)]
        after = yield halves
        blocks = add_blocks(held[0, 0][0], arrived, rows, after)
        more = [self.shift(blocks[s], (s, 0, 0), back=True) for s in range(1, na)]
        after = yield blocks
        yield add_last(blocks[0], more, after)


def compiler_params():
    return pltpu.CompilerParams(vmem_limit_bytes=20 * 2**20)


def in_vmem(count):
    return [pl.BlockSpec(memory_space=pltpu.VMEM)] * count


ANYWHERE = pl.BlockSpec(memory_space=pl.ANY)
LAST = (((1,), (1,)), ((), ()))
PLAIN = (((1,), (0,)), ((), ()))


def dot(left, right, dims=PLAIN):
    return lax.dot_general(left, right, dims, preferred_element_type=jnp.float32)


def local_kernel(kernel, name, outs, args, after=(), flops=0, scalars=0, **more):
    args = list(args)
    in_specs = [pl.BlockSpec(memory_space=pltpu.SMEM)] * scalars + in_vmem(len(args) - scalars)
    count = len(args)
    body = kernel
    if after:
        args += after
        in_specs += [ANYWHERE] * len(after)

        def body(*refs):
            kernel(*refs[:count], *refs[count + len(after) :])

    moved = sum(x.size * x.dtype.itemsize for x in args[:count]) + sum(
        x.size * x.dtype.itemsize for x in outs
    )
    return pl.pallas_call(
        body,
        out_shape=tuple(outs),
        in_specs=in_specs,
        out_specs=tuple(in_vmem(len(outs))),
        compiler_params=compiler_params(),
        cost_estimate=pl.CostEstimate(flops=flops, bytes_accessed=moved, transcendentals=0),
        name=name,
        **more,
    )(*args)


def join(blocks):
    if blocks[0].shape[0] % 8:
        return jnp.concatenate(blocks, axis=0)

    def kernel(*refs):
        rows = jnp.concatenate([r[...].astype(jnp.float32) for r in refs[:-1]], axis=0)
        refs[-1][...] = rows.astype(jnp.bfloat16)

    one = jax.ShapeDtypeStruct((len(blocks) * blocks[0].shape[0], blocks[0].shape[1]), jnp.bfloat16)
    return local_kernel(kernel, "join", [one], blocks)[0]


def add_half(piece, more, start, after):
    rows = more[0].shape[0]

    def add(whole, terms):
        there = whole[start : start + rows]
        for term in terms:
            there = there + term.astype(jnp.float32)
        parts = [whole[:start], there, whole[start + rows :]]
        return jnp.concatenate([p for p in parts if p.shape[0]], axis=0).astype(jnp.bfloat16)

    if rows % 16:
        return add(piece, more)

    def kernel(piece_ref, *refs):
        refs[-1][...] = add(piece_ref[...], [r[...] for r in refs[:-1]])

    one = jax.ShapeDtypeStruct(piece.shape, jnp.bfloat16)
    return local_kernel(kernel, "add_half", [one], [piece, *more], after)[0]


def add_blocks(piece, more, rows, after):
    count = piece.shape[0] // rows
    types = [jnp.float32] + [jnp.bfloat16] * (count - 1)

    def add(whole, terms):
        for term in terms:
            whole = whole + term.astype(jnp.float32)
        return [whole[s * rows : (s + 1) * rows].astype(t) for s, t in enumerate(types)]

    if rows % 8:
        return add(piece, more)

    def kernel(*refs):
        terms = [r[...] for r in refs[: 1 + len(more)]]
        for ref, block in zip(refs[1 + len(more) :], add(terms[0], terms[1:])):
            ref[...] = block

    outs = [jax.ShapeDtypeStruct((rows, piece.shape[1]), t) for t in types]
    return local_kernel(kernel, "add_blocks", outs, [piece, *more], after)


def add_last(block, more, after):
    def kernel(block_ref, *refs):
        total = block_ref[...]
        for ref in refs[:-1]:
            total = total + ref[...].astype(jnp.float32)
        refs[-1][...] = total

    one = jax.ShapeDtypeStruct(block.shape, jnp.float32)
    return local_kernel(kernel, "add_last", [one], [block, *more], after)[0]


def head_loop(heads, some_heads):
    few = next(u for u in (5, 4, 2, 1) if heads % u == 0)

    def step(g, carry):
        numbers = [g * few + u for u in range(few)]
        some_heads(numbers, [pl.ds(pl.multiple_of(h * HD, HD), HD) for h in numbers])
        return carry

    lax.fori_loop(0, heads // few, step, 0)


def beside(columns, width):
    return [pl.ds(pl.multiple_of(width + c.start, HD), HD) for c in columns]


def stacked(refs, columns):
    return [jnp.concatenate([r[:, c] for r in refs], axis=0) for c in columns]


EXTRA = 16


def extra_rows(gate, slots):
    high = gate.astype(jnp.bfloat16).astype(jnp.float32)
    middle = (gate - high).astype(jnp.bfloat16).astype(jnp.float32)
    none = jnp.zeros((EXTRA - 4, gate.shape[1]), jnp.float32)
    rows = [high, middle, gate - high - middle, slots, none]
    return jnp.concatenate(rows, axis=0).astype(jnp.bfloat16)


def make_queries(x, gain, gate, slots, after):
    tokens, width = x.shape
    half = width // 2

    quarter = half // 2

    def kernel(x_ref, gain_ref, gate_ref, slot_ref, copy_ref, *refs):
        *q_refs, gates_ref = refs
        gate, slots = gate_ref[...], slot_ref[...].astype(jnp.float32)
        copy_ref[:tokens] = x_ref[...]
        copy_ref[tokens:] = jnp.zeros((EXTRA, width), jnp.bfloat16)
        copy_ref[tokens:, :tokens] = extra_rows(gate, slots)
        gates_ref[0:1] = gate
        gates_ref[1:2] = slots
        x = x_ref[...].astype(jnp.float32)
        inverse = lax.rsqrt(jnp.mean(x * x, axis=-1, keepdims=True) + 1e-06)
        for at, ref in zip((0, quarter, half), q_refs):
            columns = slice(at, at + ref.shape[1])
            x = x_ref[:, columns].astype(jnp.float32)
            ref[...] = (x * inverse * gain_ref[:, columns]).astype(jnp.bfloat16)

    part = jax.ShapeDtypeStruct((tokens, quarter), jnp.bfloat16)
    one = jax.ShapeDtypeStruct((tokens, half), jnp.bfloat16)
    same = jax.ShapeDtypeStruct((tokens + EXTRA, width), x.dtype)
    pair = jax.ShapeDtypeStruct((2, tokens), jnp.float32)
    return local_kernel(
        kernel, "queries", [same, part, part, one, pair], [x, gain, gate, slots], after
    )


def cut(x, after):
    tokens, width = x.shape
    widths = [width // 4, width // 4, width // 2]

    def kernel(x_ref, *refs):
        at = 0
        for ref in refs:
            ref[...] = x_ref[:, at : at + ref.shape[1]]
            at += ref.shape[1]

    outs = [jax.ShapeDtypeStruct((tokens, n), x.dtype) for n in widths]
    return local_kernel(kernel, "cut", outs, [x], after)


def choose(section, sections, first_refs, second_ref, out_ref):
    @pl.when(section[0] >= sections // 2)
    def _():
        out_ref[...] = second_ref[...]

    @pl.when(section[0] < sections // 2)
    def _():
        at = 0
        for ref in first_refs:
            out_ref[:, at : at + ref.shape[1]] = ref[...]
            at += ref.shape[1]


def attend(section, sections, first, second, pieces, after):
    tokens, width = second.shape
    heads = width // HD
    rows = sum(p.shape[0] for p in pieces)
    count = len(pieces)

    def kernel(section, *refs):
        *first_refs, second_ref = refs[: len(first) + 1]
        refs = refs[len(first) + 1 :]
        kv_refs, (mixed_ref, p_ref, q_ref) = refs[:count], refs[count:]
        choose(section, sections, first_refs, second_ref, q_ref)

        def some_heads(numbers, columns):
            keys = stacked(kv_refs, columns)
            values = stacked(kv_refs, beside(columns, width))
            scores = [dot(k, q_ref[:, c], LAST) * HD**-0.5 for k, c in zip(keys, columns)]
            e = [jnp.exp(s - jnp.max(s, axis=0, keepdims=True)) for s in scores]
            w = [x * (1.0 / jnp.sum(x, axis=0, keepdims=True)) for x in e]
            mixed = [dot(x.astype(jnp.bfloat16).T, v) for x, v in zip(w, values)]
            for h, c, x, m in zip(numbers, columns, w, mixed):
                p_ref[h] = x
                mixed_ref[:, c] = m.astype(jnp.bfloat16)

        head_loop(heads, some_heads)

    outs = [
        jax.ShapeDtypeStruct((tokens, width), jnp.bfloat16),
        jax.ShapeDtypeStruct((heads, rows, tokens), jnp.float32),
        jax.ShapeDtypeStruct((tokens, width), jnp.bfloat16),
    ]
    args = [section.reshape(1), *first, second, *pieces]
    return local_kernel(
        kernel, "attend", outs, args, after, flops=4 * tokens * rows * width, scalars=1
    )


def gradient(section, sections, q, first, second, p, pieces, heights, types):
    tokens, width = q.shape
    heads, rows, _ = p.shape
    count = len(pieces)

    def kernel(section, q_ref, *refs):
        *first_refs, second_ref, p_ref = refs[: len(first) + 2]
        refs = refs[len(first) + 2 :]
        kv_refs, out_refs, cot_ref = refs[:count], refs[count:-1], refs[-1]
        choose(section, sections, first_refs, second_ref, cot_ref)

        def some_heads(numbers, columns):
            values = stacked(kv_refs, beside(columns, width))
            q = [q_ref[:, c] for c in columns]
            cot = [cot_ref[:, c] for c in columns]
            w = [p_ref[h] for h in numbers]
            dp = [dot(v, c, LAST) for v, c in zip(values, cot)]
            ds = [
                x * (d - jnp.sum(d * x, axis=0, keepdims=True)) * HD**-0.5 for d, x in zip(dp, w)
            ]
            upper = [x.astype(jnp.bfloat16) for x in ds]
            lower = [(x - u.astype(jnp.float32)).astype(jnp.bfloat16) for x, u in zip(ds, upper)]
            dk = [
                dot(jnp.concatenate([u, v], axis=1), jnp.concatenate([x, x], axis=0))
                for u, v, x in zip(upper, lower, q)
            ]
            dv = [dot(x.astype(jnp.bfloat16), c) for x, c in zip(w, cot)]
            for there, grads in ((columns, dk), (beside(columns, width), dv)):
                for c, g in zip(there, grads):
                    at = 0
                    for ref in out_refs:
                        ref[:, c] = g[at : at + ref.shape[0]].astype(ref.dtype)
                        at += ref.shape[0]

        head_loop(heads, some_heads)

    outs = [jax.ShapeDtypeStruct((n, 2 * width), t) for n, t in zip(heights, types)]
    return local_kernel(
        kernel,
        "gradient",
        outs,
        [section.reshape(1), q, *first, second, p, *pieces],
        flops=10 * tokens * rows * width,
        scalars=1,
        scratch_shapes=[pltpu.VMEM((tokens, width), jnp.bfloat16)],
    )


def settle(section, sections, x, first, second, norm_gain, gates, after):
    tokens, width = first.shape[0], x.shape[1]
    half = width // 2

    def kernel(section, x_ref, first_ref, second_ref, norm_ref, gate_ref, res_ref, cap_ref):
        slots = lax.broadcasted_iota(jnp.int32, (CAP, tokens), 0).astype(jnp.float32)
        onehot = jnp.where(gate_ref[1:2] == slots, 1.0, 0.0).astype(jnp.bfloat16)
        attends = jnp.full((tokens, 1), section[0], jnp.int32) >= sections // 2
        chosen = []
        for at, ref in ((0, first_ref), (half, second_ref)):
            mixed = jnp.where(attends, ref[...].astype(jnp.float32), 0.0)
            res = (x_ref[:tokens, at : at + half].astype(jnp.float32) + mixed).astype(jnp.bfloat16)
            res_ref[:, at : at + half] = res
            chosen.append(dot(onehot, res))
        squares = sum(jnp.sum(c * c, axis=-1, keepdims=True) for c in chosen)
        inverse = lax.rsqrt(squares / width + 1e-06)
        for at, c in zip((0, half), chosen):
            rows = (c * inverse * norm_ref[:, at : at + half]).astype(jnp.bfloat16)
            cap_ref[:, at : at + half] = rows

    outs = [
        jax.ShapeDtypeStruct((tokens, width), jnp.bfloat16),
        jax.ShapeDtypeStruct((CAP, width), jnp.bfloat16),
    ]
    return local_kernel(
        kernel, "settle", outs, [section.reshape(1), x, first, second, norm_gain, gates], after,
        scalars=1,
    )


def expert(w1, w2, pieces, heights, types, after):
    width, units = w1.shape
    rows = sum(heights)
    count = len(pieces)
    steps = next(s for s in (4, 2, 1) if width % (s * 128) == 0)
    step = width // steps

    def kernel(w1_ref, w2_ref, *refs):
        in_refs, out_refs = refs[:count], refs[count:]
        parts = [slice(i * step, (i + 1) * step) for i in range(steps)]
        hidden = jnp.zeros((rows, units), jnp.float32)
        for c in parts:
            hidden = hidden + dot(jnp.concatenate([r[:, c] for r in in_refs], axis=0), w1_ref[c, :])
        hidden = jax.nn.gelu(hidden).astype(jnp.bfloat16)
        for c in parts:
            y = dot(hidden, w2_ref[:, c])
            at = 0
            for ref in out_refs:
                ref[:, c] = y[at : at + ref.shape[0]].astype(ref.dtype)
                at += ref.shape[0]

    outs = [jax.ShapeDtypeStruct((n, width), t) for n, t in zip(heights, types)]
    return local_kernel(
        kernel, "expert", outs, [w1, w2, *pieces], after, flops=4 * rows * width * units
    )


def finish(res, back, gates=None):
    tokens, width = res.shape[0] - (EXTRA if gates is None else 0), res.shape[1]
    one = jax.ShapeDtypeStruct((tokens, width), jnp.bfloat16)
    step = next(s for s in (1280, 1024, 512, 256, 128) if width % s == 0)

    def kernel(res_ref, back_ref, *refs):
        out_ref = refs[-1]
        if gates is None:
            extra = res_ref[tokens:, :tokens].astype(jnp.float32)
            gate, slot = extra[0:1] + extra[1:2] + extra[2:3], extra[3:4]
        else:
            gate, slot = refs[0][0:1], refs[0][1:2]
        gate = jnp.broadcast_to(gate, (CAP, tokens)).T[:, 0:1]
        slots = lax.broadcasted_iota(jnp.int32, (CAP, tokens), 0).astype(jnp.float32)
        onehot = jnp.where(slot == slots, 1.0, 0.0).T
        onehot = jnp.concatenate([onehot] * 3, axis=1).astype(jnp.bfloat16)
        for at in range(0, width, step):
            columns = slice(at, at + step)
            back = back_ref[:, columns]
            high = back.astype(jnp.bfloat16).astype(jnp.float32)
            middle = (back - high).astype(jnp.bfloat16).astype(jnp.float32)
            parts = jnp.concatenate([high, middle, back - high - middle], axis=0)
            moved = dot(onehot, parts.astype(jnp.bfloat16))
            here = res_ref[:tokens, columns].astype(jnp.float32)
            out_ref[:, columns] = (here + gate * moved).astype(jnp.bfloat16)

    args = [res, back] + ([] if gates is None else [gates])
    return local_kernel(kernel, "finish", [one], args, flops=50 * tokens * width)[0]


def local(
    layer_in, memory, cotangent, norm_gain, attn_gain, expert_in, expert_out, slot_index, gate_prob
):
    sections = lax.axis_size("section")
    section = lax.axis_index("section")
    decoder = section >= sections // 2
    grid = Grid(lax.axis_size("expert"))
    own_rows, _, width = memory[0].shape
    half = width // 2
    heights = grid.heights(own_rows)
    narrow = any(n % 16 for n in heights)

    first = swapped(memory[0, :, :, :half].reshape(own_rows, width))
    second = memory[0, :, :, half:].reshape(own_rows, width)
    pieces = grid.gather(jnp.where(decoder, second, first))
    current, *first, second, gates = make_queries(
        layer_in[0], attn_gain, gate_prob, slot_index, [pieces[0]]
    )
    first = [swapped(q) for q in first]
    *upstream, cot_second = cut(cotangent[0], [gates])
    upstream = [swapped(c) for c in upstream]
    if narrow:
        pieces = [jnp.concatenate(pieces, axis=0)]

    mixed, weights, queries = attend(
        section, sections, first, second, pieces, upstream
    )
    cots = (upstream, cot_second)
    if narrow:
        whole = [sum(heights)], [jnp.float32]
        (whole,) = gradient(section, sections, queries, *cots, weights, pieces, *whole)
        parts, at = [], 0
        for n, t in zip(heights, grid.types()):
            parts.append(whole[at : at + n].astype(t))
            at += n
    else:
        parts = gradient(section, sections, queries, *cots, weights, pieces, heights, grid.types())
    residual, capacity = settle(
        section, sections, current, to_decoder(mixed), mixed, norm_gain, gates, [parts[0]]
    )
    if sections == 2:
        residual_before = passed_along(current, "section", 1)
    else:
        extra = extra_rows(gates[0:1], gates[1:2])
        extra = jnp.pad(extra, ((0, 0), (0, width - extra.shape[1])))
        residual_before = passed_along(jnp.concatenate([residual, extra], axis=0), "section", 1)
    gathered = grid.gather(capacity)
    grads = grid.scatter(parts, own_rows, [gathered[1]])
    halves = next(grads)
    computed = expert(
        expert_in[0], expert_out[0], gathered, grid.heights(CAP), grid.types(),
        [residual_before, *halves],
    )
    blocks = grads.send([computed[0]])
    results = grid.scatter(computed, CAP, [blocks[0]])
    total_grad = grads.send(next(results))
    results.send([total_grad])
    returned = results.send([])
    returned_before = passed_along(returned, "section", 1)
    output = finish(residual, returned, gates)
    arriving = finish(residual_before, returned_before)
    first = to_decoder(total_grad).reshape(own_rows, 2, half)
    total_grad = jnp.concatenate([first, total_grad.reshape(own_rows, 2, half)], axis=2)
    total_grad = jnp.where(decoder, total_grad, 0.0)
    return (output[None], arriving[None], total_grad[None])


def solution(mesh):
    placed = (
        P("section", "expert", None),
        P("section", "expert", None, None),
        P("section", "expert", None),
        P("section", None),
        P("section", None),
        P("section", None, "expert"),
        P("section", "expert", None),
        P("section", "expert"),
        P("section", "expert"),
    )
    return jax.shard_map(
        local,
        mesh=mesh,
        in_specs=placed,
        out_specs=(
            P("section", "expert", None),
            P("section", "expert", None),
            P("section", "expert", None, None),
        ),
        check_vma=False,
    )
```

```python
import functools

import jax
import jax.numpy as jnp
from jax import lax
from jax.experimental import pallas as pl
from jax.experimental.pallas import tpu as pltpu
from jax.sharding import PartitionSpec as P

HD = 128
CAP = 8


def passed_along(block, axis, distance):
    devices = range(lax.axis_size(axis))
    route = [(i - distance, i) for i in devices if i - distance in devices]
    return lax.ppermute(block, axis, route)


def swapped(block):
    sections = lax.axis_size("section")
    return lax.ppermute(block, "section", [(i, (i + sections // 2) % sections) for i in range(sections)])


def to_decoder(block):
    apart = lax.axis_size("section") // 2
    return lax.ppermute(block, "section", [(i, i + apart) for i in range(apart)])


def partner(position, distance, size):
    return position ^ distance if size & (size - 1) == 0 else (position + distance) % size


class Grid:
    def __init__(self, size):
        a = 4 if size % 4 == 0 else 1
        c = 2 if (size // a) % 2 == 0 else 1
        self.sizes = (a, size // a // c, c)
        self.size = size

    def shift(self, block, by, back=False):
        sizes = self.sizes
        route = []
        for index in range(self.size):
            at = (index // (sizes[1] * sizes[2]), index // sizes[2] % sizes[1], index % sizes[2])
            to = [partner(p, d, n) for p, d, n in zip(at, by, sizes)]
            route.append((index, (to[0] * sizes[1] + to[1]) * sizes[2] + to[2]))
        if back:
            route = [(target, source) for source, target in route]
        return lax.ppermute(block, "expert", route)

    def offsets(self):
        _, nb, nc = self.sizes
        return [(b, c) for b in range(nb) for c in range(nc)]

    def heights(self, rows):
        na = self.sizes[0]
        half = rows * (na - na // 2)
        listed = []
        for b, c in self.offsets():
            listed += [half, na * rows - half] if b and c else [na * rows]
        return listed

    def types(self):
        listed = []
        for b, c in self.offsets():
            listed += [jnp.bfloat16] * 2 if b and c else [jnp.float32]
        return listed

    def gather(self, block, first=(), second=lambda own: ()):
        na, nb, nc = self.sizes
        rows = block.shape[0]
        own = join([block] + [self.shift(block, (s, 0, 0)) for s in range(1, na)], first)
        half = rows * (na - na // 2)
        pieces = {(0, 0): [own]}
        for b in range(1, nb):
            pieces[b, 0] = [self.shift(own, (0, b, 0))]
        for c in range(1, nc):
            pieces[0, c] = [self.shift(own, (0, 0, c))]
        for b in range(1, nb):
            for c in range(1, nc):
                upper, lower = halves_of(pieces[b, 0][0], pieces[0, c][0], half, second(own))
                pieces[b, c] = [self.shift(upper, (0, 0, c)), self.shift(lower, (0, b, 0))]
        return sum((pieces[k] for k in self.offsets()), [])

    def scatter(self, pieces, rows, after=()):
        na, nb, nc = self.sizes
        half = rows * (na - na // 2)
        held, at = {}, 0
        for k in self.offsets():
            count = 2 if k[0] and k[1] else 1
            held[k] = pieces[at : at + count]
            at += count
        arrived = []
        for b in range(1, nb):
            more = [self.shift(held[b, c][0], (0, 0, c), back=True) for c in range(1, nc)]
            arrived.append((held[b, 0][0], more, 0, (0, b, 0)))
        for c in range(1, nc):
            more = [self.shift(held[b, c][1], (0, b, 0), back=True) for b in range(1, nb)]
            arrived.append((held[0, c][0], more, half, (0, 0, c)))
        halves = [add_half(piece, more, start, after) for piece, more, start, _ in arrived]
        arrived = [self.shift(piece, by, back=True) for piece, (*_, by) in zip(halves, arrived)]
        after = yield halves
        blocks = add_blocks(held[0, 0][0], arrived, rows, after)
        more = [self.shift(blocks[s], (s, 0, 0), back=True) for s in range(1, na)]
        after = yield blocks, more
        yield add_last(blocks[0], more, after)


def compiler_params():
    return pltpu.CompilerParams(vmem_limit_bytes=20 * 2**20)


def in_vmem(count):
    return [pl.BlockSpec(memory_space=pltpu.VMEM)] * count


ANYWHERE = pl.BlockSpec(memory_space=pl.ANY)
LAST = (((1,), (1,)), ((), ()))
PLAIN = (((1,), (0,)), ((), ()))


def dot(left, right, dims=PLAIN):
    return lax.dot_general(left, right, dims, preferred_element_type=jnp.float32)


def local_kernel(kernel, name, outs, args, after=(), flops=0, scalars=0, **more):
    args = list(args)
    in_specs = [pl.BlockSpec(memory_space=pltpu.SMEM)] * scalars + in_vmem(len(args) - scalars)
    count = len(args)
    body = kernel
    if after:
        args += after
        in_specs += [ANYWHERE] * len(after)

        def body(*refs):
            kernel(*refs[:count], *refs[count + len(after) :])

    moved = sum(x.size * x.dtype.itemsize for x in args[:count]) + sum(
        x.size * x.dtype.itemsize for x in outs
    )
    return pl.pallas_call(
        body,
        out_shape=tuple(outs),
        in_specs=in_specs,
        out_specs=tuple(in_vmem(len(outs))),
        compiler_params=compiler_params(),
        cost_estimate=pl.CostEstimate(flops=flops, bytes_accessed=moved, transcendentals=0),
        name=name,
        **more,
    )(*args)


def join(blocks, after=()):
    if blocks[0].shape[0] % 8:
        return jnp.concatenate(blocks, axis=0)

    def kernel(*refs):
        rows = jnp.concatenate([r[...].astype(jnp.float32) for r in refs[:-1]], axis=0)
        refs[-1][...] = rows.astype(jnp.bfloat16)

    one = jax.ShapeDtypeStruct((len(blocks) * blocks[0].shape[0], blocks[0].shape[1]), jnp.bfloat16)
    return local_kernel(kernel, "join", [one], blocks, after)[0]


def halves_of(first, second, half, after):
    if half % 16 or not after:
        return first[:half], second[half:]

    def kernel(first_ref, second_ref, upper_ref, lower_ref):
        upper_ref[...] = first_ref[:half]
        lower_ref[...] = second_ref[half:]

    width = first.shape[1]
    outs = [
        jax.ShapeDtypeStruct((half, width), first.dtype),
        jax.ShapeDtypeStruct((second.shape[0] - half, width), first.dtype),
    ]
    return local_kernel(kernel, "halves", outs, [first, second], after)


def add_half(piece, more, start, after):
    rows = more[0].shape[0]

    def add(whole, terms):
        there = whole[start : start + rows]
        for term in terms:
            there = there + term.astype(jnp.float32)
        parts = [whole[:start], there, whole[start + rows :]]
        return jnp.concatenate([p for p in parts if p.shape[0]], axis=0).astype(jnp.bfloat16)

    if rows % 16:
        return add(piece, more)

    def kernel(piece_ref, *refs):
        refs[-1][...] = add(piece_ref[...], [r[...] for r in refs[:-1]])

    one = jax.ShapeDtypeStruct(piece.shape, jnp.bfloat16)
    return local_kernel(kernel, "add_half", [one], [piece, *more], after)[0]


def add_blocks(piece, more, rows, after):
    count = piece.shape[0] // rows
    types = [jnp.float32] + [jnp.bfloat16] * (count - 1)

    def add(whole, terms):
        for term in terms:
            whole = whole + term.astype(jnp.float32)
        return [whole[s * rows : (s + 1) * rows].astype(t) for s, t in enumerate(types)]

    if rows % 8:
        return add(piece, more)

    def kernel(*refs):
        terms = [r[...] for r in refs[: 1 + len(more)]]
        for ref, block in zip(refs[1 + len(more) :], add(terms[0], terms[1:])):
            ref[...] = block

    outs = [jax.ShapeDtypeStruct((rows, piece.shape[1]), t) for t in types]
    return local_kernel(kernel, "add_blocks", outs, [piece, *more], after)


def add_last(block, more, after):
    def kernel(block_ref, *refs):
        total = block_ref[...]
        for ref in refs[:-1]:
            total = total + ref[...].astype(jnp.float32)
        refs[-1][...] = total

    one = jax.ShapeDtypeStruct(block.shape, jnp.float32)
    return local_kernel(kernel, "add_last", [one], [block, *more], after)[0]


def head_loop(heads, some_heads):
    few = next(u for u in (5, 4, 2, 1) if heads % u == 0)

    def step(g, carry):
        numbers = [g * few + u for u in range(few)]
        some_heads(numbers, [pl.ds(pl.multiple_of(h * HD, HD), HD) for h in numbers])
        return carry

    lax.fori_loop(0, heads // few, step, 0)


def beside(columns, width):
    return [pl.ds(pl.multiple_of(width + c.start, HD), HD) for c in columns]


def stacked(refs, columns):
    return [jnp.concatenate([r[:, c] for r in refs], axis=0) for c in columns]


EXTRA = 16


def extra_rows(gate, slots):
    high = gate.astype(jnp.bfloat16).astype(jnp.float32)
    middle = (gate - high).astype(jnp.bfloat16).astype(jnp.float32)
    none = jnp.zeros((EXTRA - 4, gate.shape[1]), jnp.float32)
    rows = [high, middle, gate - high - middle, slots, none]
    return jnp.concatenate(rows, axis=0).astype(jnp.bfloat16)


def make_queries(x, gain, gate, slots, after):
    tokens, width = x.shape
    half = width // 2

    quarter = half // 2

    def kernel(x_ref, gain_ref, gate_ref, slot_ref, copy_ref, *refs):
        *q_refs, gates_ref = refs
        gate, slots = gate_ref[...], slot_ref[...].astype(jnp.float32)
        copy_ref[:tokens] = x_ref[...]
        copy_ref[tokens:] = jnp.zeros((EXTRA, width), jnp.bfloat16)
        copy_ref[tokens:, :tokens] = extra_rows(gate, slots)
        gates_ref[0:1] = gate
        gates_ref[1:2] = slots
        x = x_ref[...].astype(jnp.float32)
        inverse = lax.rsqrt(jnp.mean(x * x, axis=-1, keepdims=True) + 1e-06)
        for at, ref in zip((0, quarter, half), q_refs):
            columns = slice(at, at + ref.shape[1])
            x = x_ref[:, columns].astype(jnp.float32)
            ref[...] = (x * inverse * gain_ref[:, columns]).astype(jnp.bfloat16)

    part = jax.ShapeDtypeStruct((tokens, quarter), jnp.bfloat16)
    one = jax.ShapeDtypeStruct((tokens, half), jnp.bfloat16)
    same = jax.ShapeDtypeStruct((tokens + EXTRA, width), x.dtype)
    pair = jax.ShapeDtypeStruct((2, tokens), jnp.float32)
    return local_kernel(
        kernel, "queries", [same, part, part, one, pair], [x, gain, gate, slots], after
    )


def cut(x, after):
    tokens, width = x.shape
    widths = [width // 4, width // 4, width // 2]

    def kernel(x_ref, *refs):
        at = 0
        for ref in refs:
            ref[...] = x_ref[:, at : at + ref.shape[1]]
            at += ref.shape[1]

    outs = [jax.ShapeDtypeStruct((tokens, n), x.dtype) for n in widths]
    return local_kernel(kernel, "cut", outs, [x], after)


def choose(section, sections, first_refs, second_ref, out_ref):
    @pl.when(section[0] >= sections // 2)
    def _():
        out_ref[...] = second_ref[...]

    @pl.when(section[0] < sections // 2)
    def _():
        at = 0
        for ref in first_refs:
            out_ref[:, at : at + ref.shape[1]] = ref[...]
            at += ref.shape[1]


def attend(section, sections, first, second, pieces, after):
    tokens, width = second.shape
    heads = width // HD
    rows = sum(p.shape[0] for p in pieces)
    count = len(pieces)

    def kernel(section, *refs):
        *first_refs, second_ref = refs[: len(first) + 1]
        refs = refs[len(first) + 1 :]
        kv_refs, (mixed_ref, p_ref, q_ref) = refs[:count], refs[count:]
        choose(section, sections, first_refs, second_ref, q_ref)

        def some_heads(numbers, columns):
            keys = stacked(kv_refs, columns)
            values = stacked(kv_refs, beside(columns, width))
            scores = [dot(k, q_ref[:, c], LAST) * HD**-0.5 for k, c in zip(keys, columns)]
            e = [jnp.exp(s - jnp.max(s, axis=0, keepdims=True)) for s in scores]
            w = [x * (1.0 / jnp.sum(x, axis=0, keepdims=True)) for x in e]
            mixed = [dot(x.astype(jnp.bfloat16).T, v) for x, v in zip(w, values)]
            for h, c, x, m in zip(numbers, columns, w, mixed):
                p_ref[h] = x
                mixed_ref[:, c] = m.astype(jnp.bfloat16)

        head_loop(heads, some_heads)

    outs = [
        jax.ShapeDtypeStruct((tokens, width), jnp.bfloat16),
        jax.ShapeDtypeStruct((heads, rows, tokens), jnp.float32),
        jax.ShapeDtypeStruct((tokens, width), jnp.bfloat16),
    ]
    args = [section.reshape(1), *first, second, *pieces]
    return local_kernel(
        kernel, "attend", outs, args, after, flops=4 * tokens * rows * width, scalars=1
    )


def gradient(section, sections, q, first, second, p, pieces, heights, types):
    tokens, width = q.shape
    heads, rows, _ = p.shape
    count = len(pieces)

    def kernel(section, q_ref, *refs):
        *first_refs, second_ref, p_ref = refs[: len(first) + 2]
        refs = refs[len(first) + 2 :]
        kv_refs, out_refs, cot_ref = refs[:count], refs[count:-1], refs[-1]
        choose(section, sections, first_refs, second_ref, cot_ref)

        def some_heads(numbers, columns):
            values = stacked(kv_refs, beside(columns, width))
            q = [q_ref[:, c] for c in columns]
            cot = [cot_ref[:, c] for c in columns]
            w = [p_ref[h] for h in numbers]
            dp = [dot(v, c, LAST) for v, c in zip(values, cot)]
            ds = [
                x * (d - jnp.sum(d * x, axis=0, keepdims=True)) * HD**-0.5 for d, x in zip(dp, w)
            ]
            upper = [x.astype(jnp.bfloat16) for x in ds]
            lower = [(x - u.astype(jnp.float32)).astype(jnp.bfloat16) for x, u in zip(ds, upper)]
            dk = [
                dot(jnp.concatenate([u, v], axis=1), jnp.concatenate([x, x], axis=0))
                for u, v, x in zip(upper, lower, q)
            ]
            dv = [dot(x.astype(jnp.bfloat16), c) for x, c in zip(w, cot)]
            for there, grads in ((columns, dk), (beside(columns, width), dv)):
                for c, g in zip(there, grads):
                    at = 0
                    for ref in out_refs:
                        ref[:, c] = g[at : at + ref.shape[0]].astype(ref.dtype)
                        at += ref.shape[0]

        head_loop(heads, some_heads)

    outs = [jax.ShapeDtypeStruct((n, 2 * width), t) for n, t in zip(heights, types)]
    return local_kernel(
        kernel,
        "gradient",
        outs,
        [section.reshape(1), q, *first, second, p, *pieces],
        flops=10 * tokens * rows * width,
        scalars=1,
        scratch_shapes=[pltpu.VMEM((tokens, width), jnp.bfloat16)],
    )


def settle(section, sections, x, first, second, norm_gain, gates, after):
    tokens, width = first.shape[0], x.shape[1]
    half = width // 2

    def kernel(section, x_ref, first_ref, second_ref, norm_ref, gate_ref, res_ref, cap_ref):
        slots = lax.broadcasted_iota(jnp.int32, (CAP, tokens), 0).astype(jnp.float32)
        onehot = jnp.where(gate_ref[1:2] == slots, 1.0, 0.0).astype(jnp.bfloat16)
        attends = jnp.full((tokens, 1), section[0], jnp.int32) >= sections // 2
        chosen = []
        for at, ref in ((0, first_ref), (half, second_ref)):
            mixed = jnp.where(attends, ref[...].astype(jnp.float32), 0.0)
            res = (x_ref[:tokens, at : at + half].astype(jnp.float32) + mixed).astype(jnp.bfloat16)
            res_ref[:, at : at + half] = res
            chosen.append(dot(onehot, res))
        squares = sum(jnp.sum(c * c, axis=-1, keepdims=True) for c in chosen)
        inverse = lax.rsqrt(squares / width + 1e-06)
        for at, c in zip((0, half), chosen):
            rows = (c * inverse * norm_ref[:, at : at + half]).astype(jnp.bfloat16)
            cap_ref[:, at : at + half] = rows

    outs = [
        jax.ShapeDtypeStruct((tokens, width), jnp.bfloat16),
        jax.ShapeDtypeStruct((CAP, width), jnp.bfloat16),
    ]
    return local_kernel(
        kernel, "settle", outs, [section.reshape(1), x, first, second, norm_gain, gates], after,
        scalars=1,
    )


def expert(w1, w2, pieces, heights, types, after):
    width, units = w1.shape
    rows = sum(heights)
    count = len(pieces)
    steps = next(s for s in (4, 2, 1) if width % (s * 128) == 0)
    step = width // steps

    def kernel(w1_ref, w2_ref, *refs):
        in_refs, out_refs = refs[:count], refs[count:]
        parts = [slice(i * step, (i + 1) * step) for i in range(steps)]
        hidden = jnp.zeros((rows, units), jnp.float32)
        for c in parts:
            hidden = hidden + dot(jnp.concatenate([r[:, c] for r in in_refs], axis=0), w1_ref[c, :])
        hidden = jax.nn.gelu(hidden).astype(jnp.bfloat16)
        for c in parts:
            y = dot(hidden, w2_ref[:, c])
            at = 0
            for ref in out_refs:
                ref[:, c] = y[at : at + ref.shape[0]].astype(ref.dtype)
                at += ref.shape[0]

    outs = [jax.ShapeDtypeStruct((n, width), t) for n, t in zip(heights, types)]
    return local_kernel(
        kernel, "expert", outs, [w1, w2, *pieces], after, flops=4 * rows * width * units
    )


def finish(section, res, back, gates=None):
    tokens, width = res.shape[0] - (EXTRA if gates is None else 0), res.shape[1]
    one = jax.ShapeDtypeStruct((tokens, width), jnp.bfloat16)
    step = next(s for s in (1280, 1024, 512, 256, 128) if width % s == 0)
    parts = [slice(at, at + step) for at in range(0, width, step)]

    def kernel(section, res_ref, back_ref, *refs):
        out_any, out_ref, sems = refs[-3:]
        copies = [
            pltpu.make_async_copy(out_ref.at[:, c], out_any.at[:, c], sems.at[i])
            for i, c in enumerate(parts)
        ]

        def compute():
            if gates is None:
                extra = res_ref[tokens:, :tokens].astype(jnp.float32)
                gate, slot = extra[0:1] + extra[1:2] + extra[2:3], extra[3:4]
            else:
                gate, slot = refs[0][0:1], refs[0][1:2]
            gate = jnp.broadcast_to(gate, (CAP, tokens)).T[:, 0:1]
            slots = lax.broadcasted_iota(jnp.int32, (CAP, tokens), 0).astype(jnp.float32)
            onehot = jnp.where(slot == slots, 1.0, 0.0).T
            onehot = jnp.concatenate([onehot] * 3, axis=1).astype(jnp.bfloat16)
            for copy, columns in zip(copies, parts):
                back = back_ref[:, columns]
                high = back.astype(jnp.bfloat16).astype(jnp.float32)
                middle = (back - high).astype(jnp.bfloat16).astype(jnp.float32)
                three = jnp.concatenate([high, middle, back - high - middle], axis=0)
                moved = dot(onehot, three.astype(jnp.bfloat16))
                here = res_ref[:tokens, columns].astype(jnp.float32)
                out_ref[:, columns] = (here + gate * moved).astype(jnp.bfloat16)
                copy.start()

        if gates is None:
            pl.when(section[0] > 0)(compute)

            @pl.when(section[0] == 0)
            def _():
                out_ref[...] = jnp.zeros_like(out_ref)
                for copy in copies:
                    copy.start()
        else:
            compute()
        for copy in copies:
            copy.wait()

    args = [section.reshape(1), res, back] + ([] if gates is None else [gates])
    return pl.pallas_call(
        kernel,
        out_shape=one,
        in_specs=[pl.BlockSpec(memory_space=pltpu.SMEM)] + in_vmem(len(args) - 1),
        out_specs=ANYWHERE,
        scratch_shapes=[
            pltpu.VMEM(one.shape, one.dtype),
            pltpu.SemaphoreType.DMA((len(parts),)),
        ],
        compiler_params=compiler_params(),
        cost_estimate=pl.CostEstimate(
            flops=50 * tokens * width, bytes_accessed=5 * tokens * width, transcendentals=0
        ),
        name="finish",
    )(*args)


def local(
    layer_in, memory, cotangent, norm_gain, attn_gain, expert_in, expert_out, slot_index, gate_prob
):
    sections = lax.axis_size("section")
    section = lax.axis_index("section")
    decoder = section >= sections // 2
    grid = Grid(lax.axis_size("expert"))
    own_rows, _, width = memory[0].shape
    half = width // 2
    heights = grid.heights(own_rows)
    narrow = any(n % 16 for n in heights)

    first = swapped(memory[0, :, :, :half].reshape(own_rows, width))
    second = memory[0, :, :, half:].reshape(own_rows, width)
    pieces = grid.gather(jnp.where(decoder, second, first))
    current, *first, second, gates = make_queries(
        layer_in[0], attn_gain, gate_prob, slot_index, [pieces[0]]
    )
    first = [swapped(q) for q in first]
    *upstream, cot_second = cut(cotangent[0], [gates])
    upstream = [swapped(c) for c in upstream]
    if narrow:
        pieces = [jnp.concatenate(pieces, axis=0)]

    mixed, weights, queries = attend(
        section, sections, first, second, pieces, upstream
    )
    cots = (upstream, cot_second)
    if narrow:
        whole = [sum(heights)], [jnp.float32]
        (whole,) = gradient(section, sections, queries, *cots, weights, pieces, *whole)
        parts, at = [], 0
        for n, t in zip(heights, grid.types()):
            parts.append(whole[at : at + n].astype(t))
            at += n
    else:
        parts = gradient(section, sections, queries, *cots, weights, pieces, heights, grid.types())
    residual, capacity = settle(
        section, sections, current, to_decoder(mixed), mixed, norm_gain, gates, [parts[0]]
    )
    if sections == 2:
        residual_before = passed_along(current, "section", 1)
    else:
        extra = extra_rows(gates[0:1], gates[1:2])
        extra = jnp.pad(extra, ((0, 0), (0, width - extra.shape[1])))
        residual_before = passed_along(jnp.concatenate([residual, extra], axis=0), "section", 1)
    grads = grid.scatter(parts, own_rows)
    halves = next(grads)
    sums = []

    def plane_sums(own):
        if not sums:
            sums.append(grads.send([own])[0])
        return [sums[0][0]]

    gathered = grid.gather(capacity, halves, plane_sums)
    total_grad = grads.send([])
    computed = expert(
        expert_in[0], expert_out[0], gathered, grid.heights(CAP), grid.types(), [total_grad]
    )
    results = grid.scatter(computed, CAP)
    next(results)
    results.send([residual_before])
    returned = results.send([])
    returned_before = passed_along(returned, "section", 1)
    output = finish(section, residual, returned, gates)
    arriving = finish(section, residual_before, returned_before)
    first = to_decoder(total_grad).reshape(own_rows, 2, half)
    total_grad = jnp.concatenate([first, total_grad.reshape(own_rows, 2, half)], axis=2)
    total_grad = jnp.where(decoder, total_grad, 0.0)
    return (output[None], arriving[None], total_grad[None])


def solution(mesh):
    placed = (
        P("section", "expert", None),
        P("section", "expert", None, None),
        P("section", "expert", None),
        P("section", None),
        P("section", None),
        P("section", None, "expert"),
        P("section", "expert", None),
        P("section", "expert"),
        P("section", "expert"),
    )
    return jax.shard_map(
        local,
        mesh=mesh,
        in_specs=placed,
        out_specs=(
            P("section", "expert", None),
            P("section", "expert", None),
            P("section", "expert", None, None),
        ),
        check_vma=False,
    )
```

```python
import functools

import jax
import jax.numpy as jnp
from jax import lax
from jax.experimental import pallas as pl
from jax.experimental.pallas import tpu as pltpu
from jax.sharding import PartitionSpec as P

HD = 128
CAP = 8


def passed_along(block, axis, distance):
    devices = range(lax.axis_size(axis))
    route = [(i - distance, i) for i in devices if i - distance in devices]
    return lax.ppermute(block, axis, route)


def swapped(block):
    sections = lax.axis_size("section")
    return lax.ppermute(block, "section", [(i, (i + sections // 2) % sections) for i in range(sections)])


def to_decoder(block):
    apart = lax.axis_size("section") // 2
    return lax.ppermute(block, "section", [(i, i + apart) for i in range(apart)])


def partner(position, distance, size):
    return position ^ distance if size & (size - 1) == 0 else (position + distance) % size


class Grid:
    def __init__(self, size):
        a = 4 if size % 4 == 0 else 1
        c = 2 if (size // a) % 2 == 0 else 1
        self.sizes = (a, size // a // c, c)
        self.size = size

    def shift(self, block, by, back=False):
        sizes = self.sizes
        route = []
        for index in range(self.size):
            at = (index // (sizes[1] * sizes[2]), index // sizes[2] % sizes[1], index % sizes[2])
            to = [partner(p, d, n) for p, d, n in zip(at, by, sizes)]
            route.append((index, (to[0] * sizes[1] + to[1]) * sizes[2] + to[2]))
        if back:
            route = [(target, source) for source, target in route]
        return lax.ppermute(block, "expert", route)

    def offsets(self):
        _, nb, nc = self.sizes
        return [(b, c) for b in range(nb) for c in range(nc)]

    def heights(self, rows):
        na = self.sizes[0]
        half = rows * (na - na // 2)
        listed = []
        for b, c in self.offsets():
            listed += [half, na * rows - half] if b and c else [na * rows]
        return listed

    def types(self):
        listed = []
        for b, c in self.offsets():
            listed += [jnp.bfloat16] * 2 if b and c else [jnp.float32]
        return listed

    def gather(self, block, first=(), second=lambda own: ()):
        na, nb, nc = self.sizes
        rows = block.shape[0]
        own = join([block] + [self.shift(block, (s, 0, 0)) for s in range(1, na)], first)
        half = rows * (na - na // 2)
        pieces = {(0, 0): [own]}
        for b in range(1, nb):
            pieces[b, 0] = [self.shift(own, (0, b, 0))]
        for c in range(1, nc):
            pieces[0, c] = [self.shift(own, (0, 0, c))]
        for b in range(1, nb):
            for c in range(1, nc):
                upper, lower = halves_of(pieces[b, 0][0], pieces[0, c][0], half, second(own))
                pieces[b, c] = [self.shift(upper, (0, 0, c)), self.shift(lower, (0, b, 0))]
        return sum((pieces[k] for k in self.offsets()), [])

    def scatter(self, pieces, rows, after=()):
        na, nb, nc = self.sizes
        half = rows * (na - na // 2)
        held, at = {}, 0
        for k in self.offsets():
            count = 2 if k[0] and k[1] else 1
            held[k] = pieces[at : at + count]
            at += count
        arrived = []
        for b in range(1, nb):
            more = [self.shift(held[b, c][0], (0, 0, c), back=True) for c in range(1, nc)]
            arrived.append((held[b, 0][0], more, 0, (0, b, 0)))
        for c in range(1, nc):
            more = [self.shift(held[b, c][1], (0, b, 0), back=True) for b in range(1, nb)]
            arrived.append((held[0, c][0], more, half, (0, 0, c)))
        halves = [add_half(piece, more, start, after) for piece, more, start, _ in arrived]
        arrived = [self.shift(piece, by, back=True) for piece, (*_, by) in zip(halves, arrived)]
        after = yield halves
        blocks = add_blocks(held[0, 0][0], arrived, rows, after)
        more = [self.shift(blocks[s], (s, 0, 0), back=True) for s in range(1, na)]
        after = yield blocks, more
        yield add_last(blocks[0], more, after)


def compiler_params():
    return pltpu.CompilerParams(vmem_limit_bytes=20 * 2**20)


def in_vmem(count):
    return [pl.BlockSpec(memory_space=pltpu.VMEM)] * count


ANYWHERE = pl.BlockSpec(memory_space=pl.ANY)
LAST = (((1,), (1,)), ((), ()))
PLAIN = (((1,), (0,)), ((), ()))


def dot(left, right, dims=PLAIN):
    return lax.dot_general(left, right, dims, preferred_element_type=jnp.float32)


def local_kernel(kernel, name, outs, args, after=(), flops=0, scalars=0, **more):
    args = list(args)
    in_specs = [pl.BlockSpec(memory_space=pltpu.SMEM)] * scalars + in_vmem(len(args) - scalars)
    count = len(args)
    body = kernel
    if after:
        args += after
        in_specs += [ANYWHERE] * len(after)

        def body(*refs):
            kernel(*refs[:count], *refs[count + len(after) :])

    moved = sum(x.size * x.dtype.itemsize for x in args[:count]) + sum(
        x.size * x.dtype.itemsize for x in outs
    )
    return pl.pallas_call(
        body,
        out_shape=tuple(outs),
        in_specs=in_specs,
        out_specs=tuple(in_vmem(len(outs))),
        compiler_params=compiler_params(),
        cost_estimate=pl.CostEstimate(flops=flops, bytes_accessed=moved, transcendentals=0),
        name=name,
        **more,
    )(*args)


def join(blocks, after=()):
    if blocks[0].shape[0] % 8:
        return jnp.concatenate(blocks, axis=0)

    def kernel(*refs):
        rows = jnp.concatenate([r[...].astype(jnp.float32) for r in refs[:-1]], axis=0)
        refs[-1][...] = rows.astype(jnp.bfloat16)

    one = jax.ShapeDtypeStruct((len(blocks) * blocks[0].shape[0], blocks[0].shape[1]), jnp.bfloat16)
    return local_kernel(kernel, "join", [one], blocks, after)[0]


def halves_of(first, second, half, after):
    if half % 16 or not after:
        return first[:half], second[half:]

    def kernel(first_ref, second_ref, upper_ref, lower_ref):
        upper_ref[...] = first_ref[:half]
        lower_ref[...] = second_ref[half:]

    width = first.shape[1]
    outs = [
        jax.ShapeDtypeStruct((half, width), first.dtype),
        jax.ShapeDtypeStruct((second.shape[0] - half, width), first.dtype),
    ]
    return local_kernel(kernel, "halves", outs, [first, second], after)


def add_half(piece, more, start, after):
    rows = more[0].shape[0]

    def add(whole, terms):
        there = whole[start : start + rows]
        for term in terms:
            there = there + term.astype(jnp.float32)
        parts = [whole[:start], there, whole[start + rows :]]
        return jnp.concatenate([p for p in parts if p.shape[0]], axis=0).astype(jnp.bfloat16)

    if rows % 16:
        return add(piece, more)

    def kernel(piece_ref, *refs):
        refs[-1][...] = add(piece_ref[...], [r[...] for r in refs[:-1]])

    one = jax.ShapeDtypeStruct(piece.shape, jnp.bfloat16)
    return local_kernel(kernel, "add_half", [one], [piece, *more], after)[0]


def add_blocks(piece, more, rows, after):
    count = piece.shape[0] // rows
    types = [jnp.float32] + [jnp.bfloat16] * (count - 1)

    def add(whole, terms):
        for term in terms:
            whole = whole + term.astype(jnp.float32)
        return [whole[s * rows : (s + 1) * rows].astype(t) for s, t in enumerate(types)]

    if rows % 8:
        return add(piece, more)

    def kernel(*refs):
        terms = [r[...] for r in refs[: 1 + len(more)]]
        for ref, block in zip(refs[1 + len(more) :], add(terms[0], terms[1:])):
            ref[...] = block

    outs = [jax.ShapeDtypeStruct((rows, piece.shape[1]), t) for t in types]
    return local_kernel(kernel, "add_blocks", outs, [piece, *more], after)


def add_last(block, more, after):
    def kernel(block_ref, *refs):
        total = block_ref[...]
        for ref in refs[:-1]:
            total = total + ref[...].astype(jnp.float32)
        refs[-1][...] = total

    one = jax.ShapeDtypeStruct(block.shape, jnp.float32)
    return local_kernel(kernel, "add_last", [one], [block, *more], after)[0]


def head_loop(heads, some_heads):
    few = next(u for u in (5, 4, 2, 1) if heads % u == 0)

    def step(g, carry):
        numbers = [g * few + u for u in range(few)]
        some_heads(numbers, [pl.ds(pl.multiple_of(h * HD, HD), HD) for h in numbers])
        return carry

    lax.fori_loop(0, heads // few, step, 0)


def beside(columns, width):
    return [pl.ds(pl.multiple_of(width + c.start, HD), HD) for c in columns]


def stacked(refs, columns):
    return [jnp.concatenate([r[:, c] for r in refs], axis=0) for c in columns]


EXTRA = 16


def extra_rows(gate, slots):
    high = gate.astype(jnp.bfloat16).astype(jnp.float32)
    middle = (gate - high).astype(jnp.bfloat16).astype(jnp.float32)
    none = jnp.zeros((EXTRA - 4, gate.shape[1]), jnp.float32)
    rows = [high, middle, gate - high - middle, slots, none]
    return jnp.concatenate(rows, axis=0).astype(jnp.bfloat16)


def make_queries(x, gain, gate, slots, after):
    tokens, width = x.shape
    half = width // 2

    quarter = half // 2

    def kernel(x_ref, gain_ref, gate_ref, slot_ref, copy_ref, left_ref, right_ref, *refs):
        *q_refs, gates_ref = refs
        gate, slots = gate_ref[...], slot_ref[...].astype(jnp.float32)
        copy_ref[...] = x_ref[...]
        left_ref[:tokens] = x_ref[:, :half]
        left_ref[tokens:] = jnp.zeros((EXTRA, half), jnp.bfloat16)
        left_ref[tokens:, :tokens] = extra_rows(gate, slots)
        right_ref[...] = x_ref[:, half:]
        gates_ref[0:1] = gate
        gates_ref[1:2] = slots
        x = x_ref[...].astype(jnp.float32)
        inverse = lax.rsqrt(jnp.mean(x * x, axis=-1, keepdims=True) + 1e-06)
        for at, ref in zip((0, quarter, half), q_refs):
            columns = slice(at, at + ref.shape[1])
            x = x_ref[:, columns].astype(jnp.float32)
            ref[...] = (x * inverse * gain_ref[:, columns]).astype(jnp.bfloat16)

    part = jax.ShapeDtypeStruct((tokens, quarter), jnp.bfloat16)
    one = jax.ShapeDtypeStruct((tokens, half), jnp.bfloat16)
    same = jax.ShapeDtypeStruct((tokens, width), x.dtype)
    left = jax.ShapeDtypeStruct((tokens + EXTRA, half), x.dtype)
    right = jax.ShapeDtypeStruct((tokens, half), x.dtype)
    pair = jax.ShapeDtypeStruct((2, tokens), jnp.float32)
    return local_kernel(
        kernel,
        "queries",
        [same, left, right, part, part, one, pair],
        [x, gain, gate, slots],
        after,
    )


def cut(x, after):
    tokens, width = x.shape
    widths = [width // 4, width // 4, width // 2]

    def kernel(x_ref, *refs):
        at = 0
        for ref in refs:
            ref[...] = x_ref[:, at : at + ref.shape[1]]
            at += ref.shape[1]

    outs = [jax.ShapeDtypeStruct((tokens, n), x.dtype) for n in widths]
    return local_kernel(kernel, "cut", outs, [x], after)


def choose(section, sections, first_refs, second_ref, out_ref):
    @pl.when(section[0] >= sections // 2)
    def _():
        out_ref[...] = second_ref[...]

    @pl.when(section[0] < sections // 2)
    def _():
        at = 0
        for ref in first_refs:
            out_ref[:, at : at + ref.shape[1]] = ref[...]
            at += ref.shape[1]


def attend(section, sections, first, second, pieces, after):
    tokens, width = second.shape
    heads = width // HD
    rows = sum(p.shape[0] for p in pieces)
    count = len(pieces)

    def kernel(section, *refs):
        *first_refs, second_ref = refs[: len(first) + 1]
        refs = refs[len(first) + 1 :]
        kv_refs, (mixed_ref, p_ref, q_ref) = refs[:count], refs[count:]
        choose(section, sections, first_refs, second_ref, q_ref)

        def some_heads(numbers, columns):
            keys = stacked(kv_refs, columns)
            values = stacked(kv_refs, beside(columns, width))
            scores = [dot(k, q_ref[:, c], LAST) * HD**-0.5 for k, c in zip(keys, columns)]
            e = [jnp.exp(s - jnp.max(s, axis=0, keepdims=True)) for s in scores]
            w = [x * (1.0 / jnp.sum(x, axis=0, keepdims=True)) for x in e]
            mixed = [dot(x.astype(jnp.bfloat16).T, v) for x, v in zip(w, values)]
            for h, c, x, m in zip(numbers, columns, w, mixed):
                p_ref[h] = x
                mixed_ref[:, c] = m.astype(jnp.bfloat16)

        head_loop(heads, some_heads)

    outs = [
        jax.ShapeDtypeStruct((tokens, width), jnp.bfloat16),
        jax.ShapeDtypeStruct((heads, rows, tokens), jnp.float32),
        jax.ShapeDtypeStruct((tokens, width), jnp.bfloat16),
    ]
    args = [section.reshape(1), *first, second, *pieces]
    return local_kernel(
        kernel, "attend", outs, args, after, flops=4 * tokens * rows * width, scalars=1
    )


def gradient(section, sections, q, first, second, p, pieces, heights, types):
    tokens, width = q.shape
    heads, rows, _ = p.shape
    count = len(pieces)

    def kernel(section, q_ref, *refs):
        *first_refs, second_ref, p_ref = refs[: len(first) + 2]
        refs = refs[len(first) + 2 :]
        kv_refs, out_refs, cot_ref = refs[:count], refs[count:-1], refs[-1]
        choose(section, sections, first_refs, second_ref, cot_ref)

        def some_heads(numbers, columns):
            values = stacked(kv_refs, beside(columns, width))
            q = [q_ref[:, c] for c in columns]
            cot = [cot_ref[:, c] for c in columns]
            w = [p_ref[h] for h in numbers]
            dp = [dot(v, c, LAST) for v, c in zip(values, cot)]
            ds = [
                x * (d - jnp.sum(d * x, axis=0, keepdims=True)) * HD**-0.5 for d, x in zip(dp, w)
            ]
            upper = [x.astype(jnp.bfloat16) for x in ds]
            lower = [(x - u.astype(jnp.float32)).astype(jnp.bfloat16) for x, u in zip(ds, upper)]
            dk = [
                dot(jnp.concatenate([u, v], axis=1), jnp.concatenate([x, x], axis=0))
                for u, v, x in zip(upper, lower, q)
            ]
            dv = [dot(x.astype(jnp.bfloat16), c) for x, c in zip(w, cot)]
            for there, grads in ((columns, dk), (beside(columns, width), dv)):
                for c, g in zip(there, grads):
                    at = 0
                    for ref in out_refs:
                        ref[:, c] = g[at : at + ref.shape[0]].astype(ref.dtype)
                        at += ref.shape[0]

        head_loop(heads, some_heads)

    outs = [jax.ShapeDtypeStruct((n, 2 * width), t) for n, t in zip(heights, types)]
    return local_kernel(
        kernel,
        "gradient",
        outs,
        [section.reshape(1), q, *first, second, p, *pieces],
        flops=10 * tokens * rows * width,
        scalars=1,
        scratch_shapes=[pltpu.VMEM((tokens, width), jnp.bfloat16)],
    )


def settle(section, sections, x, first, second, norm_gain, gates, after):
    tokens, width = first.shape[0], x.shape[1]
    half = width // 2

    def kernel(section, x_ref, first_ref, second_ref, norm_ref, gate_ref, res_ref, cap_ref):
        slots = lax.broadcasted_iota(jnp.int32, (CAP, tokens), 0).astype(jnp.float32)
        onehot = jnp.where(gate_ref[1:2] == slots, 1.0, 0.0).astype(jnp.bfloat16)
        attends = jnp.full((tokens, 1), section[0], jnp.int32) >= sections // 2
        chosen = []
        for at, ref in ((0, first_ref), (half, second_ref)):
            mixed = jnp.where(attends, ref[...].astype(jnp.float32), 0.0)
            res = (x_ref[:tokens, at : at + half].astype(jnp.float32) + mixed).astype(jnp.bfloat16)
            res_ref[:, at : at + half] = res
            chosen.append(dot(onehot, res))
        squares = sum(jnp.sum(c * c, axis=-1, keepdims=True) for c in chosen)
        inverse = lax.rsqrt(squares / width + 1e-06)
        for at, c in zip((0, half), chosen):
            rows = (c * inverse * norm_ref[:, at : at + half]).astype(jnp.bfloat16)
            cap_ref[:, at : at + half] = rows

    outs = [
        jax.ShapeDtypeStruct((tokens, width), jnp.bfloat16),
        jax.ShapeDtypeStruct((CAP, width), jnp.bfloat16),
    ]
    return local_kernel(
        kernel, "settle", outs, [section.reshape(1), x, first, second, norm_gain, gates], after,
        scalars=1,
    )


def expert(w1, w2, pieces, heights, types, after):
    width, units = w1.shape
    rows = sum(heights)
    count = len(pieces)
    steps = next(s for s in (4, 2, 1) if width % (s * 128) == 0)
    step = width // steps

    def kernel(w1_ref, w2_ref, *refs):
        in_refs, out_refs = refs[:count], refs[count:]
        parts = [slice(i * step, (i + 1) * step) for i in range(steps)]
        hidden = jnp.zeros((rows, units), jnp.float32)
        for c in parts:
            hidden = hidden + dot(jnp.concatenate([r[:, c] for r in in_refs], axis=0), w1_ref[c, :])
        hidden = jax.nn.gelu(hidden).astype(jnp.bfloat16)
        for c in parts:
            y = dot(hidden, w2_ref[:, c])
            at = 0
            for ref in out_refs:
                ref[:, c] = y[at : at + ref.shape[0]].astype(ref.dtype)
                at += ref.shape[0]

    outs = [jax.ShapeDtypeStruct((n, width), t) for n, t in zip(heights, types)]
    return local_kernel(
        kernel, "expert", outs, [w1, w2, *pieces], after, flops=4 * rows * width * units
    )


def lay_out(section, sections, first, second):
    rows, width = first.shape
    half = width // 2

    def kernel(section, first_ref, second_ref, out_ref, after_ref):
        decodes = jnp.full((rows, 1), section[0]) >= sections // 2
        after_ref[...] = jnp.zeros_like(after_ref)
        for at, ref in ((0, first_ref), (half, second_ref)):
            for side in (0, 1):
                block = jnp.where(decodes, ref[:, side * half : (side + 1) * half], 0.0)
                out_ref[:, side, at : at + half] = block

    outs = [
        jax.ShapeDtypeStruct((rows, 2, width), jnp.float32),
        jax.ShapeDtypeStruct((8, HD), jnp.float32),
    ]
    return local_kernel(kernel, "lay_out", outs, [section.reshape(1), first, second], scalars=1)


def blank(section, after, like):
    def kernel(section, after_any, out_any, after_ref, zero_ref, sem):
        after_ref[...] = jnp.zeros_like(after_ref)

        @pl.when(section[0] == 0)
        def _():
            zero_ref[...] = jnp.zeros_like(zero_ref)
            copy = pltpu.make_async_copy(zero_ref, out_any, sem)
            copy.start()
            copy.wait()

    return pl.pallas_call(
        kernel,
        out_shape=(
            jax.ShapeDtypeStruct(like.shape, like.dtype),
            jax.ShapeDtypeStruct((8, HD), jnp.float32),
        ),
        in_specs=[pl.BlockSpec(memory_space=pltpu.SMEM), ANYWHERE],
        out_specs=(pl.BlockSpec(memory_space=pltpu.HBM), in_vmem(1)[0]),
        scratch_shapes=[pltpu.VMEM(like.shape, like.dtype), pltpu.SemaphoreType.DMA],
        compiler_params=compiler_params(),
        name="blank",
    )(section.reshape(1), after)


def finish(section, res, back, room=None, gates=None):
    tokens, part = res[-1].shape
    width = part * len(res)
    one = jax.ShapeDtypeStruct((tokens, width), jnp.bfloat16)
    step = next(s for s in (1280, 1024, 512, 256, 128) if part % s == 0)
    parts = [slice(at, at + step) for at in range(0, width, step)]

    def kernel(section, *refs):
        res_refs, (back_ref, last, out_any, out_ref, sems) = refs[: len(res)], refs[len(res) :]

        def compute():
            if gates is None:
                extra = res_refs[0][tokens:, :tokens].astype(jnp.float32)
                gate, slot = extra[0:1] + extra[1:2] + extra[2:3], extra[3:4]
            else:
                gate, slot = last[0:1], last[1:2]
            gate = jnp.broadcast_to(gate, (CAP, tokens)).T[:, 0:1]
            slots = lax.broadcasted_iota(jnp.int32, (CAP, tokens), 0).astype(jnp.float32)
            onehot = jnp.where(slot == slots, 1.0, 0.0).T
            onehot = jnp.concatenate([onehot] * 3, axis=1).astype(jnp.bfloat16)
            copies = []
            for i, columns in enumerate(parts):
                back = back_ref[:, columns]
                high = back.astype(jnp.bfloat16).astype(jnp.float32)
                middle = (back - high).astype(jnp.bfloat16).astype(jnp.float32)
                three = jnp.concatenate([high, middle, back - high - middle], axis=0)
                moved = dot(onehot, three.astype(jnp.bfloat16))
                of, at = divmod(columns.start, part)
                here = res_refs[of][:tokens, at : at + step].astype(jnp.float32)
                out_ref[:, columns] = (here + gate * moved).astype(jnp.bfloat16)
                copy = pltpu.make_async_copy(
                    out_ref.at[:, columns], out_any.at[:, columns], sems.at[i]
                )
                copy.start()
                copies.append(copy)
            for copy in copies:
                copy.wait()

        if gates is None:
            pl.when(section[0] > 0)(compute)
        else:
            compute()

    last = (room, pl.BlockSpec(memory_space=pltpu.HBM)) if gates is None else (gates, in_vmem(1)[0])
    return pl.pallas_call(
        kernel,
        out_shape=one,
        in_specs=[pl.BlockSpec(memory_space=pltpu.SMEM), *in_vmem(len(res) + 1), last[1]],
        out_specs=pl.BlockSpec(memory_space=pltpu.HBM),
        scratch_shapes=[
            pltpu.VMEM(one.shape, one.dtype),
            pltpu.SemaphoreType.DMA((len(parts),)),
        ],
        input_output_aliases={len(res) + 2: 0} if gates is None else {},
        compiler_params=compiler_params(),
        cost_estimate=pl.CostEstimate(
            flops=50 * tokens * width, bytes_accessed=5 * tokens * width, transcendentals=0
        ),
        name="finish",
    )(section.reshape(1), *res, back, last[0])


def local(
    layer_in, memory, cotangent, norm_gain, attn_gain, expert_in, expert_out, slot_index, gate_prob
):
    sections = lax.axis_size("section")
    section = lax.axis_index("section")
    decoder = section >= sections // 2
    grid = Grid(lax.axis_size("expert"))
    own_rows, _, width = memory[0].shape
    half = width // 2
    heights = grid.heights(own_rows)
    narrow = any(n % 16 for n in heights)

    first = swapped(memory[0, :, :, :half].reshape(own_rows, width))
    second = memory[0, :, :, half:].reshape(own_rows, width)
    pieces = grid.gather(jnp.where(decoder, second, first))
    current, left, right, *first, second, gates = make_queries(
        layer_in[0], attn_gain, gate_prob, slot_index, [pieces[0]]
    )
    first = [swapped(q) for q in first]
    *upstream, cot_second = cut(cotangent[0], [gates])
    upstream = [swapped(c) for c in upstream]
    if narrow:
        pieces = [jnp.concatenate(pieces, axis=0)]

    mixed, weights, queries = attend(
        section, sections, first, second, pieces, upstream
    )
    cots = (upstream, cot_second)
    if narrow:
        whole = [sum(heights)], [jnp.float32]
        (whole,) = gradient(section, sections, queries, *cots, weights, pieces, *whole)
        parts, at = [], 0
        for n, t in zip(heights, grid.types()):
            parts.append(whole[at : at + n].astype(t))
            at += n
    else:
        parts = gradient(section, sections, queries, *cots, weights, pieces, heights, grid.types())
    residual, capacity = settle(
        section, sections, current, to_decoder(mixed), mixed, norm_gain, gates, [parts[0]]
    )
    if sections != 2:
        extra = extra_rows(gates[0:1], gates[1:2])
        extra = jnp.pad(extra, ((0, 0), (0, half - extra.shape[1])))
        left, right = jnp.concatenate([residual[:, :half], extra], axis=0), residual[:, half:]
    residual_before = [passed_along(x, "section", 1) for x in (left, right)]
    grads = grid.scatter(parts, own_rows)
    halves = next(grads)
    sums = []

    def plane_sums(own):
        if not sums:
            sums.append(grads.send([own]))
        return [sums[0][0][0]]

    gathered = grid.gather(capacity, halves, plane_sums)
    computed = expert(
        expert_in[0], expert_out[0], gathered, grid.heights(CAP), grid.types(), sums[0][1][:2]
    )
    total_grad = grads.send([computed[0]])
    room, made = blank(section, capacity, residual)
    results = grid.scatter(computed, CAP, [total_grad, made])
    next(results)
    results.send([])
    total_grad, laid = lay_out(section, sections, to_decoder(total_grad), total_grad)
    returned = results.send([laid])
    returned_before = passed_along(returned, "section", 1)
    output = finish(section, [residual], returned, gates=gates)
    arriving = finish(section, residual_before, returned_before, room)
    return (output[None], arriving[None], total_grad[None])


def solution(mesh):
    placed = (
        P("section", "expert", None),
        P("section", "expert", None, None),
        P("section", "expert", None),
        P("section", None),
        P("section", None),
        P("section", None, "expert"),
        P("section", "expert", None),
        P("section", "expert"),
        P("section", "expert"),
    )
    return jax.shard_map(
        local,
        mesh=mesh,
        in_specs=placed,
        out_specs=(
            P("section", "expert", None),
            P("section", "expert", None),
            P("section", "expert", None, None),
        ),
        check_vma=False,
    )
```

```python
import functools

import jax
import jax.numpy as jnp
from jax import lax
from jax.experimental import pallas as pl
from jax.experimental.pallas import tpu as pltpu
from jax.sharding import PartitionSpec as P

HD = 128
CAP = 8


def passed_along(block, axis, distance):
    devices = range(lax.axis_size(axis))
    route = [(i - distance, i) for i in devices if i - distance in devices]
    return lax.ppermute(block, axis, route)


def swapped(block):
    sections = lax.axis_size("section")
    return lax.ppermute(block, "section", [(i, (i + sections // 2) % sections) for i in range(sections)])


def to_decoder(block):
    apart = lax.axis_size("section") // 2
    return lax.ppermute(block, "section", [(i, i + apart) for i in range(apart)])


def partner(position, distance, size):
    return position ^ distance if size & (size - 1) == 0 else (position + distance) % size


class Grid:
    def __init__(self, size):
        a = 4 if size % 4 == 0 else 1
        c = 2 if (size // a) % 2 == 0 else 1
        self.sizes = (a, size // a // c, c)
        self.size = size

    def shift(self, block, by, back=False):
        sizes = self.sizes
        route = []
        for index in range(self.size):
            at = (index // (sizes[1] * sizes[2]), index // sizes[2] % sizes[1], index % sizes[2])
            to = [partner(p, d, n) for p, d, n in zip(at, by, sizes)]
            route.append((index, (to[0] * sizes[1] + to[1]) * sizes[2] + to[2]))
        if back:
            route = [(target, source) for source, target in route]
        return lax.ppermute(block, "expert", route)

    def offsets(self):
        _, nb, nc = self.sizes
        return [(b, c) for b in range(nb) for c in range(nc)]

    def heights(self, rows):
        na = self.sizes[0]
        half = rows * (na - na // 2)
        listed = []
        for b, c in self.offsets():
            listed += [half, na * rows - half] if b and c else [na * rows]
        return listed

    def types(self):
        listed = []
        for b, c in self.offsets():
            listed += [jnp.bfloat16] * 2 if b and c else [jnp.float32]
        return listed

    def gather(self, block, first=(), second=lambda own: ()):
        na, nb, nc = self.sizes
        rows = block.shape[0]
        own = join([block] + [self.shift(block, (s, 0, 0)) for s in range(1, na)], first)
        half = rows * (na - na // 2)
        pieces = {(0, 0): [own]}
        for b in range(1, nb):
            pieces[b, 0] = [self.shift(own, (0, b, 0))]
        for c in range(1, nc):
            pieces[0, c] = [self.shift(own, (0, 0, c))]
        for b in range(1, nb):
            for c in range(1, nc):
                upper, lower = halves_of(pieces[b, 0][0], pieces[0, c][0], half, second(own))
                pieces[b, c] = [self.shift(upper, (0, 0, c)), self.shift(lower, (0, b, 0))]
        return sum((pieces[k] for k in self.offsets()), [])

    def scatter(self, pieces, rows, after=()):
        na, nb, nc = self.sizes
        half = rows * (na - na // 2)
        held, at = {}, 0
        for k in self.offsets():
            count = 2 if k[0] and k[1] else 1
            held[k] = pieces[at : at + count]
            at += count
        arrived = []
        for b in range(1, nb):
            more = [self.shift(held[b, c][0], (0, 0, c), back=True) for c in range(1, nc)]
            arrived.append((held[b, 0][0], more, 0, (0, b, 0)))
        for c in range(1, nc):
            more = [self.shift(held[b, c][1], (0, b, 0), back=True) for b in range(1, nb)]
            arrived.append((held[0, c][0], more, half, (0, 0, c)))
        halves = [add_half(piece, more, start, after) for piece, more, start, _ in arrived]
        arrived = [self.shift(piece, by, back=True) for piece, (*_, by) in zip(halves, arrived)]
        after = yield halves
        blocks = add_blocks(held[0, 0][0], arrived, rows, after)
        more = [self.shift(blocks[s], (s, 0, 0), back=True) for s in range(1, na)]
        after = yield blocks, more
        yield add_last(blocks[0], more, after)


def compiler_params():
    return pltpu.CompilerParams(vmem_limit_bytes=20 * 2**20)


def in_vmem(count):
    return [pl.BlockSpec(memory_space=pltpu.VMEM)] * count


ANYWHERE = pl.BlockSpec(memory_space=pl.ANY)
LAST = (((1,), (1,)), ((), ()))
PLAIN = (((1,), (0,)), ((), ()))


def dot(left, right, dims=PLAIN):
    return lax.dot_general(left, right, dims, preferred_element_type=jnp.float32)


def local_kernel(kernel, name, outs, args, after=(), flops=0, scalars=0, **more):
    args = list(args)
    in_specs = [pl.BlockSpec(memory_space=pltpu.SMEM)] * scalars + in_vmem(len(args) - scalars)
    count = len(args)
    body = kernel
    if after:
        args += after
        in_specs += [ANYWHERE] * len(after)

        def body(*refs):
            kernel(*refs[:count], *refs[count + len(after) :])

    moved = sum(x.size * x.dtype.itemsize for x in args[:count]) + sum(
        x.size * x.dtype.itemsize for x in outs
    )
    return pl.pallas_call(
        body,
        out_shape=tuple(outs),
        in_specs=in_specs,
        out_specs=tuple(in_vmem(len(outs))),
        compiler_params=compiler_params(),
        cost_estimate=pl.CostEstimate(flops=flops, bytes_accessed=moved, transcendentals=0),
        name=name,
        **more,
    )(*args)


def join(blocks, after=()):
    if blocks[0].shape[0] % 8:
        return jnp.concatenate(blocks, axis=0)

    def kernel(*refs):
        rows = jnp.concatenate([r[...].astype(jnp.float32) for r in refs[:-1]], axis=0)
        refs[-1][...] = rows.astype(jnp.bfloat16)

    one = jax.ShapeDtypeStruct((len(blocks) * blocks[0].shape[0], blocks[0].shape[1]), jnp.bfloat16)
    return local_kernel(kernel, "join", [one], blocks, after)[0]


def halves_of(first, second, half, after):
    if half % 16 or not after:
        return first[:half], second[half:]

    def kernel(first_ref, second_ref, upper_ref, lower_ref):
        upper_ref[...] = first_ref[:half]
        lower_ref[...] = second_ref[half:]

    width = first.shape[1]
    outs = [
        jax.ShapeDtypeStruct((half, width), first.dtype),
        jax.ShapeDtypeStruct((second.shape[0] - half, width), first.dtype),
    ]
    return local_kernel(kernel, "halves", outs, [first, second], after)


def add_half(piece, more, start, after):
    rows = more[0].shape[0]

    def add(whole, terms):
        there = whole[start : start + rows]
        for term in terms:
            there = there + term.astype(jnp.float32)
        parts = [whole[:start], there, whole[start + rows :]]
        return jnp.concatenate([p for p in parts if p.shape[0]], axis=0).astype(jnp.bfloat16)

    if rows % 16:
        return add(piece, more)

    def kernel(piece_ref, *refs):
        refs[-1][...] = add(piece_ref[...], [r[...] for r in refs[:-1]])

    one = jax.ShapeDtypeStruct(piece.shape, jnp.bfloat16)
    return local_kernel(kernel, "add_half", [one], [piece, *more], after)[0]


def add_blocks(piece, more, rows, after):
    count = piece.shape[0] // rows
    types = [jnp.float32] + [jnp.bfloat16] * (count - 1)

    def add(whole, terms):
        for term in terms:
            whole = whole + term.astype(jnp.float32)
        return [whole[s * rows : (s + 1) * rows].astype(t) for s, t in enumerate(types)]

    if rows % 8:
        return add(piece, more)

    def kernel(*refs):
        terms = [r[...] for r in refs[: 1 + len(more)]]
        for ref, block in zip(refs[1 + len(more) :], add(terms[0], terms[1:])):
            ref[...] = block

    outs = [jax.ShapeDtypeStruct((rows, piece.shape[1]), t) for t in types]
    return local_kernel(kernel, "add_blocks", outs, [piece, *more], after)


def add_last(block, more, after):
    def kernel(block_ref, *refs):
        total = block_ref[...]
        for ref in refs[:-1]:
            total = total + ref[...].astype(jnp.float32)
        refs[-1][...] = total

    one = jax.ShapeDtypeStruct(block.shape, jnp.float32)
    return local_kernel(kernel, "add_last", [one], [block, *more], after)[0]


def head_loop(heads, some_heads):
    few = next(u for u in (5, 4, 2, 1) if heads % u == 0)

    def step(g, carry):
        numbers = [g * few + u for u in range(few)]
        some_heads(numbers, [pl.ds(pl.multiple_of(h * HD, HD), HD) for h in numbers])
        return carry

    lax.fori_loop(0, heads // few, step, 0)


def beside(columns, width):
    return [pl.ds(pl.multiple_of(width + c.start, HD), HD) for c in columns]


def stacked(refs, columns):
    return [jnp.concatenate([r[:, c] for r in refs], axis=0) for c in columns]


EXTRA = 16


def extra_rows(gate, slots):
    high = gate.astype(jnp.bfloat16).astype(jnp.float32)
    middle = (gate - high).astype(jnp.bfloat16).astype(jnp.float32)
    none = jnp.zeros((EXTRA - 4, gate.shape[1]), jnp.float32)
    rows = [high, middle, gate - high - middle, slots, none]
    return jnp.concatenate(rows, axis=0).astype(jnp.bfloat16)


def make_queries(x, gain, gate, slots, after):
    tokens, width = x.shape
    half = width // 2

    quarter = half // 2

    def kernel(x_ref, gain_ref, gate_ref, slot_ref, copy_ref, left_ref, right_ref, *refs):
        *q_refs, gates_ref = refs
        gate, slots = gate_ref[...], slot_ref[...].astype(jnp.float32)
        copy_ref[...] = x_ref[...]
        left_ref[:tokens] = x_ref[:, :half]
        left_ref[tokens:] = jnp.zeros((EXTRA, half), jnp.bfloat16)
        left_ref[tokens:, :tokens] = extra_rows(gate, slots)
        right_ref[...] = x_ref[:, half:]
        gates_ref[0:1] = gate
        gates_ref[1:2] = slots
        x = x_ref[...].astype(jnp.float32)
        inverse = lax.rsqrt(jnp.mean(x * x, axis=-1, keepdims=True) + 1e-06)
        for at, ref in zip((0, quarter, half), q_refs):
            columns = slice(at, at + ref.shape[1])
            x = x_ref[:, columns].astype(jnp.float32)
            ref[...] = (x * inverse * gain_ref[:, columns]).astype(jnp.bfloat16)

    part = jax.ShapeDtypeStruct((tokens, quarter), jnp.bfloat16)
    one = jax.ShapeDtypeStruct((tokens, half), jnp.bfloat16)
    same = jax.ShapeDtypeStruct((tokens, width), x.dtype)
    left = jax.ShapeDtypeStruct((tokens + EXTRA, half), x.dtype)
    right = jax.ShapeDtypeStruct((tokens, half), x.dtype)
    pair = jax.ShapeDtypeStruct((2, tokens), jnp.float32)
    return local_kernel(
        kernel,
        "queries",
        [same, left, right, part, part, one, pair],
        [x, gain, gate, slots],
        after,
    )


def cut(x, after):
    tokens, width = x.shape
    widths = [width // 4, width // 4, width // 2]

    def kernel(x_ref, *refs):
        at = 0
        for ref in refs:
            ref[...] = x_ref[:, at : at + ref.shape[1]]
            at += ref.shape[1]

    outs = [jax.ShapeDtypeStruct((tokens, n), x.dtype) for n in widths]
    return local_kernel(kernel, "cut", outs, [x], after)


def choose(section, sections, first_refs, second_ref, out_ref):
    @pl.when(section[0] >= sections // 2)
    def _():
        out_ref[...] = second_ref[...]

    @pl.when(section[0] < sections // 2)
    def _():
        at = 0
        for ref in first_refs:
            out_ref[:, at : at + ref.shape[1]] = ref[...]
            at += ref.shape[1]


def attend(section, sections, first, second, pieces, after):
    tokens, width = second.shape
    heads = width // HD
    rows = sum(p.shape[0] for p in pieces)
    count = len(pieces)

    def kernel(section, *refs):
        *first_refs, second_ref = refs[: len(first) + 1]
        refs = refs[len(first) + 1 :]
        kv_refs, (mixed_ref, p_ref, q_ref) = refs[:count], refs[count:]
        choose(section, sections, first_refs, second_ref, q_ref)

        def some_heads(numbers, columns):
            keys = stacked(kv_refs, columns)
            values = stacked(kv_refs, beside(columns, width))
            scores = [dot(k, q_ref[:, c], LAST) * HD**-0.5 for k, c in zip(keys, columns)]
            e = [jnp.exp(s - jnp.max(s, axis=0, keepdims=True)) for s in scores]
            w = [x * (1.0 / jnp.sum(x, axis=0, keepdims=True)) for x in e]
            mixed = [dot(x.astype(jnp.bfloat16).T, v) for x, v in zip(w, values)]
            for h, c, x, m in zip(numbers, columns, w, mixed):
                p_ref[h] = x
                mixed_ref[:, c] = m.astype(jnp.bfloat16)

        head_loop(heads, some_heads)

    outs = [
        jax.ShapeDtypeStruct((tokens, width), jnp.bfloat16),
        jax.ShapeDtypeStruct((heads, rows, tokens), jnp.float32),
        jax.ShapeDtypeStruct((tokens, width), jnp.bfloat16),
    ]
    args = [section.reshape(1), *first, second, *pieces]
    return local_kernel(
        kernel, "attend", outs, args, after, flops=4 * tokens * rows * width, scalars=1
    )


def gradient(section, sections, q, first, second, p, pieces, heights, types):
    tokens, width = q.shape
    heads, rows, _ = p.shape
    count = len(pieces)

    def kernel(section, q_ref, *refs):
        *first_refs, second_ref, p_ref = refs[: len(first) + 2]
        refs = refs[len(first) + 2 :]
        kv_refs, out_refs, cot_ref = refs[:count], refs[count:-1], refs[-1]
        choose(section, sections, first_refs, second_ref, cot_ref)

        def some_heads(numbers, columns):
            values = stacked(kv_refs, beside(columns, width))
            q = [q_ref[:, c] for c in columns]
            cot = [cot_ref[:, c] for c in columns]
            w = [p_ref[h] for h in numbers]
            dp = [dot(v, c, LAST) for v, c in zip(values, cot)]
            ds = [
                x * (d - jnp.sum(d * x, axis=0, keepdims=True)) * HD**-0.5 for d, x in zip(dp, w)
            ]
            upper = [x.astype(jnp.bfloat16) for x in ds]
            lower = [(x - u.astype(jnp.float32)).astype(jnp.bfloat16) for x, u in zip(ds, upper)]
            dk = [
                dot(jnp.concatenate([u, v], axis=1), jnp.concatenate([x, x], axis=0))
                for u, v, x in zip(upper, lower, q)
            ]
            dv = [dot(x.astype(jnp.bfloat16), c) for x, c in zip(w, cot)]
            for there, grads in ((columns, dk), (beside(columns, width), dv)):
                for c, g in zip(there, grads):
                    at = 0
                    for ref in out_refs:
                        ref[:, c] = g[at : at + ref.shape[0]].astype(ref.dtype)
                        at += ref.shape[0]

        head_loop(heads, some_heads)

    outs = [jax.ShapeDtypeStruct((n, 2 * width), t) for n, t in zip(heights, types)]
    return local_kernel(
        kernel,
        "gradient",
        outs,
        [section.reshape(1), q, *first, second, p, *pieces],
        flops=10 * tokens * rows * width,
        scalars=1,
        scratch_shapes=[pltpu.VMEM((tokens, width), jnp.bfloat16)],
    )


def settle(section, sections, x, first, second, norm_gain, gates, after):
    tokens, width = first.shape[0], x.shape[1]
    half = width // 2

    def kernel(section, x_ref, first_ref, second_ref, norm_ref, gate_ref, res_ref, cap_ref):
        slots = lax.broadcasted_iota(jnp.int32, (CAP, tokens), 0).astype(jnp.float32)
        onehot = jnp.where(gate_ref[1:2] == slots, 1.0, 0.0).astype(jnp.bfloat16)
        attends = jnp.full((tokens, 1), section[0], jnp.int32) >= sections // 2
        chosen = []
        for at, ref in ((0, first_ref), (half, second_ref)):
            mixed = jnp.where(attends, ref[...].astype(jnp.float32), 0.0)
            res = (x_ref[:tokens, at : at + half].astype(jnp.float32) + mixed).astype(jnp.bfloat16)
            res_ref[:, at : at + half] = res
            chosen.append(dot(onehot, res))
        squares = sum(jnp.sum(c * c, axis=-1, keepdims=True) for c in chosen)
        inverse = lax.rsqrt(squares / width + 1e-06)
        for at, c in zip((0, half), chosen):
            rows = (c * inverse * norm_ref[:, at : at + half]).astype(jnp.bfloat16)
            cap_ref[:, at : at + half] = rows

    outs = [
        jax.ShapeDtypeStruct((tokens, width), jnp.bfloat16),
        jax.ShapeDtypeStruct((CAP, width), jnp.bfloat16),
    ]
    return local_kernel(
        kernel, "settle", outs, [section.reshape(1), x, first, second, norm_gain, gates], after,
        scalars=1,
    )


def expert(w1, w2, pieces, heights, types, after):
    width, units = w1.shape
    rows = sum(heights)
    count = len(pieces)
    steps = next(s for s in (4, 2, 1) if width % (s * 128) == 0)
    step = width // steps

    def kernel(w1_ref, w2_ref, *refs):
        in_refs, out_refs = refs[:count], refs[count:]
        parts = [slice(i * step, (i + 1) * step) for i in range(steps)]
        hidden = jnp.zeros((rows, units), jnp.float32)
        for c in parts:
            hidden = hidden + dot(jnp.concatenate([r[:, c] for r in in_refs], axis=0), w1_ref[c, :])
        hidden = jax.nn.gelu(hidden).astype(jnp.bfloat16)
        for c in parts:
            y = dot(hidden, w2_ref[:, c])
            at = 0
            for ref in out_refs:
                ref[:, c] = y[at : at + ref.shape[0]].astype(ref.dtype)
                at += ref.shape[0]

    outs = [jax.ShapeDtypeStruct((n, width), t) for n, t in zip(heights, types)]
    return local_kernel(
        kernel, "expert", outs, [w1, w2, *pieces], after, flops=4 * rows * width * units
    )


def lay_out(section, sections, first, second):
    rows, width = first.shape
    half = width // 2

    def kernel(section, first_ref, second_ref, out_ref, after_ref):
        decodes = jnp.full((rows, 1), section[0]) >= sections // 2
        after_ref[...] = jnp.zeros_like(after_ref)
        for at, ref in ((0, first_ref), (half, second_ref)):
            for side in (0, 1):
                block = jnp.where(decodes, ref[:, side * half : (side + 1) * half], 0.0)
                out_ref[:, side, at : at + half] = block

    outs = [
        jax.ShapeDtypeStruct((rows, 2, width), jnp.float32),
        jax.ShapeDtypeStruct((8, HD), jnp.float32),
    ]
    return local_kernel(kernel, "lay_out", outs, [section.reshape(1), first, second], scalars=1)


def blank(section, after, like):
    def kernel(section, after_any, out_any, after_ref, zero_ref, sem):
        after_ref[...] = jnp.zeros_like(after_ref)

        @pl.when(section[0] == 0)
        def _():
            zero_ref[...] = jnp.zeros_like(zero_ref)
            copy = pltpu.make_async_copy(zero_ref, out_any, sem)
            copy.start()
            copy.wait()

    return pl.pallas_call(
        kernel,
        out_shape=(
            jax.ShapeDtypeStruct(like.shape, like.dtype),
            jax.ShapeDtypeStruct((8, HD), jnp.float32),
        ),
        in_specs=[pl.BlockSpec(memory_space=pltpu.SMEM), ANYWHERE],
        out_specs=(pl.BlockSpec(memory_space=pltpu.HBM), in_vmem(1)[0]),
        scratch_shapes=[pltpu.VMEM(like.shape, like.dtype), pltpu.SemaphoreType.DMA],
        compiler_params=compiler_params(),
        name="blank",
    )(section.reshape(1), after)


def finish(section, res, back, room=None, gates=None):
    tokens, part = res[-1].shape
    width = part * len(res)
    one = jax.ShapeDtypeStruct((tokens, width), jnp.bfloat16)
    step = next(s for s in (1280, 1024, 512, 256, 128) if part % s == 0)
    parts = [slice(at, at + step) for at in range(0, width, step)]

    def kernel(section, *refs):
        res_refs, (back_ref, last, out_any, out_ref, sems) = refs[: len(res)], refs[len(res) :]

        def compute():
            if gates is None:
                extra = res_refs[0][tokens:, :tokens].astype(jnp.float32)
                gate, slot = extra[0:1] + extra[1:2] + extra[2:3], extra[3:4]
            else:
                gate, slot = last[0:1], last[1:2]
            gate = jnp.broadcast_to(gate, (CAP, tokens)).T[:, 0:1]
            slots = lax.broadcasted_iota(jnp.int32, (CAP, tokens), 0).astype(jnp.float32)
            onehot = jnp.where(slot == slots, 1.0, 0.0).T
            onehot = jnp.concatenate([onehot] * 3, axis=1).astype(jnp.bfloat16)
            copies = []
            for i, columns in enumerate(parts):
                back = back_ref[:, columns]
                high = back.astype(jnp.bfloat16).astype(jnp.float32)
                middle = (back - high).astype(jnp.bfloat16).astype(jnp.float32)
                three = jnp.concatenate([high, middle, back - high - middle], axis=0)
                moved = dot(onehot, three.astype(jnp.bfloat16))
                of, at = divmod(columns.start, part)
                here = res_refs[of][:tokens, at : at + step].astype(jnp.float32)
                out_ref[:, columns] = (here + gate * moved).astype(jnp.bfloat16)
                copy = pltpu.make_async_copy(
                    out_ref.at[:, columns], out_any.at[:, columns], sems.at[i]
                )
                copy.start()
                copies.append(copy)
            for copy in copies:
                copy.wait()

        if gates is None:
            pl.when(section[0] > 0)(compute)
        else:
            compute()

    last = (room, pl.BlockSpec(memory_space=pltpu.HBM)) if gates is None else (gates, in_vmem(1)[0])
    return pl.pallas_call(
        kernel,
        out_shape=one,
        in_specs=[pl.BlockSpec(memory_space=pltpu.SMEM), *in_vmem(len(res) + 1), last[1]],
        out_specs=pl.BlockSpec(memory_space=pltpu.HBM),
        scratch_shapes=[
            pltpu.VMEM(one.shape, one.dtype),
            pltpu.SemaphoreType.DMA((len(parts),)),
        ],
        input_output_aliases={len(res) + 2: 0} if gates is None else {},
        compiler_params=compiler_params(),
        cost_estimate=pl.CostEstimate(
            flops=50 * tokens * width, bytes_accessed=5 * tokens * width, transcendentals=0
        ),
        name="finish",
    )(section.reshape(1), *res, back, last[0])


def local(
    layer_in, memory, cotangent, norm_gain, attn_gain, expert_in, expert_out, slot_index, gate_prob
):
    sections = lax.axis_size("section")
    section = lax.axis_index("section")
    decoder = section >= sections // 2
    grid = Grid(lax.axis_size("expert"))
    own_rows, _, width = memory[0].shape
    half = width // 2
    heights = grid.heights(own_rows)
    narrow = any(n % 16 for n in heights)

    first = swapped(memory[0, :, :, :half].reshape(own_rows, width))
    second = memory[0, :, :, half:].reshape(own_rows, width)
    pieces = grid.gather(jnp.where(decoder, second, first))
    current, left, right, *first, second, gates = make_queries(
        layer_in[0], attn_gain, gate_prob, slot_index, [pieces[0]]
    )
    first = [swapped(q) for q in first]
    *upstream, cot_second = cut(cotangent[0], [gates])
    upstream = [swapped(c) for c in upstream]
    if narrow:
        pieces = [jnp.concatenate(pieces, axis=0)]

    mixed, weights, queries = attend(
        section, sections, first, second, pieces, upstream
    )
    cots = (upstream, cot_second)
    if narrow:
        whole = [sum(heights)], [jnp.float32]
        (whole,) = gradient(section, sections, queries, *cots, weights, pieces, *whole)
        parts, at = [], 0
        for n, t in zip(heights, grid.types()):
            parts.append(whole[at : at + n].astype(t))
            at += n
    else:
        parts = gradient(section, sections, queries, *cots, weights, pieces, heights, grid.types())
    residual, capacity = settle(
        section, sections, current, to_decoder(mixed), mixed, norm_gain, gates, [parts[0]]
    )
    if sections != 2:
        extra = extra_rows(gates[0:1], gates[1:2])
        extra = jnp.pad(extra, ((0, 0), (0, half - extra.shape[1])))
        left, right = jnp.concatenate([residual[:, :half], extra], axis=0), residual[:, half:]
    residual_before = [passed_along(x, "section", 1) for x in (left, right)]
    grads = grid.scatter(parts, own_rows)
    halves = next(grads)
    sums = []

    def plane_sums(own):
        if not sums:
            sums.append(grads.send([own]))
        return [sums[0][0][0]]

    gathered = grid.gather(capacity, halves, plane_sums)
    computed = expert(
        expert_in[0], expert_out[0], gathered, grid.heights(CAP), grid.types(), sums[0][1][:2]
    )
    total_grad = grads.send([computed[0]])
    room, made = blank(section, capacity, residual)
    results = grid.scatter(computed, CAP)
    next(results)
    results.send([total_grad, made])
    total_grad, laid = lay_out(section, sections, to_decoder(total_grad), total_grad)
    returned = results.send([laid])
    returned_before = passed_along(returned, "section", 1)
    output = finish(section, [residual], returned, gates=gates)
    arriving = finish(section, residual_before, returned_before, room)
    return (output[None], arriving[None], total_grad[None])


def solution(mesh):
    placed = (
        P("section", "expert", None),
        P("section", "expert", None, None),
        P("section", "expert", None),
        P("section", None),
        P("section", None),
        P("section", None, "expert"),
        P("section", "expert", None),
        P("section", "expert"),
        P("section", "expert"),
    )
    return jax.shard_map(
        local,
        mesh=mesh,
        in_specs=placed,
        out_specs=(
            P("section", "expert", None),
            P("section", "expert", None),
            P("section", "expert", None, None),
        ),
        check_vma=False,
    )
```

```python
import functools

import jax
import jax.numpy as jnp
from jax import lax
from jax.experimental import pallas as pl
from jax.experimental.pallas import tpu as pltpu
from jax.sharding import PartitionSpec as P

HD = 128
CAP = 8


def passed_along(block, axis, distance):
    devices = range(lax.axis_size(axis))
    route = [(i - distance, i) for i in devices if i - distance in devices]
    return lax.ppermute(block, axis, route)


def swapped(block):
    sections = lax.axis_size("section")
    return lax.ppermute(block, "section", [(i, (i + sections // 2) % sections) for i in range(sections)])


def to_decoder(block):
    apart = lax.axis_size("section") // 2
    return lax.ppermute(block, "section", [(i, i + apart) for i in range(apart)])


def partner(position, distance, size):
    return position ^ distance if size & (size - 1) == 0 else (position + distance) % size


class Grid:
    def __init__(self, size):
        a = 4 if size % 4 == 0 else 1
        c = 2 if (size // a) % 2 == 0 else 1
        self.sizes = (a, size // a // c, c)
        self.size = size

    def shift(self, block, by, back=False):
        sizes = self.sizes
        route = []
        for index in range(self.size):
            at = (index // (sizes[1] * sizes[2]), index // sizes[2] % sizes[1], index % sizes[2])
            to = [partner(p, d, n) for p, d, n in zip(at, by, sizes)]
            route.append((index, (to[0] * sizes[1] + to[1]) * sizes[2] + to[2]))
        if back:
            route = [(target, source) for source, target in route]
        return lax.ppermute(block, "expert", route)

    def offsets(self):
        _, nb, nc = self.sizes
        return [(b, c) for b in range(nb) for c in range(nc)]

    def heights(self, rows):
        na = self.sizes[0]
        half = rows * (na - na // 2)
        listed = []
        for b, c in self.offsets():
            listed += [half, na * rows - half] if b and c else [na * rows]
        return listed

    def types(self):
        listed = []
        for b, c in self.offsets():
            listed += [jnp.bfloat16] * 2 if b and c else [jnp.float32]
        return listed

    def gather(self, block, first=(), second=lambda own: ()):
        na, nb, nc = self.sizes
        rows = block.shape[0]
        own = join([block] + [self.shift(block, (s, 0, 0)) for s in range(1, na)], first)
        half = rows * (na - na // 2)
        pieces = {(0, 0): [own]}
        for b in range(1, nb):
            pieces[b, 0] = [self.shift(own, (0, b, 0))]
        for c in range(1, nc):
            pieces[0, c] = [self.shift(own, (0, 0, c))]
        for b in range(1, nb):
            for c in range(1, nc):
                upper, lower = halves_of(pieces[b, 0][0], pieces[0, c][0], half, second(own))
                pieces[b, c] = [self.shift(upper, (0, 0, c)), self.shift(lower, (0, b, 0))]
        return sum((pieces[k] for k in self.offsets()), [])

    def scatter(self, pieces, rows, after=(), extra=None):
        na, nb, nc = self.sizes
        half = rows * (na - na // 2)
        held, at = {}, 0
        for k in self.offsets():
            count = 2 if k[0] and k[1] else 1
            held[k] = pieces[at : at + count]
            at += count
        arrived = []
        for b in range(1, nb):
            more = [self.shift(held[b, c][0], (0, 0, c), back=True) for c in range(1, nc)]
            arrived.append((held[b, 0][0], more, 0, (0, b, 0)))
        for c in range(1, nc):
            more = [self.shift(held[b, c][1], (0, b, 0), back=True) for b in range(1, nb)]
            arrived.append((held[0, c][0], more, half, (0, 0, c)))
        halves = [add_half(piece, more, start, after) for piece, more, start, _ in arrived]
        arrived = [self.shift(piece, by, back=True) for piece, (*_, by) in zip(halves, arrived)]
        after = yield halves
        blocks = add_blocks(held[0, 0][0], arrived, rows, after)
        more = [self.shift(blocks[s], (s, 0, 0), back=True) for s in range(1, na)]
        after = yield blocks, more
        yield add_last(blocks[0], more, after, extra)


def compiler_params():
    return pltpu.CompilerParams(vmem_limit_bytes=20 * 2**20)


def in_vmem(count):
    return [pl.BlockSpec(memory_space=pltpu.VMEM)] * count


ANYWHERE = pl.BlockSpec(memory_space=pl.ANY)
LAST = (((1,), (1,)), ((), ()))
PLAIN = (((1,), (0,)), ((), ()))


def dot(left, right, dims=PLAIN):
    return lax.dot_general(left, right, dims, preferred_element_type=jnp.float32)


def local_kernel(kernel, name, outs, args, after=(), flops=0, scalars=0, **more):
    args = list(args)
    in_specs = [pl.BlockSpec(memory_space=pltpu.SMEM)] * scalars + in_vmem(len(args) - scalars)
    count = len(args)
    body = kernel
    if after:
        args += after
        in_specs += [ANYWHERE] * len(after)

        def body(*refs):
            kernel(*refs[:count], *refs[count + len(after) :])

    moved = sum(x.size * x.dtype.itemsize for x in args[:count]) + sum(
        x.size * x.dtype.itemsize for x in outs
    )
    return pl.pallas_call(
        body,
        out_shape=tuple(outs),
        in_specs=in_specs,
        out_specs=tuple(in_vmem(len(outs))),
        compiler_params=compiler_params(),
        cost_estimate=pl.CostEstimate(flops=flops, bytes_accessed=moved, transcendentals=0),
        name=name,
        **more,
    )(*args)


def join(blocks, after=()):
    if blocks[0].shape[0] % 8:
        return jnp.concatenate(blocks, axis=0)

    def kernel(*refs):
        rows = jnp.concatenate([r[...].astype(jnp.float32) for r in refs[:-1]], axis=0)
        refs[-1][...] = rows.astype(jnp.bfloat16)

    one = jax.ShapeDtypeStruct((len(blocks) * blocks[0].shape[0], blocks[0].shape[1]), jnp.bfloat16)
    return local_kernel(kernel, "join", [one], blocks, after)[0]


def halves_of(first, second, half, after):
    if half % 16 or not after:
        return first[:half], second[half:]

    def kernel(first_ref, second_ref, upper_ref, lower_ref):
        upper_ref[...] = first_ref[:half]
        lower_ref[...] = second_ref[half:]

    width = first.shape[1]
    outs = [
        jax.ShapeDtypeStruct((half, width), first.dtype),
        jax.ShapeDtypeStruct((second.shape[0] - half, width), first.dtype),
    ]
    return local_kernel(kernel, "halves", outs, [first, second], after)


def add_half(piece, more, start, after):
    rows = more[0].shape[0]

    def add(whole, terms):
        there = whole[start : start + rows]
        for term in terms:
            there = there + term.astype(jnp.float32)
        parts = [whole[:start], there, whole[start + rows :]]
        return jnp.concatenate([p for p in parts if p.shape[0]], axis=0).astype(jnp.bfloat16)

    if rows % 16:
        return add(piece, more)

    def kernel(piece_ref, *refs):
        refs[-1][...] = add(piece_ref[...], [r[...] for r in refs[:-1]])

    one = jax.ShapeDtypeStruct(piece.shape, jnp.bfloat16)
    return local_kernel(kernel, "add_half", [one], [piece, *more], after)[0]


def add_blocks(piece, more, rows, after):
    count = piece.shape[0] // rows
    types = [jnp.float32] + [jnp.bfloat16] * (count - 1)

    def add(whole, terms):
        for term in terms:
            whole = whole + term.astype(jnp.float32)
        return [whole[s * rows : (s + 1) * rows].astype(t) for s, t in enumerate(types)]

    if rows % 8:
        return add(piece, more)

    def kernel(*refs):
        terms = [r[...] for r in refs[: 1 + len(more)]]
        for ref, block in zip(refs[1 + len(more) :], add(terms[0], terms[1:])):
            ref[...] = block

    outs = [jax.ShapeDtypeStruct((rows, piece.shape[1]), t) for t in types]
    return local_kernel(kernel, "add_blocks", outs, [piece, *more], after)


def add_last(block, more, after, extra=None):
    rows, width = block.shape
    wide = 0 if extra is None else extra.shape[1]

    def kernel(block_ref, *refs):
        total = block_ref[...]
        for ref in refs[: len(more)]:
            total = total + ref[...].astype(jnp.float32)
        refs[-1][:, :width] = total
        if wide:
            refs[-1][:, width:] = jnp.zeros((rows, wide), jnp.float32)
            refs[-1][: extra.shape[0], width:] = refs[len(more)][...]

    one = jax.ShapeDtypeStruct((rows, width + wide), jnp.float32)
    args = [block, *more] + ([extra] if wide else [])
    return local_kernel(kernel, "add_last", [one], args, after)[0]


def head_loop(heads, some_heads):
    few = next(u for u in (5, 4, 2, 1) if heads % u == 0)

    def step(g, carry):
        numbers = [g * few + u for u in range(few)]
        some_heads(numbers, [pl.ds(pl.multiple_of(h * HD, HD), HD) for h in numbers])
        return carry

    lax.fori_loop(0, heads // few, step, 0)


def beside(columns, width):
    return [pl.ds(pl.multiple_of(width + c.start, HD), HD) for c in columns]


def stacked(refs, columns):
    return [jnp.concatenate([r[:, c] for r in refs], axis=0) for c in columns]


def make_queries(x, gain, gate, slots, after):
    tokens, width = x.shape
    half = width // 2

    quarter = half // 2

    def kernel(x_ref, gain_ref, gate_ref, slot_ref, copy_ref, *refs):
        *q_refs, gates_ref = refs
        copy_ref[...] = x_ref[...]
        gates_ref[0:1] = gate_ref[...]
        gates_ref[1:2] = slot_ref[...].astype(jnp.float32)
        x = x_ref[...].astype(jnp.float32)
        inverse = lax.rsqrt(jnp.mean(x * x, axis=-1, keepdims=True) + 1e-06)
        for at, ref in zip((0, quarter, half), q_refs):
            columns = slice(at, at + ref.shape[1])
            x = x_ref[:, columns].astype(jnp.float32)
            ref[...] = (x * inverse * gain_ref[:, columns]).astype(jnp.bfloat16)

    part = jax.ShapeDtypeStruct((tokens, quarter), jnp.bfloat16)
    one = jax.ShapeDtypeStruct((tokens, half), jnp.bfloat16)
    same = jax.ShapeDtypeStruct((tokens, width), x.dtype)
    pair = jax.ShapeDtypeStruct((2, tokens), jnp.float32)
    return local_kernel(
        kernel,
        "queries",
        [same, part, part, one, pair],
        [x, gain, gate, slots],
        after,
    )


def cut(x, after):
    tokens, width = x.shape
    widths = [width // 4, width // 4, width // 2]

    def kernel(x_ref, *refs):
        at = 0
        for ref in refs:
            ref[...] = x_ref[:, at : at + ref.shape[1]]
            at += ref.shape[1]

    outs = [jax.ShapeDtypeStruct((tokens, n), x.dtype) for n in widths]
    return local_kernel(kernel, "cut", outs, [x], after)


def choose(section, sections, first_refs, second_ref, out_ref):
    @pl.when(section[0] >= sections // 2)
    def _():
        out_ref[...] = second_ref[...]

    @pl.when(section[0] < sections // 2)
    def _():
        at = 0
        for ref in first_refs:
            out_ref[:, at : at + ref.shape[1]] = ref[...]
            at += ref.shape[1]


def attend(section, sections, first, second, pieces, after):
    tokens, width = second.shape
    heads = width // HD
    rows = sum(p.shape[0] for p in pieces)
    count = len(pieces)

    def kernel(section, *refs):
        *first_refs, second_ref = refs[: len(first) + 1]
        refs = refs[len(first) + 1 :]
        kv_refs, (mixed_ref, p_ref, q_ref) = refs[:count], refs[count:]
        choose(section, sections, first_refs, second_ref, q_ref)

        def some_heads(numbers, columns):
            keys = stacked(kv_refs, columns)
            values = stacked(kv_refs, beside(columns, width))
            scores = [dot(k, q_ref[:, c], LAST) * HD**-0.5 for k, c in zip(keys, columns)]
            e = [jnp.exp(s - jnp.max(s, axis=0, keepdims=True)) for s in scores]
            w = [x * (1.0 / jnp.sum(x, axis=0, keepdims=True)) for x in e]
            mixed = [dot(x.astype(jnp.bfloat16).T, v) for x, v in zip(w, values)]
            for h, c, x, m in zip(numbers, columns, w, mixed):
                p_ref[h] = x
                mixed_ref[:, c] = m.astype(jnp.bfloat16)

        head_loop(heads, some_heads)

    outs = [
        jax.ShapeDtypeStruct((tokens, width), jnp.bfloat16),
        jax.ShapeDtypeStruct((heads, rows, tokens), jnp.float32),
        jax.ShapeDtypeStruct((tokens, width), jnp.bfloat16),
    ]
    args = [section.reshape(1), *first, second, *pieces]
    return local_kernel(
        kernel, "attend", outs, args, after, flops=4 * tokens * rows * width, scalars=1
    )


def gradient(section, sections, q, first, second, p, pieces, heights, types):
    tokens, width = q.shape
    heads, rows, _ = p.shape
    count = len(pieces)

    def kernel(section, q_ref, *refs):
        *first_refs, second_ref, p_ref = refs[: len(first) + 2]
        refs = refs[len(first) + 2 :]
        kv_refs, out_refs, cot_ref = refs[:count], refs[count:-1], refs[-1]
        choose(section, sections, first_refs, second_ref, cot_ref)

        def some_heads(numbers, columns):
            values = stacked(kv_refs, beside(columns, width))
            q = [q_ref[:, c] for c in columns]
            cot = [cot_ref[:, c] for c in columns]
            w = [p_ref[h] for h in numbers]
            dp = [dot(v, c, LAST) for v, c in zip(values, cot)]
            ds = [
                x * (d - jnp.sum(d * x, axis=0, keepdims=True)) * HD**-0.5 for d, x in zip(dp, w)
            ]
            upper = [x.astype(jnp.bfloat16) for x in ds]
            lower = [(x - u.astype(jnp.float32)).astype(jnp.bfloat16) for x, u in zip(ds, upper)]
            dk = [
                dot(jnp.concatenate([u, v], axis=1), jnp.concatenate([x, x], axis=0))
                for u, v, x in zip(upper, lower, q)
            ]
            dv = [dot(x.astype(jnp.bfloat16), c) for x, c in zip(w, cot)]
            for there, grads in ((columns, dk), (beside(columns, width), dv)):
                for c, g in zip(there, grads):
                    at = 0
                    for ref in out_refs:
                        ref[:, c] = g[at : at + ref.shape[0]].astype(ref.dtype)
                        at += ref.shape[0]

        head_loop(heads, some_heads)

    outs = [jax.ShapeDtypeStruct((n, 2 * width), t) for n, t in zip(heights, types)]
    return local_kernel(
        kernel,
        "gradient",
        outs,
        [section.reshape(1), q, *first, second, p, *pieces],
        flops=10 * tokens * rows * width,
        scalars=1,
        scratch_shapes=[pltpu.VMEM((tokens, width), jnp.bfloat16)],
    )


def settle(section, sections, x, first, second, norm_gain, gates, after):
    tokens, width = first.shape[0], x.shape[1]
    half = width // 2

    def kernel(section, x_ref, first_ref, second_ref, norm_ref, gate_ref, res_ref, cap_ref):
        slots = lax.broadcasted_iota(jnp.int32, (CAP, tokens), 0).astype(jnp.float32)
        onehot = jnp.where(gate_ref[1:2] == slots, 1.0, 0.0).astype(jnp.bfloat16)
        attends = jnp.full((tokens, 1), section[0], jnp.int32) >= sections // 2
        chosen = []
        for at, ref in ((0, first_ref), (half, second_ref)):
            mixed = jnp.where(attends, ref[...].astype(jnp.float32), 0.0)
            res = (x_ref[:tokens, at : at + half].astype(jnp.float32) + mixed).astype(jnp.bfloat16)
            res_ref[:, at : at + half] = res
            chosen.append(dot(onehot, res))
        squares = sum(jnp.sum(c * c, axis=-1, keepdims=True) for c in chosen)
        inverse = lax.rsqrt(squares / width + 1e-06)
        for at, c in zip((0, half), chosen):
            rows = (c * inverse * norm_ref[:, at : at + half]).astype(jnp.bfloat16)
            cap_ref[:, at : at + half] = rows

    outs = [
        jax.ShapeDtypeStruct((tokens, width), jnp.bfloat16),
        jax.ShapeDtypeStruct((CAP, width), jnp.bfloat16),
    ]
    return local_kernel(
        kernel, "settle", outs, [section.reshape(1), x, first, second, norm_gain, gates], after,
        scalars=1,
    )


def expert(w1, w2, pieces, heights, types, after):
    width, units = w1.shape
    rows = sum(heights)
    count = len(pieces)
    steps = next(s for s in (4, 2, 1) if width % (s * 128) == 0)
    step = width // steps

    def kernel(w1_ref, w2_ref, *refs):
        in_refs, out_refs = refs[:count], refs[count:]
        parts = [slice(i * step, (i + 1) * step) for i in range(steps)]
        hidden = jnp.zeros((rows, units), jnp.float32)
        for c in parts:
            hidden = hidden + dot(jnp.concatenate([r[:, c] for r in in_refs], axis=0), w1_ref[c, :])
        hidden = jax.nn.gelu(hidden).astype(jnp.bfloat16)
        for c in parts:
            y = dot(hidden, w2_ref[:, c])
            at = 0
            for ref in out_refs:
                ref[:, c] = y[at : at + ref.shape[0]].astype(ref.dtype)
                at += ref.shape[0]

    outs = [jax.ShapeDtypeStruct((n, width), t) for n, t in zip(heights, types)]
    return local_kernel(
        kernel, "expert", outs, [w1, w2, *pieces], after, flops=4 * rows * width * units
    )


def lay_out(section, sections, first, second):
    rows, width = first.shape
    half = width // 2

    def kernel(section, first_ref, second_ref, out_ref, after_ref):
        decodes = jnp.full((rows, 1), section[0]) >= sections // 2
        after_ref[...] = jnp.zeros_like(after_ref)
        for at, ref in ((0, first_ref), (half, second_ref)):
            for side in (0, 1):
                block = jnp.where(decodes, ref[:, side * half : (side + 1) * half], 0.0)
                out_ref[:, side, at : at + half] = block

    outs = [
        jax.ShapeDtypeStruct((rows, 2, width), jnp.float32),
        jax.ShapeDtypeStruct((8, HD), jnp.float32),
    ]
    return local_kernel(kernel, "lay_out", outs, [section.reshape(1), first, second], scalars=1)


def blank(section, after, like):
    def kernel(section, after_any, out_any, after_ref, zero_ref, sem):
        after_ref[...] = jnp.zeros_like(after_ref)

        @pl.when(section[0] == 0)
        def _():
            zero_ref[...] = jnp.zeros_like(zero_ref)
            copy = pltpu.make_async_copy(zero_ref, out_any, sem)
            copy.start()
            copy.wait()

    return pl.pallas_call(
        kernel,
        out_shape=(
            jax.ShapeDtypeStruct(like.shape, like.dtype),
            jax.ShapeDtypeStruct((8, HD), jnp.float32),
        ),
        in_specs=[pl.BlockSpec(memory_space=pltpu.SMEM), ANYWHERE],
        out_specs=(pl.BlockSpec(memory_space=pltpu.HBM), in_vmem(1)[0]),
        scratch_shapes=[pltpu.VMEM(like.shape, like.dtype), pltpu.SemaphoreType.DMA],
        compiler_params=compiler_params(),
        name="blank",
    )(section.reshape(1), after)


def finish(section, res, back, room=None):
    tokens, width = res.shape
    one = jax.ShapeDtypeStruct((tokens, width), jnp.bfloat16)
    step = next(s for s in (1280, 1024, 512, 256, 128) if width % s == 0)
    parts = [slice(at, at + step) for at in range(0, width, step)]

    def kernel(section, res_ref, back_ref, *refs):
        out_any, out_ref, sems = refs[-3:]

        def compute():
            gate, slot = back_ref[0:1, width:], back_ref[1:2, width:]
            gate = jnp.broadcast_to(gate, (CAP, tokens)).T[:, 0:1]
            slots = lax.broadcasted_iota(jnp.int32, (CAP, tokens), 0).astype(jnp.float32)
            onehot = jnp.where(slot == slots, 1.0, 0.0).T
            onehot = jnp.concatenate([onehot] * 3, axis=1).astype(jnp.bfloat16)
            copies = []
            for i, columns in enumerate(parts):
                back = back_ref[:, columns]
                high = back.astype(jnp.bfloat16).astype(jnp.float32)
                middle = (back - high).astype(jnp.bfloat16).astype(jnp.float32)
                three = jnp.concatenate([high, middle, back - high - middle], axis=0)
                moved = dot(onehot, three.astype(jnp.bfloat16))
                here = res_ref[:, columns].astype(jnp.float32)
                out_ref[:, columns] = (here + gate * moved).astype(jnp.bfloat16)
                copy = pltpu.make_async_copy(
                    out_ref.at[:, columns], out_any.at[:, columns], sems.at[i]
                )
                copy.start()
                copies.append(copy)
            for copy in copies:
                copy.wait()

        if room is None:
            compute()
        else:
            pl.when(section[0] > 0)(compute)

    aliased = [] if room is None else [pl.BlockSpec(memory_space=pltpu.HBM)]
    return pl.pallas_call(
        kernel,
        out_shape=one,
        in_specs=[pl.BlockSpec(memory_space=pltpu.SMEM), *in_vmem(2), *aliased],
        out_specs=pl.BlockSpec(memory_space=pltpu.HBM),
        scratch_shapes=[
            pltpu.VMEM(one.shape, one.dtype),
            pltpu.SemaphoreType.DMA((len(parts),)),
        ],
        input_output_aliases={} if room is None else {3: 0},
        compiler_params=compiler_params(),
        cost_estimate=pl.CostEstimate(
            flops=50 * tokens * width, bytes_accessed=5 * tokens * width, transcendentals=0
        ),
        name="finish",
    )(section.reshape(1), res, back, *([] if room is None else [room]))


def local(
    layer_in, memory, cotangent, norm_gain, attn_gain, expert_in, expert_out, slot_index, gate_prob
):
    sections = lax.axis_size("section")
    section = lax.axis_index("section")
    decoder = section >= sections // 2
    grid = Grid(lax.axis_size("expert"))
    own_rows, _, width = memory[0].shape
    half = width // 2
    heights = grid.heights(own_rows)
    narrow = any(n % 16 for n in heights)

    first = swapped(memory[0, :, :, :half].reshape(own_rows, width))
    second = memory[0, :, :, half:].reshape(own_rows, width)
    pieces = grid.gather(jnp.where(decoder, second, first))
    current, *first, second, gates = make_queries(
        layer_in[0], attn_gain, gate_prob, slot_index, [pieces[0]]
    )
    first = [swapped(q) for q in first]
    *upstream, cot_second = cut(cotangent[0], [gates])
    upstream = [swapped(c) for c in upstream]
    if narrow:
        pieces = [jnp.concatenate(pieces, axis=0)]

    mixed, weights, queries = attend(
        section, sections, first, second, pieces, upstream
    )
    cots = (upstream, cot_second)
    if narrow:
        whole = [sum(heights)], [jnp.float32]
        (whole,) = gradient(section, sections, queries, *cots, weights, pieces, *whole)
        parts, at = [], 0
        for n, t in zip(heights, grid.types()):
            parts.append(whole[at : at + n].astype(t))
            at += n
    else:
        parts = gradient(section, sections, queries, *cots, weights, pieces, heights, grid.types())
    residual, capacity = settle(
        section, sections, current, to_decoder(mixed), mixed, norm_gain, gates, [parts[0]]
    )
    residual_before = passed_along(current if sections == 2 else residual, "section", 1)
    grads = grid.scatter(parts, own_rows)
    halves = next(grads)
    sums = []

    def plane_sums(own):
        if not sums:
            sums.append(grads.send([own]))
        return [sums[0][0][0]]

    gathered = grid.gather(capacity, halves, plane_sums)
    computed = expert(
        expert_in[0], expert_out[0], gathered, grid.heights(CAP), grid.types(), [residual_before, *sums[0][1][:2]]
    )
    total_grad = grads.send([computed[0]])
    room, made = blank(section, capacity, residual)
    results = grid.scatter(computed, CAP, [total_grad], gates)
    next(results)
    results.send([made])
    total_grad, laid = lay_out(section, sections, to_decoder(total_grad), total_grad)
    returned = results.send([laid])
    returned_before = passed_along(returned, "section", 1)
    output = finish(section, residual, returned)
    arriving = finish(section, residual_before, returned_before, room)
    return (output[None], arriving[None], total_grad[None])


def solution(mesh):
    placed = (
        P("section", "expert", None),
        P("section", "expert", None, None),
        P("section", "expert", None),
        P("section", None),
        P("section", None),
        P("section", None, "expert"),
        P("section", "expert", None),
        P("section", "expert"),
        P("section", "expert"),
    )
    return jax.shard_map(
        local,
        mesh=mesh,
        in_specs=placed,
        out_specs=(
            P("section", "expert", None),
            P("section", "expert", None),
            P("section", "expert", None, None),
        ),
        check_vma=False,
    )
```

```python
import functools

import jax
import jax.numpy as jnp
from jax import lax
from jax.experimental import pallas as pl
from jax.experimental.pallas import tpu as pltpu
from jax.sharding import PartitionSpec as P

HD = 128
CAP = 8


def passed_along(block, axis, distance):
    devices = range(lax.axis_size(axis))
    route = [(i - distance, i) for i in devices if i - distance in devices]
    return lax.ppermute(block, axis, route)


def swapped(block):
    sections = lax.axis_size("section")
    return lax.ppermute(block, "section", [(i, (i + sections // 2) % sections) for i in range(sections)])


def to_decoder(block):
    apart = lax.axis_size("section") // 2
    return lax.ppermute(block, "section", [(i, i + apart) for i in range(apart)])


def partner(position, distance, size):
    return position ^ distance if size & (size - 1) == 0 else (position + distance) % size


class Grid:
    def __init__(self, size):
        a = 4 if size % 4 == 0 else 1
        c = 2 if (size // a) % 2 == 0 else 1
        self.sizes = (a, size // a // c, c)
        self.size = size

    def shift(self, block, by, back=False):
        sizes = self.sizes
        route = []
        for index in range(self.size):
            at = (index // (sizes[1] * sizes[2]), index // sizes[2] % sizes[1], index % sizes[2])
            to = [partner(p, d, n) for p, d, n in zip(at, by, sizes)]
            route.append((index, (to[0] * sizes[1] + to[1]) * sizes[2] + to[2]))
        if back:
            route = [(target, source) for source, target in route]
        return lax.ppermute(block, "expert", route)

    def offsets(self):
        _, nb, nc = self.sizes
        return [(b, c) for b in range(nb) for c in range(nc)]

    def heights(self, rows):
        na = self.sizes[0]
        half = rows * (na - na // 2)
        listed = []
        for b, c in self.offsets():
            listed += [half, na * rows - half] if b and c else [na * rows]
        return listed

    def types(self):
        listed = []
        for b, c in self.offsets():
            listed += [jnp.bfloat16] * 2 if b and c else [jnp.float32]
        return listed

    def gather(self, block, first=(), second=lambda own: ()):
        na, nb, nc = self.sizes
        rows = block.shape[0]
        own = join([block] + [self.shift(block, (s, 0, 0)) for s in range(1, na)], first)
        half = rows * (na - na // 2)
        pieces = {(0, 0): [own]}
        for b in range(1, nb):
            pieces[b, 0] = [self.shift(own, (0, b, 0))]
        for c in range(1, nc):
            pieces[0, c] = [self.shift(own, (0, 0, c))]
        for b in range(1, nb):
            for c in range(1, nc):
                upper, lower = halves_of(pieces[b, 0][0], pieces[0, c][0], half, second(own))
                pieces[b, c] = [self.shift(upper, (0, 0, c)), self.shift(lower, (0, b, 0))]
        return sum((pieces[k] for k in self.offsets()), [])

    def scatter(self, pieces, rows, after=(), extra=None):
        na, nb, nc = self.sizes
        half = rows * (na - na // 2)
        held, at = {}, 0
        for k in self.offsets():
            count = 2 if k[0] and k[1] else 1
            held[k] = pieces[at : at + count]
            at += count
        arrived = []
        for b in range(1, nb):
            more = [self.shift(held[b, c][0], (0, 0, c), back=True) for c in range(1, nc)]
            arrived.append((held[b, 0][0], more, 0, (0, b, 0)))
        for c in range(1, nc):
            more = [self.shift(held[b, c][1], (0, b, 0), back=True) for b in range(1, nb)]
            arrived.append((held[0, c][0], more, half, (0, 0, c)))
        halves = [add_half(piece, more, start, after) for piece, more, start, _ in arrived]
        arrived = [self.shift(piece, by, back=True) for piece, (*_, by) in zip(halves, arrived)]
        after = yield halves
        blocks = add_blocks(held[0, 0][0], arrived, rows, after)
        more = [self.shift(blocks[s], (s, 0, 0), back=True) for s in range(1, na)]
        after = yield blocks, more
        yield add_last(blocks[0], more, after, extra)


def compiler_params():
    return pltpu.CompilerParams(vmem_limit_bytes=20 * 2**20)


def in_vmem(count):
    return [pl.BlockSpec(memory_space=pltpu.VMEM)] * count


ANYWHERE = pl.BlockSpec(memory_space=pl.ANY)
LAST = (((1,), (1,)), ((), ()))
PLAIN = (((1,), (0,)), ((), ()))


def dot(left, right, dims=PLAIN):
    return lax.dot_general(left, right, dims, preferred_element_type=jnp.float32)


def local_kernel(kernel, name, outs, args, after=(), flops=0, scalars=0, **more):
    args = list(args)
    in_specs = [pl.BlockSpec(memory_space=pltpu.SMEM)] * scalars + in_vmem(len(args) - scalars)
    count = len(args)
    body = kernel
    if after:
        args += after
        in_specs += [ANYWHERE] * len(after)

        def body(*refs):
            kernel(*refs[:count], *refs[count + len(after) :])

    moved = sum(x.size * x.dtype.itemsize for x in args[:count]) + sum(
        x.size * x.dtype.itemsize for x in outs
    )
    return pl.pallas_call(
        body,
        out_shape=tuple(outs),
        in_specs=in_specs,
        out_specs=tuple(in_vmem(len(outs))),
        compiler_params=compiler_params(),
        cost_estimate=pl.CostEstimate(flops=flops, bytes_accessed=moved, transcendentals=0),
        name=name,
        **more,
    )(*args)


def join(blocks, after=()):
    if blocks[0].shape[0] % 8:
        return jnp.concatenate(blocks, axis=0)

    def kernel(*refs):
        rows = jnp.concatenate([r[...].astype(jnp.float32) for r in refs[:-1]], axis=0)
        refs[-1][...] = rows.astype(jnp.bfloat16)

    one = jax.ShapeDtypeStruct((len(blocks) * blocks[0].shape[0], blocks[0].shape[1]), jnp.bfloat16)
    return local_kernel(kernel, "join", [one], blocks, after)[0]


def halves_of(first, second, half, after):
    if half % 16 or not after:
        return first[:half], second[half:]

    def kernel(first_ref, second_ref, upper_ref, lower_ref):
        upper_ref[...] = first_ref[:half]
        lower_ref[...] = second_ref[half:]

    width = first.shape[1]
    outs = [
        jax.ShapeDtypeStruct((half, width), first.dtype),
        jax.ShapeDtypeStruct((second.shape[0] - half, width), first.dtype),
    ]
    return local_kernel(kernel, "halves", outs, [first, second], after)


def add_half(piece, more, start, after):
    rows = more[0].shape[0]

    def add(whole, terms):
        there = whole[start : start + rows]
        for term in terms:
            there = there + term.astype(jnp.float32)
        parts = [whole[:start], there, whole[start + rows :]]
        return jnp.concatenate([p for p in parts if p.shape[0]], axis=0).astype(jnp.bfloat16)

    if rows % 16:
        return add(piece, more)

    def kernel(piece_ref, *refs):
        refs[-1][...] = add(piece_ref[...], [r[...] for r in refs[:-1]])

    one = jax.ShapeDtypeStruct(piece.shape, jnp.bfloat16)
    return local_kernel(kernel, "add_half", [one], [piece, *more], after)[0]


def add_blocks(piece, more, rows, after):
    count = piece.shape[0] // rows
    types = [jnp.float32] + [jnp.bfloat16] * (count - 1)

    def add(whole, terms):
        for term in terms:
            whole = whole + term.astype(jnp.float32)
        return [whole[s * rows : (s + 1) * rows].astype(t) for s, t in enumerate(types)]

    if rows % 8:
        return add(piece, more)

    def kernel(*refs):
        terms = [r[...] for r in refs[: 1 + len(more)]]
        for ref, block in zip(refs[1 + len(more) :], add(terms[0], terms[1:])):
            ref[...] = block

    outs = [jax.ShapeDtypeStruct((rows, piece.shape[1]), t) for t in types]
    return local_kernel(kernel, "add_blocks", outs, [piece, *more], after)


def add_last(block, more, after, extra=None):
    rows, width = block.shape
    wide = 0 if extra is None else extra.shape[1]

    def kernel(block_ref, *refs):
        total = block_ref[...]
        for ref in refs[: len(more)]:
            total = total + ref[...].astype(jnp.float32)
        refs[-1][:, :width] = total
        if wide:
            refs[-1][:, width:] = jnp.zeros((rows, wide), jnp.float32)
            refs[-1][: extra.shape[0], width:] = refs[len(more)][...]

    one = jax.ShapeDtypeStruct((rows, width + wide), jnp.float32)
    args = [block, *more] + ([extra] if wide else [])
    return local_kernel(kernel, "add_last", [one], args, after)[0]


def head_loop(heads, some_heads):
    few = next(u for u in (5, 4, 2, 1) if heads % u == 0)

    def step(g, carry):
        numbers = [g * few + u for u in range(few)]
        some_heads(numbers, [pl.ds(pl.multiple_of(h * HD, HD), HD) for h in numbers])
        return carry

    lax.fori_loop(0, heads // few, step, 0)


def beside(columns, width):
    return [pl.ds(pl.multiple_of(width + c.start, HD), HD) for c in columns]


def stacked(refs, columns):
    return [jnp.concatenate([r[:, c] for r in refs], axis=0) for c in columns]


def make_queries(x, gain, gate, slots, after):
    tokens, width = x.shape
    half = width // 2

    quarter = half // 2

    def kernel(x_ref, gain_ref, gate_ref, slot_ref, copy_ref, *refs):
        *q_refs, gates_ref = refs
        copy_ref[...] = x_ref[...]
        gates_ref[0:1] = gate_ref[...]
        gates_ref[1:2] = slot_ref[...].astype(jnp.float32)
        x = x_ref[...].astype(jnp.float32)
        inverse = lax.rsqrt(jnp.mean(x * x, axis=-1, keepdims=True) + 1e-06)
        for at, ref in zip((0, quarter, half), q_refs):
            columns = slice(at, at + ref.shape[1])
            x = x_ref[:, columns].astype(jnp.float32)
            ref[...] = (x * inverse * gain_ref[:, columns]).astype(jnp.bfloat16)

    part = jax.ShapeDtypeStruct((tokens, quarter), jnp.bfloat16)
    one = jax.ShapeDtypeStruct((tokens, half), jnp.bfloat16)
    same = jax.ShapeDtypeStruct((tokens, width), x.dtype)
    pair = jax.ShapeDtypeStruct((2, tokens), jnp.float32)
    return local_kernel(
        kernel,
        "queries",
        [same, part, part, one, pair],
        [x, gain, gate, slots],
        after,
    )


def cut(x, after):
    tokens, width = x.shape
    widths = [width // 4, width // 4, width // 2]

    def kernel(x_ref, *refs):
        at = 0
        for ref in refs:
            ref[...] = x_ref[:, at : at + ref.shape[1]]
            at += ref.shape[1]

    outs = [jax.ShapeDtypeStruct((tokens, n), x.dtype) for n in widths]
    return local_kernel(kernel, "cut", outs, [x], after)


def choose(section, sections, first_refs, second_ref, out_ref):
    @pl.when(section[0] >= sections // 2)
    def _():
        out_ref[...] = second_ref[...]

    @pl.when(section[0] < sections // 2)
    def _():
        at = 0
        for ref in first_refs:
            out_ref[:, at : at + ref.shape[1]] = ref[...]
            at += ref.shape[1]


def attend(section, sections, first, second, pieces, after):
    tokens, width = second.shape
    heads = width // HD
    rows = sum(p.shape[0] for p in pieces)
    count = len(pieces)

    def kernel(section, *refs):
        *first_refs, second_ref = refs[: len(first) + 1]
        refs = refs[len(first) + 1 :]
        kv_refs, (mixed_ref, p_ref, q_ref) = refs[:count], refs[count:]
        choose(section, sections, first_refs, second_ref, q_ref)

        def some_heads(numbers, columns):
            keys = stacked(kv_refs, columns)
            values = stacked(kv_refs, beside(columns, width))
            scores = [dot(k, q_ref[:, c], LAST) * HD**-0.5 for k, c in zip(keys, columns)]
            e = [jnp.exp(s - jnp.max(s, axis=0, keepdims=True)) for s in scores]
            w = [x * (1.0 / jnp.sum(x, axis=0, keepdims=True)) for x in e]
            mixed = [dot(x.astype(jnp.bfloat16).T, v) for x, v in zip(w, values)]
            for h, c, x, m in zip(numbers, columns, w, mixed):
                p_ref[h] = x
                mixed_ref[:, c] = m.astype(jnp.bfloat16)

        head_loop(heads, some_heads)

    outs = [
        jax.ShapeDtypeStruct((tokens, width), jnp.bfloat16),
        jax.ShapeDtypeStruct((heads, rows, tokens), jnp.float32),
        jax.ShapeDtypeStruct((tokens, width), jnp.bfloat16),
    ]
    args = [section.reshape(1), *first, second, *pieces]
    return local_kernel(
        kernel, "attend", outs, args, after, flops=4 * tokens * rows * width, scalars=1
    )


def gradient(section, sections, q, first, second, p, pieces, heights, types):
    tokens, width = q.shape
    heads, rows, _ = p.shape
    count = len(pieces)

    def kernel(section, q_ref, *refs):
        *first_refs, second_ref, p_ref = refs[: len(first) + 2]
        refs = refs[len(first) + 2 :]
        kv_refs, out_refs, cot_ref = refs[:count], refs[count:-1], refs[-1]
        choose(section, sections, first_refs, second_ref, cot_ref)

        def some_heads(numbers, columns):
            values = stacked(kv_refs, beside(columns, width))
            q = [q_ref[:, c] for c in columns]
            cot = [cot_ref[:, c] for c in columns]
            w = [p_ref[h] for h in numbers]
            dp = [dot(v, c, LAST) for v, c in zip(values, cot)]
            ds = [
                x * (d - jnp.sum(d * x, axis=0, keepdims=True)) * HD**-0.5 for d, x in zip(dp, w)
            ]
            upper = [x.astype(jnp.bfloat16) for x in ds]
            lower = [(x - u.astype(jnp.float32)).astype(jnp.bfloat16) for x, u in zip(ds, upper)]
            dk = [
                dot(jnp.concatenate([u, v], axis=1), jnp.concatenate([x, x], axis=0))
                for u, v, x in zip(upper, lower, q)
            ]
            dv = [dot(x.astype(jnp.bfloat16), c) for x, c in zip(w, cot)]
            for there, grads in ((columns, dk), (beside(columns, width), dv)):
                for c, g in zip(there, grads):
                    at = 0
                    for ref in out_refs:
                        ref[:, c] = g[at : at + ref.shape[0]].astype(ref.dtype)
                        at += ref.shape[0]

        head_loop(heads, some_heads)

    outs = [jax.ShapeDtypeStruct((n, 2 * width), t) for n, t in zip(heights, types)]
    return local_kernel(
        kernel,
        "gradient",
        outs,
        [section.reshape(1), q, *first, second, p, *pieces],
        flops=10 * tokens * rows * width,
        scalars=1,
        scratch_shapes=[pltpu.VMEM((tokens, width), jnp.bfloat16)],
    )


def settle(section, sections, x, first, second, norm_gain, gates, after):
    tokens, width = first.shape[0], x.shape[1]
    half = width // 2

    def kernel(section, x_ref, first_ref, second_ref, norm_ref, gate_ref, res_ref, cap_ref):
        slots = lax.broadcasted_iota(jnp.int32, (CAP, tokens), 0).astype(jnp.float32)
        onehot = jnp.where(gate_ref[1:2] == slots, 1.0, 0.0).astype(jnp.bfloat16)
        attends = jnp.full((tokens, 1), section[0], jnp.int32) >= sections // 2
        chosen = []
        for at, ref in ((0, first_ref), (half, second_ref)):
            mixed = jnp.where(attends, ref[...].astype(jnp.float32), 0.0)
            res = (x_ref[:tokens, at : at + half].astype(jnp.float32) + mixed).astype(jnp.bfloat16)
            res_ref[:, at : at + half] = res
            chosen.append(dot(onehot, res))
        squares = sum(jnp.sum(c * c, axis=-1, keepdims=True) for c in chosen)
        inverse = lax.rsqrt(squares / width + 1e-06)
        for at, c in zip((0, half), chosen):
            rows = (c * inverse * norm_ref[:, at : at + half]).astype(jnp.bfloat16)
            cap_ref[:, at : at + half] = rows

    outs = [
        jax.ShapeDtypeStruct((tokens, width), jnp.bfloat16),
        jax.ShapeDtypeStruct((CAP, width), jnp.bfloat16),
    ]
    return local_kernel(
        kernel, "settle", outs, [section.reshape(1), x, first, second, norm_gain, gates], after,
        scalars=1,
    )


def expert(w1, w2, pieces, heights, types, after):
    width, units = w1.shape
    rows = sum(heights)
    count = len(pieces)
    steps = next(s for s in (4, 2, 1) if width % (s * 128) == 0)
    step = width // steps

    def kernel(w1_ref, w2_ref, *refs):
        in_refs, out_refs = refs[:count], refs[count:]
        parts = [slice(i * step, (i + 1) * step) for i in range(steps)]
        hidden = jnp.zeros((rows, units), jnp.float32)
        for c in parts:
            hidden = hidden + dot(jnp.concatenate([r[:, c] for r in in_refs], axis=0), w1_ref[c, :])
        hidden = jax.nn.gelu(hidden).astype(jnp.bfloat16)
        for c in parts:
            y = dot(hidden, w2_ref[:, c])
            at = 0
            for ref in out_refs:
                ref[:, c] = y[at : at + ref.shape[0]].astype(ref.dtype)
                at += ref.shape[0]

    outs = [jax.ShapeDtypeStruct((n, width), t) for n, t in zip(heights, types)]
    return local_kernel(
        kernel, "expert", outs, [w1, w2, *pieces], after, flops=4 * rows * width * units
    )


def lay_out(section, sections, first, second):
    rows, width = first.shape
    half = width // 2

    def kernel(section, first_ref, second_ref, out_ref):
        decodes = jnp.full((rows, 1), section[0]) >= sections // 2
        for at, ref in ((0, first_ref), (half, second_ref)):
            for side in (0, 1):
                block = jnp.where(decodes, ref[:, side * half : (side + 1) * half], 0.0)
                out_ref[:, side, at : at + half] = block

    one = jax.ShapeDtypeStruct((rows, 2, width), jnp.float32)
    return local_kernel(kernel, "lay_out", [one], [section.reshape(1), first, second], scalars=1)[0]


def blank(section, after, like):
    def kernel(section, after_any, out_any, after_ref, zero_ref, sem):
        after_ref[...] = jnp.zeros_like(after_ref)

        @pl.when(section[0] == 0)
        def _():
            zero_ref[...] = jnp.zeros_like(zero_ref)
            copy = pltpu.make_async_copy(zero_ref, out_any, sem)
            copy.start()
            copy.wait()

    return pl.pallas_call(
        kernel,
        out_shape=(
            jax.ShapeDtypeStruct(like.shape, like.dtype),
            jax.ShapeDtypeStruct((8, HD), jnp.float32),
        ),
        in_specs=[pl.BlockSpec(memory_space=pltpu.SMEM), ANYWHERE],
        out_specs=(pl.BlockSpec(memory_space=pltpu.HBM), in_vmem(1)[0]),
        scratch_shapes=[pltpu.VMEM(like.shape, like.dtype), pltpu.SemaphoreType.DMA],
        compiler_params=compiler_params(),
        name="blank",
    )(section.reshape(1), after)


def finish(section, res, back, room=None):
    tokens, width = res.shape
    one = jax.ShapeDtypeStruct((tokens, width), jnp.bfloat16)
    step = next(s for s in (1280, 1024, 512, 256, 128) if width % s == 0)
    parts = [slice(at, at + step) for at in range(0, width, step)]

    def kernel(section, res_ref, back_ref, *refs):
        out_any, after_ref, out_ref, sems = refs[-4:]
        after_ref[...] = jnp.zeros_like(after_ref)

        def compute():
            gate, slot = back_ref[0:1, width:], back_ref[1:2, width:]
            gate = jnp.broadcast_to(gate, (CAP, tokens)).T[:, 0:1]
            slots = lax.broadcasted_iota(jnp.int32, (CAP, tokens), 0).astype(jnp.float32)
            onehot = jnp.where(slot == slots, 1.0, 0.0).T
            onehot = jnp.concatenate([onehot] * 3, axis=1).astype(jnp.bfloat16)
            copies = []
            for i, columns in enumerate(parts):
                back = back_ref[:, columns]
                high = back.astype(jnp.bfloat16).astype(jnp.float32)
                middle = (back - high).astype(jnp.bfloat16).astype(jnp.float32)
                three = jnp.concatenate([high, middle, back - high - middle], axis=0)
                moved = dot(onehot, three.astype(jnp.bfloat16))
                here = res_ref[:, columns].astype(jnp.float32)
                out_ref[:, columns] = (here + gate * moved).astype(jnp.bfloat16)
                copy = pltpu.make_async_copy(
                    out_ref.at[:, columns], out_any.at[:, columns], sems.at[i]
                )
                copy.start()
                copies.append(copy)
            for copy in copies:
                copy.wait()

        if room is None:
            compute()
        else:
            pl.when(section[0] > 0)(compute)

    aliased = [] if room is None else [pl.BlockSpec(memory_space=pltpu.HBM)]
    return pl.pallas_call(
        kernel,
        out_shape=(one, jax.ShapeDtypeStruct((8, HD), jnp.float32)),
        in_specs=[pl.BlockSpec(memory_space=pltpu.SMEM), *in_vmem(2), *aliased],
        out_specs=(pl.BlockSpec(memory_space=pltpu.HBM), in_vmem(1)[0]),
        scratch_shapes=[
            pltpu.VMEM(one.shape, one.dtype),
            pltpu.SemaphoreType.DMA((len(parts),)),
        ],
        input_output_aliases={} if room is None else {3: 0},
        compiler_params=compiler_params(),
        cost_estimate=pl.CostEstimate(
            flops=50 * tokens * width, bytes_accessed=5 * tokens * width, transcendentals=0
        ),
        name="finish",
    )(section.reshape(1), res, back, *([] if room is None else [room]))


def local(
    layer_in, memory, cotangent, norm_gain, attn_gain, expert_in, expert_out, slot_index, gate_prob
):
    sections = lax.axis_size("section")
    section = lax.axis_index("section")
    decoder = section >= sections // 2
    grid = Grid(lax.axis_size("expert"))
    own_rows, _, width = memory[0].shape
    half = width // 2
    heights = grid.heights(own_rows)
    narrow = any(n % 16 for n in heights)

    first = swapped(memory[0, :, :, :half].reshape(own_rows, width))
    second = memory[0, :, :, half:].reshape(own_rows, width)
    pieces = grid.gather(jnp.where(decoder, second, first))
    current, *first, second, gates = make_queries(
        layer_in[0], attn_gain, gate_prob, slot_index, [pieces[0]]
    )
    first = [swapped(q) for q in first]
    *upstream, cot_second = cut(cotangent[0], [gates])
    upstream = [swapped(c) for c in upstream]
    if narrow:
        pieces = [jnp.concatenate(pieces, axis=0)]

    mixed, weights, queries = attend(
        section, sections, first, second, pieces, upstream
    )
    cots = (upstream, cot_second)
    if narrow:
        whole = [sum(heights)], [jnp.float32]
        (whole,) = gradient(section, sections, queries, *cots, weights, pieces, *whole)
        parts, at = [], 0
        for n, t in zip(heights, grid.types()):
            parts.append(whole[at : at + n].astype(t))
            at += n
    else:
        parts = gradient(section, sections, queries, *cots, weights, pieces, heights, grid.types())
    residual, capacity = settle(
        section, sections, current, to_decoder(mixed), mixed, norm_gain, gates, [parts[0]]
    )
    residual_before = passed_along(current if sections == 2 else residual, "section", 1)
    grads = grid.scatter(parts, own_rows)
    halves = next(grads)
    room, made = blank(section, capacity, residual)
    sums = []

    def plane_sums(own):
        if not sums:
            sums.append(grads.send([own]))
        return [sums[0][0][0], made]

    gathered = grid.gather(capacity, halves, plane_sums)
    moved = sums[0][1]
    computed = expert(
        expert_in[0], expert_out[0], gathered, grid.heights(CAP), grid.types(),
        [residual_before, *moved[:1]],
    )
    results = grid.scatter(computed, CAP, moved[1:2], gates)
    next(results)
    results.send(moved[2:])
    returned = results.send([])
    returned_before = passed_along(returned, "section", 1)
    output, done = finish(section, residual, returned)
    arriving, _ = finish(section, residual_before, returned_before, room)
    total_grad = grads.send([done])
    total_grad = lay_out(section, sections, to_decoder(total_grad), total_grad)
    return (output[None], arriving[None], total_grad[None])


def solution(mesh):
    placed = (
        P("section", "expert", None),
        P("section", "expert", None, None),
        P("section", "expert", None),
        P("section", None),
        P("section", None),
        P("section", None, "expert"),
        P("section", "expert", None),
        P("section", "expert"),
        P("section", "expert"),
    )
    return jax.shard_map(
        local,
        mesh=mesh,
        in_specs=placed,
        out_specs=(
            P("section", "expert", None),
            P("section", "expert", None),
            P("section", "expert", None, None),
        ),
        check_vma=False,
    )
```

```python
import functools

import jax
import jax.numpy as jnp
from jax import lax
from jax.experimental import pallas as pl
from jax.experimental.pallas import tpu as pltpu
from jax.sharding import PartitionSpec as P

HD = 128
CAP = 8


def passed_along(block, axis, distance):
    devices = range(lax.axis_size(axis))
    route = [(i - distance, i) for i in devices if i - distance in devices]
    return lax.ppermute(block, axis, route)


def swapped(block):
    sections = lax.axis_size("section")
    return lax.ppermute(block, "section", [(i, (i + sections // 2) % sections) for i in range(sections)])


def to_decoder(block):
    apart = lax.axis_size("section") // 2
    return lax.ppermute(block, "section", [(i, i + apart) for i in range(apart)])


def partner(position, distance, size):
    return position ^ distance if size & (size - 1) == 0 else (position + distance) % size


class Grid:
    def __init__(self, size):
        a = 4 if size % 4 == 0 else 1
        c = 2 if (size // a) % 2 == 0 else 1
        self.sizes = (a, size // a // c, c)
        self.size = size

    def shift(self, block, by, back=False):
        sizes = self.sizes
        route = []
        for index in range(self.size):
            at = (index // (sizes[1] * sizes[2]), index // sizes[2] % sizes[1], index % sizes[2])
            to = [partner(p, d, n) for p, d, n in zip(at, by, sizes)]
            route.append((index, (to[0] * sizes[1] + to[1]) * sizes[2] + to[2]))
        if back:
            route = [(target, source) for source, target in route]
        return lax.ppermute(block, "expert", route)

    def offsets(self):
        _, nb, nc = self.sizes
        return [(b, c) for b in range(nb) for c in range(nc)]

    def heights(self, rows):
        na = self.sizes[0]
        half = rows * (na - na // 2)
        listed = []
        for b, c in self.offsets():
            listed += [half, na * rows - half] if b and c else [na * rows]
        return listed

    def types(self):
        listed = []
        for b, c in self.offsets():
            listed += [jnp.bfloat16] * 2 if b and c else [jnp.float32]
        return listed

    def gather(self, block, first=(), second=lambda own: ()):
        na, nb, nc = self.sizes
        rows = block.shape[0]
        own = join([block] + [self.shift(block, (s, 0, 0)) for s in range(1, na)], first)
        half = rows * (na - na // 2)
        pieces = {(0, 0): [own]}
        for b in range(1, nb):
            pieces[b, 0] = [self.shift(own, (0, b, 0))]
        for c in range(1, nc):
            pieces[0, c] = [self.shift(own, (0, 0, c))]
        for b in range(1, nb):
            for c in range(1, nc):
                upper, lower = halves_of(pieces[b, 0][0], pieces[0, c][0], half, second(own))
                pieces[b, c] = [self.shift(upper, (0, 0, c)), self.shift(lower, (0, b, 0))]
        return sum((pieces[k] for k in self.offsets()), [])

    def scatter(self, pieces, rows, after=(), extra=None):
        na, nb, nc = self.sizes
        half = rows * (na - na // 2)
        held, at = {}, 0
        for k in self.offsets():
            count = 2 if k[0] and k[1] else 1
            held[k] = pieces[at : at + count]
            at += count
        arrived = []
        for b in range(1, nb):
            more = [self.shift(held[b, c][0], (0, 0, c), back=True) for c in range(1, nc)]
            arrived.append((held[b, 0][0], more, 0, (0, b, 0)))
        for c in range(1, nc):
            more = [self.shift(held[b, c][1], (0, b, 0), back=True) for b in range(1, nb)]
            arrived.append((held[0, c][0], more, half, (0, 0, c)))
        halves = [add_half(piece, more, start, after) for piece, more, start, _ in arrived]
        arrived = [self.shift(piece, by, back=True) for piece, (*_, by) in zip(halves, arrived)]
        after = yield halves
        blocks = add_blocks(held[0, 0][0], arrived, rows, after)
        more = [self.shift(blocks[s], (s, 0, 0), back=True) for s in range(1, na)]
        after = yield blocks, more
        yield add_last(blocks[0], more, after, extra)


def compiler_params():
    return pltpu.CompilerParams(vmem_limit_bytes=20 * 2**20)


def in_vmem(count):
    return [pl.BlockSpec(memory_space=pltpu.VMEM)] * count


ANYWHERE = pl.BlockSpec(memory_space=pl.ANY)
LAST = (((1,), (1,)), ((), ()))
PLAIN = (((1,), (0,)), ((), ()))


def dot(left, right, dims=PLAIN):
    return lax.dot_general(left, right, dims, preferred_element_type=jnp.float32)


def local_kernel(kernel, name, outs, args, after=(), flops=0, scalars=0, **more):
    args = list(args)
    in_specs = [pl.BlockSpec(memory_space=pltpu.SMEM)] * scalars + in_vmem(len(args) - scalars)
    count = len(args)
    body = kernel
    if after:
        args += after
        in_specs += [ANYWHERE] * len(after)

        def body(*refs):
            kernel(*refs[:count], *refs[count + len(after) :])

    moved = sum(x.size * x.dtype.itemsize for x in args[:count]) + sum(
        x.size * x.dtype.itemsize for x in outs
    )
    return pl.pallas_call(
        body,
        out_shape=tuple(outs),
        in_specs=in_specs,
        out_specs=tuple(in_vmem(len(outs))),
        compiler_params=compiler_params(),
        cost_estimate=pl.CostEstimate(flops=flops, bytes_accessed=moved, transcendentals=0),
        name=name,
        **more,
    )(*args)


def join(blocks, after=()):
    if blocks[0].shape[0] % 8:
        return jnp.concatenate(blocks, axis=0)

    def kernel(*refs):
        rows = jnp.concatenate([r[...].astype(jnp.float32) for r in refs[:-1]], axis=0)
        refs[-1][...] = rows.astype(jnp.bfloat16)

    one = jax.ShapeDtypeStruct((len(blocks) * blocks[0].shape[0], blocks[0].shape[1]), jnp.bfloat16)
    return local_kernel(kernel, "join", [one], blocks, after)[0]


def halves_of(first, second, half, after):
    if half % 16 or not after:
        return first[:half], second[half:]

    def kernel(first_ref, second_ref, upper_ref, lower_ref):
        upper_ref[...] = first_ref[:half]
        lower_ref[...] = second_ref[half:]

    width = first.shape[1]
    outs = [
        jax.ShapeDtypeStruct((half, width), first.dtype),
        jax.ShapeDtypeStruct((second.shape[0] - half, width), first.dtype),
    ]
    return local_kernel(kernel, "halves", outs, [first, second], after)


def add_half(piece, more, start, after):
    rows = more[0].shape[0]

    def add(whole, terms):
        there = whole[start : start + rows]
        for term in terms:
            there = there + term.astype(jnp.float32)
        parts = [whole[:start], there, whole[start + rows :]]
        return jnp.concatenate([p for p in parts if p.shape[0]], axis=0).astype(jnp.bfloat16)

    if rows % 16:
        return add(piece, more)

    def kernel(piece_ref, *refs):
        refs[-1][...] = add(piece_ref[...], [r[...] for r in refs[:-1]])

    one = jax.ShapeDtypeStruct(piece.shape, jnp.bfloat16)
    return local_kernel(kernel, "add_half", [one], [piece, *more], after)[0]


def add_blocks(piece, more, rows, after):
    count = piece.shape[0] // rows
    types = [jnp.float32] + [jnp.bfloat16] * (count - 1)

    def add(whole, terms):
        for term in terms:
            whole = whole + term.astype(jnp.float32)
        return [whole[s * rows : (s + 1) * rows].astype(t) for s, t in enumerate(types)]

    if rows % 8:
        return add(piece, more)

    def kernel(*refs):
        terms = [r[...] for r in refs[: 1 + len(more)]]
        for ref, block in zip(refs[1 + len(more) :], add(terms[0], terms[1:])):
            ref[...] = block

    outs = [jax.ShapeDtypeStruct((rows, piece.shape[1]), t) for t in types]
    return local_kernel(kernel, "add_blocks", outs, [piece, *more], after)


def add_last(block, more, after, extra=None):
    rows, width = block.shape
    wide = 0 if extra is None else extra.shape[1]

    def kernel(block_ref, *refs):
        total = block_ref[...]
        for ref in refs[: len(more)]:
            total = total + ref[...].astype(jnp.float32)
        refs[-1][:, :width] = total
        if wide:
            refs[-1][:, width:] = jnp.zeros((rows, wide), jnp.float32)
            refs[-1][: extra.shape[0], width:] = refs[len(more)][...]

    one = jax.ShapeDtypeStruct((rows, width + wide), jnp.float32)
    args = [block, *more] + ([extra] if wide else [])
    return local_kernel(kernel, "add_last", [one], args, after)[0]


def head_loop(heads, some_heads):
    few = next(u for u in (10, 5, 4, 2, 1) if heads % u == 0)

    def step(g, carry):
        numbers = [g * few + u for u in range(few)]
        some_heads(numbers, [pl.ds(pl.multiple_of(h * HD, HD), HD) for h in numbers])
        return carry

    lax.fori_loop(0, heads // few, step, 0)


def beside(columns, width):
    return [pl.ds(pl.multiple_of(width + c.start, HD), HD) for c in columns]


def stacked(refs, columns):
    return [jnp.concatenate([r[:, c] for r in refs], axis=0) for c in columns]


def make_queries(x, gain, gate, slots, after):
    tokens, width = x.shape
    half = width // 2

    quarter = half // 2

    def kernel(x_ref, gain_ref, gate_ref, slot_ref, copy_ref, *refs):
        *q_refs, gates_ref = refs
        copy_ref[...] = x_ref[...]
        gates_ref[0:1] = gate_ref[...]
        gates_ref[1:2] = slot_ref[...].astype(jnp.float32)
        x = x_ref[...].astype(jnp.float32)
        inverse = lax.rsqrt(jnp.mean(x * x, axis=-1, keepdims=True) + 1e-06)
        for at, ref in zip((0, quarter, half), q_refs):
            columns = slice(at, at + ref.shape[1])
            x = x_ref[:, columns].astype(jnp.float32)
            ref[...] = (x * inverse * gain_ref[:, columns]).astype(jnp.bfloat16)

    part = jax.ShapeDtypeStruct((tokens, quarter), jnp.bfloat16)
    one = jax.ShapeDtypeStruct((tokens, half), jnp.bfloat16)
    same = jax.ShapeDtypeStruct((tokens, width), x.dtype)
    pair = jax.ShapeDtypeStruct((2, tokens), jnp.float32)
    return local_kernel(
        kernel,
        "queries",
        [same, part, part, one, pair],
        [x, gain, gate, slots],
        after,
    )


def cut(x, after):
    tokens, width = x.shape
    widths = [width // 4, width // 4, width // 2]

    def kernel(x_ref, *refs):
        at = 0
        for ref in refs:
            ref[...] = x_ref[:, at : at + ref.shape[1]]
            at += ref.shape[1]

    outs = [jax.ShapeDtypeStruct((tokens, n), x.dtype) for n in widths]
    return local_kernel(kernel, "cut", outs, [x], after)


def choose(section, sections, first_refs, second_ref, out_ref):
    @pl.when(section[0] >= sections // 2)
    def _():
        out_ref[...] = second_ref[...]

    @pl.when(section[0] < sections // 2)
    def _():
        at = 0
        for ref in first_refs:
            out_ref[:, at : at + ref.shape[1]] = ref[...]
            at += ref.shape[1]


def attend(section, sections, first, second, pieces, after):
    tokens, width = second.shape
    heads = width // HD
    rows = sum(p.shape[0] for p in pieces)
    count = len(pieces)

    def kernel(section, *refs):
        *first_refs, second_ref = refs[: len(first) + 1]
        refs = refs[len(first) + 1 :]
        kv_refs, (mixed_ref, p_ref, q_ref) = refs[:count], refs[count:]
        choose(section, sections, first_refs, second_ref, q_ref)

        def some_heads(numbers, columns):
            keys = stacked(kv_refs, columns)
            values = stacked(kv_refs, beside(columns, width))
            scores = [dot(k, q_ref[:, c], LAST) * HD**-0.5 for k, c in zip(keys, columns)]
            e = [jnp.exp(s - jnp.max(s, axis=0, keepdims=True)) for s in scores]
            w = [x * (1.0 / jnp.sum(x, axis=0, keepdims=True)) for x in e]
            mixed = [dot(x.astype(jnp.bfloat16).T, v) for x, v in zip(w, values)]
            for h, c, x, m in zip(numbers, columns, w, mixed):
                p_ref[h] = x
                mixed_ref[:, c] = m.astype(jnp.bfloat16)

        head_loop(heads, some_heads)

    outs = [
        jax.ShapeDtypeStruct((tokens, width), jnp.bfloat16),
        jax.ShapeDtypeStruct((heads, rows, tokens), jnp.float32),
        jax.ShapeDtypeStruct((tokens, width), jnp.bfloat16),
    ]
    args = [section.reshape(1), *first, second, *pieces]
    return local_kernel(
        kernel, "attend", outs, args, after, flops=4 * tokens * rows * width, scalars=1
    )


def gradient(section, sections, q, first, second, p, pieces, heights, types):
    tokens, width = q.shape
    heads, rows, _ = p.shape
    count = len(pieces)

    def kernel(section, q_ref, *refs):
        *first_refs, second_ref, p_ref = refs[: len(first) + 2]
        refs = refs[len(first) + 2 :]
        kv_refs, out_refs, cot_ref = refs[:count], refs[count:-1], refs[-1]
        choose(section, sections, first_refs, second_ref, cot_ref)

        def some_heads(numbers, columns):
            values = stacked(kv_refs, beside(columns, width))
            q = [q_ref[:, c] for c in columns]
            cot = [cot_ref[:, c] for c in columns]
            w = [p_ref[h] for h in numbers]
            dp = [dot(v, c, LAST) for v, c in zip(values, cot)]
            ds = [
                x * (d - jnp.sum(d * x, axis=0, keepdims=True)) * HD**-0.5 for d, x in zip(dp, w)
            ]
            upper = [x.astype(jnp.bfloat16) for x in ds]
            lower = [(x - u.astype(jnp.float32)).astype(jnp.bfloat16) for x, u in zip(ds, upper)]
            dk = [
                dot(jnp.concatenate([u, v], axis=1), jnp.concatenate([x, x], axis=0))
                for u, v, x in zip(upper, lower, q)
            ]
            dv = [dot(x.astype(jnp.bfloat16), c) for x, c in zip(w, cot)]
            for there, grads in ((columns, dk), (beside(columns, width), dv)):
                for c, g in zip(there, grads):
                    at = 0
                    for ref in out_refs:
                        ref[:, c] = g[at : at + ref.shape[0]].astype(ref.dtype)
                        at += ref.shape[0]

        head_loop(heads, some_heads)

    outs = [jax.ShapeDtypeStruct((n, 2 * width), t) for n, t in zip(heights, types)]
    return local_kernel(
        kernel,
        "gradient",
        outs,
        [section.reshape(1), q, *first, second, p, *pieces],
        flops=10 * tokens * rows * width,
        scalars=1,
        scratch_shapes=[pltpu.VMEM((tokens, width), jnp.bfloat16)],
    )


def settle(section, sections, x, first, second, norm_gain, gates, after):
    tokens, width = first.shape[0], x.shape[1]
    half = width // 2

    def kernel(section, x_ref, first_ref, second_ref, norm_ref, gate_ref, res_ref, cap_ref):
        slots = lax.broadcasted_iota(jnp.int32, (CAP, tokens), 0).astype(jnp.float32)
        onehot = jnp.where(gate_ref[1:2] == slots, 1.0, 0.0).astype(jnp.bfloat16)
        attends = jnp.full((tokens, 1), section[0], jnp.int32) >= sections // 2
        chosen = []
        for at, ref in ((0, first_ref), (half, second_ref)):
            mixed = jnp.where(attends, ref[...].astype(jnp.float32), 0.0)
            res = (x_ref[:tokens, at : at + half].astype(jnp.float32) + mixed).astype(jnp.bfloat16)
            res_ref[:, at : at + half] = res
            chosen.append(dot(onehot, res))
        squares = sum(jnp.sum(c * c, axis=-1, keepdims=True) for c in chosen)
        inverse = lax.rsqrt(squares / width + 1e-06)
        for at, c in zip((0, half), chosen):
            rows = (c * inverse * norm_ref[:, at : at + half]).astype(jnp.bfloat16)
            cap_ref[:, at : at + half] = rows

    outs = [
        jax.ShapeDtypeStruct((tokens, width), jnp.bfloat16),
        jax.ShapeDtypeStruct((CAP, width), jnp.bfloat16),
    ]
    return local_kernel(
        kernel, "settle", outs, [section.reshape(1), x, first, second, norm_gain, gates], after,
        scalars=1,
    )


def expert(w1, w2, pieces, heights, types, after):
    width, units = w1.shape
    rows = sum(heights)
    count = len(pieces)
    steps = next(s for s in (4, 2, 1) if width % (s * 128) == 0)
    step = width // steps

    def kernel(w1_ref, w2_ref, *refs):
        in_refs, out_refs = refs[:count], refs[count:]
        parts = [slice(i * step, (i + 1) * step) for i in range(steps)]
        hidden = jnp.zeros((rows, units), jnp.float32)
        for c in parts:
            hidden = hidden + dot(jnp.concatenate([r[:, c] for r in in_refs], axis=0), w1_ref[c, :])
        hidden = jax.nn.gelu(hidden).astype(jnp.bfloat16)
        for c in parts:
            y = dot(hidden, w2_ref[:, c])
            at = 0
            for ref in out_refs:
                ref[:, c] = y[at : at + ref.shape[0]].astype(ref.dtype)
                at += ref.shape[0]

    outs = [jax.ShapeDtypeStruct((n, width), t) for n, t in zip(heights, types)]
    return local_kernel(
        kernel, "expert", outs, [w1, w2, *pieces], after, flops=4 * rows * width * units
    )


def lay_out(section, sections, first, second):
    rows, width = first.shape
    half = width // 2

    def kernel(section, first_ref, second_ref, out_ref, after_ref):
        decodes = jnp.full((rows, 1), section[0]) >= sections // 2
        after_ref[...] = jnp.zeros_like(after_ref)
        for at, ref in ((0, first_ref), (half, second_ref)):
            for side in (0, 1):
                block = jnp.where(decodes, ref[:, side * half : (side + 1) * half], 0.0)
                out_ref[:, side, at : at + half] = block

    outs = [
        jax.ShapeDtypeStruct((rows, 2, width), jnp.float32),
        jax.ShapeDtypeStruct((8, HD), jnp.float32),
    ]
    return local_kernel(kernel, "lay_out", outs, [section.reshape(1), first, second], scalars=1)


def blank(section, after, like):
    def kernel(section, after_any, out_any, after_ref, zero_ref, sem):
        after_ref[...] = jnp.zeros_like(after_ref)

        @pl.when(section[0] == 0)
        def _():
            zero_ref[...] = jnp.zeros_like(zero_ref)
            copy = pltpu.make_async_copy(zero_ref, out_any, sem)
            copy.start()
            copy.wait()

    return pl.pallas_call(
        kernel,
        out_shape=(
            jax.ShapeDtypeStruct(like.shape, like.dtype),
            jax.ShapeDtypeStruct((8, HD), jnp.float32),
        ),
        in_specs=[pl.BlockSpec(memory_space=pltpu.SMEM), ANYWHERE],
        out_specs=(pl.BlockSpec(memory_space=pltpu.HBM), in_vmem(1)[0]),
        scratch_shapes=[pltpu.VMEM(like.shape, like.dtype), pltpu.SemaphoreType.DMA],
        compiler_params=compiler_params(),
        name="blank",
    )(section.reshape(1), after)


def finish(section, res, back, room=None):
    tokens, width = res.shape
    one = jax.ShapeDtypeStruct((tokens, width), jnp.bfloat16)
    step = next(s for s in (640, 512, 256, 128) if width % s == 0)
    parts = [slice(at, at + step) for at in range(0, width, step)]

    def kernel(section, res_ref, back_ref, *refs):
        out_any, out_ref, sems = refs[-3:]

        def compute():
            gate, slot = back_ref[0:1, width:], back_ref[1:2, width:]
            gate = jnp.broadcast_to(gate, (CAP, tokens)).T[:, 0:1]
            slots = lax.broadcasted_iota(jnp.int32, (CAP, tokens), 0).astype(jnp.float32)
            onehot = jnp.where(slot == slots, 1.0, 0.0).T
            onehot = jnp.concatenate([onehot] * 3, axis=1).astype(jnp.bfloat16)
            copies = []
            for i, columns in enumerate(parts):
                back = back_ref[:, columns]
                high = back.astype(jnp.bfloat16).astype(jnp.float32)
                middle = (back - high).astype(jnp.bfloat16).astype(jnp.float32)
                three = jnp.concatenate([high, middle, back - high - middle], axis=0)
                moved = dot(onehot, three.astype(jnp.bfloat16))
                here = res_ref[:, columns].astype(jnp.float32)
                out_ref[:, columns] = (here + gate * moved).astype(jnp.bfloat16)
                copy = pltpu.make_async_copy(
                    out_ref.at[:, columns], out_any.at[:, columns], sems.at[i]
                )
                copy.start()
                copies.append(copy)
            for copy in copies:
                copy.wait()

        if room is None:
            compute()
        else:
            pl.when(section[0] > 0)(compute)

    aliased = [] if room is None else [pl.BlockSpec(memory_space=pltpu.HBM)]
    return pl.pallas_call(
        kernel,
        out_shape=one,
        in_specs=[pl.BlockSpec(memory_space=pltpu.SMEM), *in_vmem(2), *aliased],
        out_specs=pl.BlockSpec(memory_space=pltpu.HBM),
        scratch_shapes=[
            pltpu.VMEM(one.shape, one.dtype),
            pltpu.SemaphoreType.DMA((len(parts),)),
        ],
        input_output_aliases={} if room is None else {3: 0},
        compiler_params=compiler_params(),
        cost_estimate=pl.CostEstimate(
            flops=50 * tokens * width, bytes_accessed=5 * tokens * width, transcendentals=0
        ),
        name="finish",
    )(section.reshape(1), res, back, *([] if room is None else [room]))


def local(
    layer_in, memory, cotangent, norm_gain, attn_gain, expert_in, expert_out, slot_index, gate_prob
):
    sections = lax.axis_size("section")
    section = lax.axis_index("section")
    decoder = section >= sections // 2
    grid = Grid(lax.axis_size("expert"))
    own_rows, _, width = memory[0].shape
    half = width // 2
    heights = grid.heights(own_rows)
    narrow = any(n % 16 for n in heights)

    first = swapped(memory[0])[:, :, :half]
    stash = jnp.where(decoder, memory[0, :, :, half:], first).reshape(own_rows, width)
    pieces = grid.gather(stash)
    current, *first, second, gates = make_queries(
        layer_in[0], attn_gain, gate_prob, slot_index, [pieces[0]]
    )
    first = [swapped(q) for q in first]
    *upstream, cot_second = cut(cotangent[0], [gates])
    upstream = [swapped(c) for c in upstream]
    if narrow:
        pieces = [jnp.concatenate(pieces, axis=0)]

    mixed, weights, queries = attend(
        section, sections, first, second, pieces, upstream
    )
    cots = (upstream, cot_second)
    if narrow:
        whole = [sum(heights)], [jnp.float32]
        (whole,) = gradient(section, sections, queries, *cots, weights, pieces, *whole)
        parts, at = [], 0
        for n, t in zip(heights, grid.types()):
            parts.append(whole[at : at + n].astype(t))
            at += n
    else:
        parts = gradient(section, sections, queries, *cots, weights, pieces, heights, grid.types())
    residual, capacity = settle(
        section, sections, current, to_decoder(mixed), mixed, norm_gain, gates, [parts[0]]
    )
    residual_before = passed_along(current if sections == 2 else residual, "section", 1)
    grads = grid.scatter(parts, own_rows)
    halves = next(grads)
    sums = []

    def plane_sums(own):
        if not sums:
            sums.append(grads.send([own]))
        return [sums[0][0][0]]

    gathered = grid.gather(capacity, halves, plane_sums)
    computed = expert(
        expert_in[0], expert_out[0], gathered, grid.heights(CAP), grid.types(), [residual_before, *sums[0][1][:2]]
    )
    total_grad = grads.send([computed[0]])
    room, made = blank(section, capacity, residual)
    results = grid.scatter(computed, CAP, [total_grad], gates)
    next(results)
    results.send([made])
    total_grad, laid = lay_out(section, sections, to_decoder(total_grad), total_grad)
    returned = results.send([laid])
    returned_before = passed_along(returned, "section", 1)
    output = finish(section, residual, returned)
    arriving = finish(section, residual_before, returned_before, room)
    return (output[None], arriving[None], total_grad[None])


def solution(mesh):
    placed = (
        P("section", "expert", None),
        P("section", "expert", None, None),
        P("section", "expert", None),
        P("section", None),
        P("section", None),
        P("section", None, "expert"),
        P("section", "expert", None),
        P("section", "expert"),
        P("section", "expert"),
    )
    return jax.shard_map(
        local,
        mesh=mesh,
        in_specs=placed,
        out_specs=(
            P("section", "expert", None),
            P("section", "expert", None),
            P("section", "expert", None, None),
        ),
        check_vma=False,
    )
```

```python
import functools

import jax
import jax.numpy as jnp
from jax import lax
from jax.experimental import pallas as pl
from jax.experimental.pallas import tpu as pltpu
from jax.sharding import PartitionSpec as P

HD = 128
CAP = 8


def passed_along(block, axis, distance):
    devices = range(lax.axis_size(axis))
    route = [(i - distance, i) for i in devices if i - distance in devices]
    return lax.ppermute(block, axis, route)


def swapped(block):
    sections = lax.axis_size("section")
    return lax.ppermute(block, "section", [(i, (i + sections // 2) % sections) for i in range(sections)])


def to_decoder(block):
    apart = lax.axis_size("section") // 2
    return lax.ppermute(block, "section", [(i, i + apart) for i in range(apart)])


def partner(position, distance, size):
    return position ^ distance if size & (size - 1) == 0 else (position + distance) % size


class Grid:
    def __init__(self, size):
        a = 4 if size % 4 == 0 else 1
        c = 2 if (size // a) % 2 == 0 else 1
        self.sizes = (a, size // a // c, c)
        self.size = size

    def shift(self, block, by, back=False):
        sizes = self.sizes
        route = []
        for index in range(self.size):
            at = (index // (sizes[1] * sizes[2]), index // sizes[2] % sizes[1], index % sizes[2])
            to = [partner(p, d, n) for p, d, n in zip(at, by, sizes)]
            route.append((index, (to[0] * sizes[1] + to[1]) * sizes[2] + to[2]))
        if back:
            route = [(target, source) for source, target in route]
        return lax.ppermute(block, "expert", route)

    def offsets(self):
        _, nb, nc = self.sizes
        return [(b, c) for b in range(nb) for c in range(nc)]

    def heights(self, rows):
        na = self.sizes[0]
        half = rows * (na - na // 2)
        listed = []
        for b, c in self.offsets():
            listed += [half, na * rows - half] if b and c else [na * rows]
        return listed

    def types(self):
        listed = []
        for b, c in self.offsets():
            listed += [jnp.bfloat16] * 2 if b and c else [jnp.float32]
        return listed

    def gather(self, block, first=(), second=lambda own: ()):
        na, nb, nc = self.sizes
        rows = block.shape[0]
        own = join([block] + [self.shift(block, (s, 0, 0)) for s in range(1, na)], first)
        half = rows * (na - na // 2)
        pieces = {(0, 0): [own]}
        for b in range(1, nb):
            pieces[b, 0] = [self.shift(own, (0, b, 0))]
        for c in range(1, nc):
            pieces[0, c] = [self.shift(own, (0, 0, c))]
        for b in range(1, nb):
            for c in range(1, nc):
                upper, lower = halves_of(pieces[b, 0][0], pieces[0, c][0], half, second(own))
                pieces[b, c] = [self.shift(upper, (0, 0, c)), self.shift(lower, (0, b, 0))]
        return sum((pieces[k] for k in self.offsets()), [])

    def scatter(self, pieces, rows, after=(), extra=None):
        na, nb, nc = self.sizes
        half = rows * (na - na // 2)
        held, at = {}, 0
        for k in self.offsets():
            count = 2 if k[0] and k[1] else 1
            held[k] = pieces[at : at + count]
            at += count
        arrived = []
        for b in range(1, nb):
            more = [self.shift(held[b, c][0], (0, 0, c), back=True) for c in range(1, nc)]
            arrived.append((held[b, 0][0], more, 0, (0, b, 0)))
        for c in range(1, nc):
            more = [self.shift(held[b, c][1], (0, b, 0), back=True) for b in range(1, nb)]
            arrived.append((held[0, c][0], more, half, (0, 0, c)))
        halves = [add_half(piece, more, start, after) for piece, more, start, _ in arrived]
        arrived = [self.shift(piece, by, back=True) for piece, (*_, by) in zip(halves, arrived)]
        after = yield halves
        blocks = add_blocks(held[0, 0][0], arrived, rows, after)
        more = [self.shift(blocks[s], (s, 0, 0), back=True) for s in range(1, na)]
        after = yield blocks, more
        yield add_last(blocks[0], more, after, extra)


def compiler_params():
    return pltpu.CompilerParams(vmem_limit_bytes=20 * 2**20)


def in_vmem(count):
    return [pl.BlockSpec(memory_space=pltpu.VMEM)] * count


ANYWHERE = pl.BlockSpec(memory_space=pl.ANY)
LAST = (((1,), (1,)), ((), ()))
PLAIN = (((1,), (0,)), ((), ()))


def dot(left, right, dims=PLAIN):
    return lax.dot_general(left, right, dims, preferred_element_type=jnp.float32)


def local_kernel(kernel, name, outs, args, after=(), flops=0, scalars=0, **more):
    args = list(args)
    in_specs = [pl.BlockSpec(memory_space=pltpu.SMEM)] * scalars + in_vmem(len(args) - scalars)
    count = len(args)
    body = kernel
    if after:
        args += after
        in_specs += [ANYWHERE] * len(after)

        def body(*refs):
            kernel(*refs[:count], *refs[count + len(after) :])

    moved = sum(x.size * x.dtype.itemsize for x in args[:count]) + sum(
        x.size * x.dtype.itemsize for x in outs
    )
    return pl.pallas_call(
        body,
        out_shape=tuple(outs),
        in_specs=in_specs,
        out_specs=tuple(in_vmem(len(outs))),
        compiler_params=compiler_params(),
        cost_estimate=pl.CostEstimate(flops=flops, bytes_accessed=moved, transcendentals=0),
        name=name,
        **more,
    )(*args)


def join(blocks, after=()):
    if blocks[0].shape[0] % 8:
        return jnp.concatenate(blocks, axis=0)

    def kernel(*refs):
        rows = jnp.concatenate([r[...].astype(jnp.float32) for r in refs[:-1]], axis=0)
        refs[-1][...] = rows.astype(jnp.bfloat16)

    one = jax.ShapeDtypeStruct((len(blocks) * blocks[0].shape[0], blocks[0].shape[1]), jnp.bfloat16)
    return local_kernel(kernel, "join", [one], blocks, after)[0]


def halves_of(first, second, half, after):
    if half % 16 or not after:
        return first[:half], second[half:]

    def kernel(first_ref, second_ref, upper_ref, lower_ref):
        upper_ref[...] = first_ref[:half]
        lower_ref[...] = second_ref[half:]

    width = first.shape[1]
    outs = [
        jax.ShapeDtypeStruct((half, width), first.dtype),
        jax.ShapeDtypeStruct((second.shape[0] - half, width), first.dtype),
    ]
    return local_kernel(kernel, "halves", outs, [first, second], after)


def add_half(piece, more, start, after):
    rows = more[0].shape[0]

    def add(whole, terms):
        there = whole[start : start + rows]
        for term in terms:
            there = there + term.astype(jnp.float32)
        parts = [whole[:start], there, whole[start + rows :]]
        return jnp.concatenate([p for p in parts if p.shape[0]], axis=0).astype(jnp.bfloat16)

    if rows % 16:
        return add(piece, more)

    def kernel(piece_ref, *refs):
        refs[-1][...] = add(piece_ref[...], [r[...] for r in refs[:-1]])

    one = jax.ShapeDtypeStruct(piece.shape, jnp.bfloat16)
    return local_kernel(kernel, "add_half", [one], [piece, *more], after)[0]


def add_blocks(piece, more, rows, after):
    count = piece.shape[0] // rows
    types = [jnp.float32] + [jnp.bfloat16] * (count - 1)

    def add(whole, terms):
        for term in terms:
            whole = whole + term.astype(jnp.float32)
        return [whole[s * rows : (s + 1) * rows].astype(t) for s, t in enumerate(types)]

    if rows % 8:
        return add(piece, more)

    def kernel(*refs):
        terms = [r[...] for r in refs[: 1 + len(more)]]
        for ref, block in zip(refs[1 + len(more) :], add(terms[0], terms[1:])):
            ref[...] = block

    outs = [jax.ShapeDtypeStruct((rows, piece.shape[1]), t) for t in types]
    return local_kernel(kernel, "add_blocks", outs, [piece, *more], after)


def add_last(block, more, after, extra=None):
    rows, width = block.shape
    wide = 0 if extra is None else extra.shape[1]

    def kernel(block_ref, *refs):
        total = block_ref[...]
        for ref in refs[: len(more)]:
            total = total + ref[...].astype(jnp.float32)
        refs[-1][:, :width] = total
        if wide:
            refs[-1][:, width:] = jnp.zeros((rows, wide), jnp.float32)
            refs[-1][: extra.shape[0], width:] = refs[len(more)][...]

    one = jax.ShapeDtypeStruct((rows, width + wide), jnp.float32)
    args = [block, *more] + ([extra] if wide else [])
    return local_kernel(kernel, "add_last", [one], args, after)[0]


def head_loop(heads, some_heads):
    few = next(u for u in (20, 10, 5, 4, 2, 1) if heads % u == 0)

    def step(g, carry):
        numbers = [g * few + u for u in range(few)]
        some_heads(numbers, [pl.ds(pl.multiple_of(h * HD, HD), HD) for h in numbers])
        return carry

    lax.fori_loop(0, heads // few, step, 0)


def beside(columns, width):
    return [pl.ds(pl.multiple_of(width + c.start, HD), HD) for c in columns]


def stacked(refs, columns):
    return [jnp.concatenate([r[:, c] for r in refs], axis=0) for c in columns]


def make_queries(x, gain, gate, slots, after):
    tokens, width = x.shape
    half = width // 2

    quarter = half // 2

    def kernel(x_ref, gain_ref, gate_ref, slot_ref, copy_ref, *refs):
        *q_refs, gates_ref = refs
        copy_ref[...] = x_ref[...]
        gates_ref[0:1] = gate_ref[...]
        gates_ref[1:2] = slot_ref[...].astype(jnp.float32)
        x = x_ref[...].astype(jnp.float32)
        inverse = lax.rsqrt(jnp.mean(x * x, axis=-1, keepdims=True) + 1e-06)
        for at, ref in zip((0, quarter, half), q_refs):
            columns = slice(at, at + ref.shape[1])
            x = x_ref[:, columns].astype(jnp.float32)
            ref[...] = (x * inverse * gain_ref[:, columns]).astype(jnp.bfloat16)

    part = jax.ShapeDtypeStruct((tokens, quarter), jnp.bfloat16)
    one = jax.ShapeDtypeStruct((tokens, half), jnp.bfloat16)
    same = jax.ShapeDtypeStruct((tokens, width), x.dtype)
    pair = jax.ShapeDtypeStruct((2, tokens), jnp.float32)
    return local_kernel(
        kernel,
        "queries",
        [same, part, part, one, pair],
        [x, gain, gate, slots],
        after,
    )


def cut(x, after):
    tokens, width = x.shape
    widths = [width // 4, width // 4, width // 2]

    def kernel(x_ref, *refs):
        at = 0
        for ref in refs:
            ref[...] = x_ref[:, at : at + ref.shape[1]]
            at += ref.shape[1]

    outs = [jax.ShapeDtypeStruct((tokens, n), x.dtype) for n in widths]
    return local_kernel(kernel, "cut", outs, [x], after)


def choose(section, sections, first_refs, second_ref, out_ref):
    @pl.when(section[0] >= sections // 2)
    def _():
        out_ref[...] = second_ref[...]

    @pl.when(section[0] < sections // 2)
    def _():
        at = 0
        for ref in first_refs:
            out_ref[:, at : at + ref.shape[1]] = ref[...]
            at += ref.shape[1]


def attend(section, sections, first, second, pieces, after):
    tokens, width = second.shape
    heads = width // HD
    rows = sum(p.shape[0] for p in pieces)
    count = len(pieces)

    def kernel(section, *refs):
        *first_refs, second_ref = refs[: len(first) + 1]
        refs = refs[len(first) + 1 :]
        kv_refs, (mixed_ref, p_ref, q_ref) = refs[:count], refs[count:]
        choose(section, sections, first_refs, second_ref, q_ref)

        def some_heads(numbers, columns):
            keys = stacked(kv_refs, columns)
            values = stacked(kv_refs, beside(columns, width))
            scores = [dot(k, q_ref[:, c], LAST) * HD**-0.5 for k, c in zip(keys, columns)]
            e = [jnp.exp(s - jnp.max(s, axis=0, keepdims=True)) for s in scores]
            w = [x * (1.0 / jnp.sum(x, axis=0, keepdims=True)) for x in e]
            mixed = [dot(x.astype(jnp.bfloat16).T, v) for x, v in zip(w, values)]
            for h, c, x, m in zip(numbers, columns, w, mixed):
                p_ref[h] = x
                mixed_ref[:, c] = m.astype(jnp.bfloat16)

        head_loop(heads, some_heads)

    outs = [
        jax.ShapeDtypeStruct((tokens, width), jnp.bfloat16),
        jax.ShapeDtypeStruct((heads, rows, tokens), jnp.float32),
        jax.ShapeDtypeStruct((tokens, width), jnp.bfloat16),
    ]
    args = [section.reshape(1), *first, second, *pieces]
    return local_kernel(
        kernel, "attend", outs, args, after, flops=4 * tokens * rows * width, scalars=1
    )


def gradient(section, sections, q, first, second, p, pieces, heights, types):
    tokens, width = q.shape
    heads, rows, _ = p.shape
    count = len(pieces)

    def kernel(section, q_ref, *refs):
        *first_refs, second_ref, p_ref = refs[: len(first) + 2]
        refs = refs[len(first) + 2 :]
        kv_refs, out_refs, cot_ref = refs[:count], refs[count:-1], refs[-1]
        choose(section, sections, first_refs, second_ref, cot_ref)

        def some_heads(numbers, columns):
            values = stacked(kv_refs, beside(columns, width))
            q = [q_ref[:, c] for c in columns]
            cot = [cot_ref[:, c] for c in columns]
            w = [p_ref[h] for h in numbers]
            dp = [dot(v, c, LAST) for v, c in zip(values, cot)]
            ds = [
                x * (d - jnp.sum(d * x, axis=0, keepdims=True)) * HD**-0.5 for d, x in zip(dp, w)
            ]
            upper = [x.astype(jnp.bfloat16) for x in ds]
            lower = [(x - u.astype(jnp.float32)).astype(jnp.bfloat16) for x, u in zip(ds, upper)]
            dk = [
                dot(jnp.concatenate([u, v], axis=1), jnp.concatenate([x, x], axis=0))
                for u, v, x in zip(upper, lower, q)
            ]
            dv = [dot(x.astype(jnp.bfloat16), c) for x, c in zip(w, cot)]
            for there, grads in ((columns, dk), (beside(columns, width), dv)):
                for c, g in zip(there, grads):
                    at = 0
                    for ref in out_refs:
                        ref[:, c] = g[at : at + ref.shape[0]].astype(ref.dtype)
                        at += ref.shape[0]

        head_loop(heads, some_heads)

    outs = [jax.ShapeDtypeStruct((n, 2 * width), t) for n, t in zip(heights, types)]
    return local_kernel(
        kernel,
        "gradient",
        outs,
        [section.reshape(1), q, *first, second, p, *pieces],
        flops=10 * tokens * rows * width,
        scalars=1,
        scratch_shapes=[pltpu.VMEM((tokens, width), jnp.bfloat16)],
    )


def settle(section, sections, x, first, second, norm_gain, gates, after):
    tokens, width = first.shape[0], x.shape[1]
    half = width // 2

    def kernel(section, x_ref, first_ref, second_ref, norm_ref, gate_ref, res_ref, cap_ref):
        slots = lax.broadcasted_iota(jnp.int32, (CAP, tokens), 0).astype(jnp.float32)
        onehot = jnp.where(gate_ref[1:2] == slots, 1.0, 0.0).astype(jnp.bfloat16)
        attends = jnp.full((tokens, 1), section[0], jnp.int32) >= sections // 2
        chosen = []
        for at, ref in ((0, first_ref), (half, second_ref)):
            mixed = jnp.where(attends, ref[...].astype(jnp.float32), 0.0)
            res = (x_ref[:tokens, at : at + half].astype(jnp.float32) + mixed).astype(jnp.bfloat16)
            res_ref[:, at : at + half] = res
            chosen.append(dot(onehot, res))
        squares = sum(jnp.sum(c * c, axis=-1, keepdims=True) for c in chosen)
        inverse = lax.rsqrt(squares / width + 1e-06)
        for at, c in zip((0, half), chosen):
            rows = (c * inverse * norm_ref[:, at : at + half]).astype(jnp.bfloat16)
            cap_ref[:, at : at + half] = rows

    outs = [
        jax.ShapeDtypeStruct((tokens, width), jnp.bfloat16),
        jax.ShapeDtypeStruct((CAP, width), jnp.bfloat16),
    ]
    return local_kernel(
        kernel, "settle", outs, [section.reshape(1), x, first, second, norm_gain, gates], after,
        scalars=1,
    )


def expert(w1, w2, pieces, heights, types, after):
    width, units = w1.shape
    rows = sum(heights)
    count = len(pieces)
    steps = next(s for s in (4, 2, 1) if width % (s * 128) == 0)
    step = width // steps

    def kernel(w1_ref, w2_ref, *refs):
        in_refs, out_refs = refs[:count], refs[count:]
        parts = [slice(i * step, (i + 1) * step) for i in range(steps)]
        hidden = jnp.zeros((rows, units), jnp.float32)
        for c in parts:
            hidden = hidden + dot(jnp.concatenate([r[:, c] for r in in_refs], axis=0), w1_ref[c, :])
        hidden = jax.nn.gelu(hidden).astype(jnp.bfloat16)
        for c in parts:
            y = dot(hidden, w2_ref[:, c])
            at = 0
            for ref in out_refs:
                ref[:, c] = y[at : at + ref.shape[0]].astype(ref.dtype)
                at += ref.shape[0]

    outs = [jax.ShapeDtypeStruct((n, width), t) for n, t in zip(heights, types)]
    return local_kernel(
        kernel, "expert", outs, [w1, w2, *pieces], after, flops=4 * rows * width * units
    )


def lay_out(section, sections, first, second):
    rows, width = first.shape
    half = width // 2

    def kernel(section, first_ref, second_ref, out_ref, after_ref):
        decodes = jnp.full((rows, 1), section[0]) >= sections // 2
        after_ref[...] = jnp.zeros_like(after_ref)
        for at, ref in ((0, first_ref), (half, second_ref)):
            for side in (0, 1):
                block = jnp.where(decodes, ref[:, side * half : (side + 1) * half], 0.0)
                out_ref[:, side, at : at + half] = block

    outs = [
        jax.ShapeDtypeStruct((rows, 2, width), jnp.float32),
        jax.ShapeDtypeStruct((8, HD), jnp.float32),
    ]
    return local_kernel(kernel, "lay_out", outs, [section.reshape(1), first, second], scalars=1)


def blank(section, after, like):
    def kernel(section, after_any, out_any, after_ref, zero_ref, sem):
        after_ref[...] = jnp.zeros_like(after_ref)

        @pl.when(section[0] == 0)
        def _():
            zero_ref[...] = jnp.zeros_like(zero_ref)
            copy = pltpu.make_async_copy(zero_ref, out_any, sem)
            copy.start()
            copy.wait()

    return pl.pallas_call(
        kernel,
        out_shape=(
            jax.ShapeDtypeStruct(like.shape, like.dtype),
            jax.ShapeDtypeStruct((8, HD), jnp.float32),
        ),
        in_specs=[pl.BlockSpec(memory_space=pltpu.SMEM), ANYWHERE],
        out_specs=(pl.BlockSpec(memory_space=pltpu.HBM), in_vmem(1)[0]),
        scratch_shapes=[pltpu.VMEM(like.shape, like.dtype), pltpu.SemaphoreType.DMA],
        compiler_params=compiler_params(),
        name="blank",
    )(section.reshape(1), after)


def finish(section, res, back, room=None):
    tokens, width = res.shape
    one = jax.ShapeDtypeStruct((tokens, width), jnp.bfloat16)
    step = next(s for s in (640, 512, 256, 128) if width % s == 0)
    parts = [slice(at, at + step) for at in range(0, width, step)]

    def kernel(section, res_ref, back_ref, *refs):
        out_any, out_ref, sems = refs[-3:]

        def compute():
            gate, slot = back_ref[0:1, width:], back_ref[1:2, width:]
            gate = jnp.broadcast_to(gate, (CAP, tokens)).T[:, 0:1]
            slots = lax.broadcasted_iota(jnp.int32, (CAP, tokens), 0).astype(jnp.float32)
            onehot = jnp.where(slot == slots, 1.0, 0.0).T
            onehot = jnp.concatenate([onehot] * 3, axis=1).astype(jnp.bfloat16)
            copies = []
            for i, columns in enumerate(parts):
                back = back_ref[:, columns]
                high = back.astype(jnp.bfloat16).astype(jnp.float32)
                middle = (back - high).astype(jnp.bfloat16).astype(jnp.float32)
                three = jnp.concatenate([high, middle, back - high - middle], axis=0)
                moved = dot(onehot, three.astype(jnp.bfloat16))
                here = res_ref[:, columns].astype(jnp.float32)
                out_ref[:, columns] = (here + gate * moved).astype(jnp.bfloat16)
                copy = pltpu.make_async_copy(
                    out_ref.at[:, columns], out_any.at[:, columns], sems.at[i]
                )
                copy.start()
                copies.append(copy)
            for copy in copies:
                copy.wait()

        if room is None:
            compute()
        else:
            pl.when(section[0] > 0)(compute)

    aliased = [] if room is None else [pl.BlockSpec(memory_space=pltpu.HBM)]
    return pl.pallas_call(
        kernel,
        out_shape=one,
        in_specs=[pl.BlockSpec(memory_space=pltpu.SMEM), *in_vmem(2), *aliased],
        out_specs=pl.BlockSpec(memory_space=pltpu.HBM),
        scratch_shapes=[
            pltpu.VMEM(one.shape, one.dtype),
            pltpu.SemaphoreType.DMA((len(parts),)),
        ],
        input_output_aliases={} if room is None else {3: 0},
        compiler_params=compiler_params(),
        cost_estimate=pl.CostEstimate(
            flops=50 * tokens * width, bytes_accessed=5 * tokens * width, transcendentals=0
        ),
        name="finish",
    )(section.reshape(1), res, back, *([] if room is None else [room]))


def local(
    layer_in, memory, cotangent, norm_gain, attn_gain, expert_in, expert_out, slot_index, gate_prob
):
    sections = lax.axis_size("section")
    section = lax.axis_index("section")
    decoder = section >= sections // 2
    grid = Grid(lax.axis_size("expert"))
    own_rows, _, width = memory[0].shape
    half = width // 2
    heights = grid.heights(own_rows)
    narrow = any(n % 16 for n in heights)

    first = swapped(memory[0, :, :, :half].reshape(own_rows, width))
    second = memory[0, :, :, half:].reshape(own_rows, width)
    pieces = grid.gather(jnp.where(decoder, second, first))
    current, *first, second, gates = make_queries(
        layer_in[0], attn_gain, gate_prob, slot_index, [pieces[0]]
    )
    first = [swapped(q) for q in first]
    *upstream, cot_second = cut(cotangent[0], [gates])
    upstream = [swapped(c) for c in upstream]
    if narrow:
        pieces = [jnp.concatenate(pieces, axis=0)]

    mixed, weights, queries = attend(
        section, sections, first, second, pieces, upstream
    )
    cots = (upstream, cot_second)
    if narrow:
        whole = [sum(heights)], [jnp.float32]
        (whole,) = gradient(section, sections, queries, *cots, weights, pieces, *whole)
        parts, at = [], 0
        for n, t in zip(heights, grid.types()):
            parts.append(whole[at : at + n].astype(t))
            at += n
    else:
        parts = gradient(section, sections, queries, *cots, weights, pieces, heights, grid.types())
    residual, capacity = settle(
        section, sections, current, to_decoder(mixed), mixed, norm_gain, gates, [parts[0]]
    )
    residual_before = passed_along(current if sections == 2 else residual, "section", 1)
    grads = grid.scatter(parts, own_rows)
    halves = next(grads)
    sums = []

    def plane_sums(own):
        if not sums:
            sums.append(grads.send([own]))
        return [sums[0][0][0]]

    gathered = grid.gather(capacity, halves, plane_sums)
    computed = expert(
        expert_in[0], expert_out[0], gathered, grid.heights(CAP), grid.types(), [residual_before, *sums[0][1][:2]]
    )
    total_grad = grads.send([computed[0]])
    room, made = blank(section, capacity, residual)
    results = grid.scatter(computed, CAP, [total_grad], gates)
    next(results)
    results.send([made])
    total_grad, laid = lay_out(section, sections, to_decoder(total_grad), total_grad)
    returned = results.send([laid])
    returned_before = passed_along(returned, "section", 1)
    output = finish(section, residual, returned)
    arriving = finish(section, residual_before, returned_before, room)
    return (output[None], arriving[None], total_grad[None])


def solution(mesh):
    placed = (
        P("section", "expert", None),
        P("section", "expert", None, None),
        P("section", "expert", None),
        P("section", None),
        P("section", None),
        P("section", None, "expert"),
        P("section", "expert", None),
        P("section", "expert"),
        P("section", "expert"),
    )
    return jax.shard_map(
        local,
        mesh=mesh,
        in_specs=placed,
        out_specs=(
            P("section", "expert", None),
            P("section", "expert", None),
            P("section", "expert", None, None),
        ),
        check_vma=False,
    )
```

```python
import functools

import jax
import jax.numpy as jnp
from jax import lax
from jax.experimental import pallas as pl
from jax.experimental.pallas import tpu as pltpu
from jax.sharding import PartitionSpec as P

HD = 128
CAP = 8


def passed_along(block, axis, distance):
    devices = range(lax.axis_size(axis))
    route = [(i - distance, i) for i in devices if i - distance in devices]
    return lax.ppermute(block, axis, route)


def swapped(block):
    sections = lax.axis_size("section")
    return lax.ppermute(block, "section", [(i, (i + sections // 2) % sections) for i in range(sections)])


def to_decoder(block):
    apart = lax.axis_size("section") // 2
    return lax.ppermute(block, "section", [(i, i + apart) for i in range(apart)])


def partner(position, distance, size):
    return position ^ distance if size & (size - 1) == 0 else (position + distance) % size


class Grid:
    def __init__(self, size):
        a = 4 if size % 4 == 0 else 1
        c = 2 if (size // a) % 2 == 0 else 1
        self.sizes = (a, size // a // c, c)
        self.size = size

    def shift(self, block, by, back=False):
        sizes = self.sizes
        route = []
        for index in range(self.size):
            at = (index // (sizes[1] * sizes[2]), index // sizes[2] % sizes[1], index % sizes[2])
            to = [partner(p, d, n) for p, d, n in zip(at, by, sizes)]
            route.append((index, (to[0] * sizes[1] + to[1]) * sizes[2] + to[2]))
        if back:
            route = [(target, source) for source, target in route]
        return lax.ppermute(block, "expert", route)

    def offsets(self):
        _, nb, nc = self.sizes
        return [(b, c) for b in range(nb) for c in range(nc)]

    def heights(self, rows):
        na = self.sizes[0]
        half = rows * (na - na // 2)
        listed = []
        for b, c in self.offsets():
            listed += [half, na * rows - half] if b and c else [na * rows]
        return listed

    def types(self):
        listed = []
        for b, c in self.offsets():
            listed += [jnp.bfloat16] * 2 if b and c else [jnp.float32]
        return listed

    def gather(self, block, first=(), second=lambda own: ()):
        na, nb, nc = self.sizes
        rows = block.shape[0]
        own = join([block] + [self.shift(block, (s, 0, 0)) for s in range(1, na)], first)
        half = rows * (na - na // 2)
        pieces = {(0, 0): [own]}
        for b in range(1, nb):
            pieces[b, 0] = [self.shift(own, (0, b, 0))]
        for c in range(1, nc):
            pieces[0, c] = [self.shift(own, (0, 0, c))]
        for b in range(1, nb):
            for c in range(1, nc):
                upper, lower = halves_of(pieces[b, 0][0], pieces[0, c][0], half, second(own))
                pieces[b, c] = [self.shift(upper, (0, 0, c)), self.shift(lower, (0, b, 0))]
        return sum((pieces[k] for k in self.offsets()), [])

    def scatter(self, pieces, rows, after=(), extra=None):
        na, nb, nc = self.sizes
        half = rows * (na - na // 2)
        held, at = {}, 0
        for k in self.offsets():
            count = 2 if k[0] and k[1] else 1
            held[k] = pieces[at : at + count]
            at += count
        arrived = []
        for b in range(1, nb):
            more = [self.shift(held[b, c][0], (0, 0, c), back=True) for c in range(1, nc)]
            arrived.append((held[b, 0][0], more, 0, (0, b, 0)))
        for c in range(1, nc):
            more = [self.shift(held[b, c][1], (0, b, 0), back=True) for b in range(1, nb)]
            arrived.append((held[0, c][0], more, half, (0, 0, c)))
        halves = [add_half(piece, more, start, after) for piece, more, start, _ in arrived]
        arrived = [self.shift(piece, by, back=True) for piece, (*_, by) in zip(halves, arrived)]
        after = yield halves
        blocks = add_blocks(held[0, 0][0], arrived, rows, after)
        more = [self.shift(blocks[s], (s, 0, 0), back=True) for s in range(1, na)]
        after = yield blocks, more
        yield add_last(blocks[0], more, after, extra)


def compiler_params():
    return pltpu.CompilerParams(vmem_limit_bytes=20 * 2**20)


def in_vmem(count):
    return [pl.BlockSpec(memory_space=pltpu.VMEM)] * count


ANYWHERE = pl.BlockSpec(memory_space=pl.ANY)
LAST = (((1,), (1,)), ((), ()))
PLAIN = (((1,), (0,)), ((), ()))


def dot(left, right, dims=PLAIN):
    return lax.dot_general(left, right, dims, preferred_element_type=jnp.float32)


def local_kernel(kernel, name, outs, args, after=(), flops=0, scalars=0, **more):
    args = list(args)
    in_specs = [pl.BlockSpec(memory_space=pltpu.SMEM)] * scalars + in_vmem(len(args) - scalars)
    count = len(args)
    body = kernel
    if after:
        args += after
        in_specs += [ANYWHERE] * len(after)

        def body(*refs):
            kernel(*refs[:count], *refs[count + len(after) :])

    moved = sum(x.size * x.dtype.itemsize for x in args[:count]) + sum(
        x.size * x.dtype.itemsize for x in outs
    )
    return pl.pallas_call(
        body,
        out_shape=tuple(outs),
        in_specs=in_specs,
        out_specs=tuple(in_vmem(len(outs))),
        compiler_params=compiler_params(),
        cost_estimate=pl.CostEstimate(flops=flops, bytes_accessed=moved, transcendentals=0),
        name=name,
        **more,
    )(*args)


def join(blocks, after=()):
    if blocks[0].shape[0] % 8:
        return jnp.concatenate(blocks, axis=0)

    def kernel(*refs):
        rows = jnp.concatenate([r[...].astype(jnp.float32) for r in refs[:-1]], axis=0)
        refs[-1][...] = rows.astype(jnp.bfloat16)

    one = jax.ShapeDtypeStruct((len(blocks) * blocks[0].shape[0], blocks[0].shape[1]), jnp.bfloat16)
    return local_kernel(kernel, "join", [one], blocks, after)[0]


def halves_of(first, second, half, after):
    if half % 16 or not after:
        return first[:half], second[half:]

    def kernel(first_ref, second_ref, upper_ref, lower_ref):
        upper_ref[...] = first_ref[:half]
        lower_ref[...] = second_ref[half:]

    width = first.shape[1]
    outs = [
        jax.ShapeDtypeStruct((half, width), first.dtype),
        jax.ShapeDtypeStruct((second.shape[0] - half, width), first.dtype),
    ]
    return local_kernel(kernel, "halves", outs, [first, second], after)


def add_half(piece, more, start, after):
    rows = more[0].shape[0]

    def add(whole, terms):
        there = whole[start : start + rows]
        for term in terms:
            there = there + term.astype(jnp.float32)
        parts = [whole[:start], there, whole[start + rows :]]
        return jnp.concatenate([p for p in parts if p.shape[0]], axis=0).astype(jnp.bfloat16)

    if rows % 16:
        return add(piece, more)

    def kernel(piece_ref, *refs):
        refs[-1][...] = add(piece_ref[...], [r[...] for r in refs[:-1]])

    one = jax.ShapeDtypeStruct(piece.shape, jnp.bfloat16)
    return local_kernel(kernel, "add_half", [one], [piece, *more], after)[0]


def add_blocks(piece, more, rows, after):
    count = piece.shape[0] // rows
    types = [jnp.float32] + [jnp.bfloat16] * (count - 1)

    def add(whole, terms):
        for term in terms:
            whole = whole + term.astype(jnp.float32)
        return [whole[s * rows : (s + 1) * rows].astype(t) for s, t in enumerate(types)]

    if rows % 8:
        return add(piece, more)

    def kernel(*refs):
        terms = [r[...] for r in refs[: 1 + len(more)]]
        for ref, block in zip(refs[1 + len(more) :], add(terms[0], terms[1:])):
            ref[...] = block

    outs = [jax.ShapeDtypeStruct((rows, piece.shape[1]), t) for t in types]
    return local_kernel(kernel, "add_blocks", outs, [piece, *more], after)


def add_last(block, more, after, extra=None):
    rows, width = block.shape
    wide = 0 if extra is None else extra.shape[1]

    def kernel(block_ref, *refs):
        total = block_ref[...]
        for ref in refs[: len(more)]:
            total = total + ref[...].astype(jnp.float32)
        refs[-1][:, :width] = total
        if wide:
            refs[-1][:, width:] = jnp.zeros((rows, wide), jnp.float32)
            refs[-1][: extra.shape[0], width:] = refs[len(more)][...]

    one = jax.ShapeDtypeStruct((rows, width + wide), jnp.float32)
    args = [block, *more] + ([extra] if wide else [])
    return local_kernel(kernel, "add_last", [one], args, after)[0]


def head_loop(heads, some_heads):
    few = next(u for u in (20, 10, 5, 4, 2, 1) if heads % u == 0)

    def step(g, carry):
        numbers = [g * few + u for u in range(few)]
        some_heads(numbers, [pl.ds(pl.multiple_of(h * HD, HD), HD) for h in numbers])
        return carry

    lax.fori_loop(0, heads // few, step, 0)


def beside(columns, width):
    return [pl.ds(pl.multiple_of(width + c.start, HD), HD) for c in columns]


def stacked(refs, columns):
    return [jnp.concatenate([r[:, c] for r in refs], axis=0) for c in columns]


def make_queries(x, gain, gate, slots, after):
    tokens, width = x.shape
    half = width // 2

    quarter = half // 2

    def kernel(x_ref, gain_ref, gate_ref, slot_ref, copy_ref, *refs):
        *q_refs, gates_ref = refs
        copy_ref[...] = x_ref[...]
        gates_ref[0:1] = gate_ref[...]
        gates_ref[1:2] = slot_ref[...].astype(jnp.float32)
        x = x_ref[...].astype(jnp.float32)
        inverse = lax.rsqrt(jnp.mean(x * x, axis=-1, keepdims=True) + 1e-06)
        for at, ref in zip((0, quarter, half), q_refs):
            columns = slice(at, at + ref.shape[1])
            x = x_ref[:, columns].astype(jnp.float32)
            ref[...] = (x * inverse * gain_ref[:, columns]).astype(jnp.bfloat16)

    part = jax.ShapeDtypeStruct((tokens, quarter), jnp.bfloat16)
    one = jax.ShapeDtypeStruct((tokens, half), jnp.bfloat16)
    same = jax.ShapeDtypeStruct((tokens, width), x.dtype)
    pair = jax.ShapeDtypeStruct((2, tokens), jnp.float32)
    return local_kernel(
        kernel,
        "queries",
        [same, part, part, one, pair],
        [x, gain, gate, slots],
        after,
    )


def cut(x, after):
    tokens, width = x.shape
    widths = [width // 4, width // 4, width // 2]

    def kernel(x_ref, *refs):
        at = 0
        for ref in refs:
            ref[...] = x_ref[:, at : at + ref.shape[1]]
            at += ref.shape[1]

    outs = [jax.ShapeDtypeStruct((tokens, n), x.dtype) for n in widths]
    return local_kernel(kernel, "cut", outs, [x], after)


def choose(section, sections, first_refs, second_ref, out_ref):
    @pl.when(section[0] >= sections // 2)
    def _():
        out_ref[...] = second_ref[...]

    @pl.when(section[0] < sections // 2)
    def _():
        at = 0
        for ref in first_refs:
            out_ref[:, at : at + ref.shape[1]] = ref[...]
            at += ref.shape[1]


def attend(section, sections, first, second, pieces, after):
    tokens, width = second.shape
    heads = width // HD
    rows = sum(p.shape[0] for p in pieces)
    count = len(pieces)

    def kernel(section, *refs):
        *first_refs, second_ref = refs[: len(first) + 1]
        refs = refs[len(first) + 1 :]
        kv_refs, (mixed_ref, p_ref, q_ref) = refs[:count], refs[count:]
        choose(section, sections, first_refs, second_ref, q_ref)

        def some_heads(numbers, columns):
            keys = stacked(kv_refs, columns)
            values = stacked(kv_refs, beside(columns, width))
            scores = [dot(k, q_ref[:, c], LAST) * HD**-0.5 for k, c in zip(keys, columns)]
            e = [jnp.exp(s - jnp.max(s, axis=0, keepdims=True)) for s in scores]
            w = [x * (1.0 / jnp.sum(x, axis=0, keepdims=True)) for x in e]
            mixed = [dot(x.astype(jnp.bfloat16).T, v) for x, v in zip(w, values)]
            for h, c, x, m in zip(numbers, columns, w, mixed):
                p_ref[h] = x
                mixed_ref[:, c] = m.astype(jnp.bfloat16)

        head_loop(heads, some_heads)

    outs = [
        jax.ShapeDtypeStruct((tokens, width), jnp.bfloat16),
        jax.ShapeDtypeStruct((heads, rows, tokens), jnp.float32),
        jax.ShapeDtypeStruct((tokens, width), jnp.bfloat16),
    ]
    args = [section.reshape(1), *first, second, *pieces]
    return local_kernel(
        kernel, "attend", outs, args, after, flops=4 * tokens * rows * width, scalars=1
    )


def gradient(section, sections, q, first, second, p, pieces, heights, types):
    tokens, width = q.shape
    heads, rows, _ = p.shape
    count = len(pieces)

    def kernel(section, q_ref, *refs):
        *first_refs, second_ref, p_ref = refs[: len(first) + 2]
        refs = refs[len(first) + 2 :]
        kv_refs, out_refs, cot_ref = refs[:count], refs[count:-1], refs[-1]
        choose(section, sections, first_refs, second_ref, cot_ref)

        def some_heads(numbers, columns):
            values = stacked(kv_refs, beside(columns, width))
            q = [q_ref[:, c] for c in columns]
            cot = [cot_ref[:, c] for c in columns]
            w = [p_ref[h] for h in numbers]
            dp = [dot(v, c, LAST) for v, c in zip(values, cot)]
            ds = [
                x * (d - jnp.sum(d * x, axis=0, keepdims=True)) * HD**-0.5 for d, x in zip(dp, w)
            ]
            upper = [x.astype(jnp.bfloat16) for x in ds]
            lower = [(x - u.astype(jnp.float32)).astype(jnp.bfloat16) for x, u in zip(ds, upper)]
            dk = [
                dot(jnp.concatenate([u, v], axis=1), jnp.concatenate([x, x], axis=0))
                for u, v, x in zip(upper, lower, q)
            ]
            dv = [dot(x.astype(jnp.bfloat16), c) for x, c in zip(w, cot)]
            for there, grads in ((columns, dk), (beside(columns, width), dv)):
                for c, g in zip(there, grads):
                    at = 0
                    for ref in out_refs:
                        ref[:, c] = g[at : at + ref.shape[0]].astype(ref.dtype)
                        at += ref.shape[0]

        head_loop(heads, some_heads)

    outs = [jax.ShapeDtypeStruct((n, 2 * width), t) for n, t in zip(heights, types)]
    return local_kernel(
        kernel,
        "gradient",
        outs,
        [section.reshape(1), q, *first, second, p, *pieces],
        flops=10 * tokens * rows * width,
        scalars=1,
        scratch_shapes=[pltpu.VMEM((tokens, width), jnp.bfloat16)],
    )


def settle(section, sections, x, first, second, norm_gain, gates, after):
    tokens, width = first.shape[0], x.shape[1]
    half = width // 2

    def kernel(section, x_ref, first_ref, second_ref, norm_ref, gate_ref, res_ref, cap_ref):
        slots = lax.broadcasted_iota(jnp.int32, (CAP, tokens), 0).astype(jnp.float32)
        onehot = jnp.where(gate_ref[1:2] == slots, 1.0, 0.0).astype(jnp.bfloat16)
        attends = jnp.full((tokens, 1), section[0], jnp.int32) >= sections // 2
        chosen = []
        for at, ref in ((0, first_ref), (half, second_ref)):
            mixed = jnp.where(attends, ref[...].astype(jnp.float32), 0.0)
            res = (x_ref[:tokens, at : at + half].astype(jnp.float32) + mixed).astype(jnp.bfloat16)
            res_ref[:, at : at + half] = res
            chosen.append(dot(onehot, res))
        squares = sum(jnp.sum(c * c, axis=-1, keepdims=True) for c in chosen)
        inverse = lax.rsqrt(squares / width + 1e-06)
        for at, c in zip((0, half), chosen):
            rows = (c * inverse * norm_ref[:, at : at + half]).astype(jnp.bfloat16)
            cap_ref[:, at : at + half] = rows

    outs = [
        jax.ShapeDtypeStruct((tokens, width), jnp.bfloat16),
        jax.ShapeDtypeStruct((CAP, width), jnp.bfloat16),
    ]
    return local_kernel(
        kernel, "settle", outs, [section.reshape(1), x, first, second, norm_gain, gates], after,
        scalars=1,
    )


def expert(w1, w2, pieces, heights, types, after):
    width, units = w1.shape
    rows = sum(heights)
    count = len(pieces)
    steps = next(s for s in (4, 2, 1) if width % (s * 128) == 0)
    step = width // steps

    def kernel(w1_ref, w2_ref, *refs):
        in_refs, out_refs = refs[:count], refs[count:]
        parts = [slice(i * step, (i + 1) * step) for i in range(steps)]
        hidden = jnp.zeros((rows, units), jnp.float32)
        for c in parts:
            hidden = hidden + dot(jnp.concatenate([r[:, c] for r in in_refs], axis=0), w1_ref[c, :])
        hidden = jax.nn.gelu(hidden).astype(jnp.bfloat16)
        for c in parts:
            y = dot(hidden, w2_ref[:, c])
            at = 0
            for ref in out_refs:
                ref[:, c] = y[at : at + ref.shape[0]].astype(ref.dtype)
                at += ref.shape[0]

    outs = [jax.ShapeDtypeStruct((n, width), t) for n, t in zip(heights, types)]
    return local_kernel(
        kernel, "expert", outs, [w1, w2, *pieces], after, flops=4 * rows * width * units
    )


def lay_out(section, sections, first, second):
    rows, width = first.shape
    half = width // 2

    def kernel(section, first_ref, second_ref, out_ref, after_ref):
        decodes = jnp.full((rows, 1), section[0]) >= sections // 2
        after_ref[...] = jnp.zeros_like(after_ref)
        for at, ref in ((0, first_ref), (half, second_ref)):
            for side in (0, 1):
                block = jnp.where(decodes, ref[:, side * half : (side + 1) * half], 0.0)
                out_ref[:, side, at : at + half] = block

    outs = [
        jax.ShapeDtypeStruct((rows, 2, width), jnp.float32),
        jax.ShapeDtypeStruct((8, HD), jnp.float32),
    ]
    return local_kernel(kernel, "lay_out", outs, [section.reshape(1), first, second], scalars=1)


def blank(section, after, like):
    def kernel(section, after_any, out_any, after_ref, zero_ref, sem):
        after_ref[...] = jnp.zeros_like(after_ref)

        @pl.when(section[0] == 0)
        def _():
            zero_ref[...] = jnp.zeros_like(zero_ref)
            copy = pltpu.make_async_copy(zero_ref, out_any, sem)
            copy.start()
            copy.wait()

    return pl.pallas_call(
        kernel,
        out_shape=(
            jax.ShapeDtypeStruct(like.shape, like.dtype),
            jax.ShapeDtypeStruct((8, HD), jnp.float32),
        ),
        in_specs=[pl.BlockSpec(memory_space=pltpu.SMEM), ANYWHERE],
        out_specs=(pl.BlockSpec(memory_space=pltpu.HBM), in_vmem(1)[0]),
        scratch_shapes=[pltpu.VMEM(like.shape, like.dtype), pltpu.SemaphoreType.DMA],
        compiler_params=compiler_params(),
        name="blank",
    )(section.reshape(1), after)


def finish(section, res, back, room=None):
    tokens, width = res.shape
    one = jax.ShapeDtypeStruct((tokens, width), jnp.bfloat16)
    step = next(s for s in (640, 512, 256, 128) if width % s == 0)
    parts = [slice(at, at + step) for at in range(0, width, step)]

    def kernel(section, res_ref, back_ref, *refs):
        out_any, out_ref, sems = refs[-3:]

        def compute():
            gate, slot = back_ref[0:1, width:], back_ref[1:2, width:]
            gate = jnp.broadcast_to(gate, (CAP, tokens)).T[:, 0:1]
            slots = lax.broadcasted_iota(jnp.int32, (CAP, tokens), 0).astype(jnp.float32)
            onehot = jnp.where(slot == slots, 1.0, 0.0).T
            onehot = jnp.concatenate([onehot] * 3, axis=1).astype(jnp.bfloat16)
            copies = []
            for i, columns in enumerate(parts):
                back = back_ref[:, columns]
                high = back.astype(jnp.bfloat16).astype(jnp.float32)
                middle = (back - high).astype(jnp.bfloat16).astype(jnp.float32)
                three = jnp.concatenate([high, middle, back - high - middle], axis=0)
                moved = dot(onehot, three.astype(jnp.bfloat16))
                here = res_ref[:, columns].astype(jnp.float32)
                out_ref[:, columns] = (here + gate * moved).astype(jnp.bfloat16)
                copy = pltpu.make_async_copy(
                    out_ref.at[:, columns], out_any.at[:, columns], sems.at[i]
                )
                copy.start()
                copies.append(copy)
            for copy in copies:
                copy.wait()

        if room is None:
            compute()
        else:
            pl.when(section[0] > 0)(compute)

    aliased = [] if room is None else [pl.BlockSpec(memory_space=pltpu.HBM)]
    return pl.pallas_call(
        kernel,
        out_shape=one,
        in_specs=[pl.BlockSpec(memory_space=pltpu.SMEM), *in_vmem(2), *aliased],
        out_specs=pl.BlockSpec(memory_space=pltpu.HBM),
        scratch_shapes=[
            pltpu.VMEM(one.shape, one.dtype),
            pltpu.SemaphoreType.DMA((len(parts),)),
        ],
        input_output_aliases={} if room is None else {3: 0},
        compiler_params=compiler_params(),
        cost_estimate=pl.CostEstimate(
            flops=50 * tokens * width, bytes_accessed=5 * tokens * width, transcendentals=0
        ),
        name="finish",
    )(section.reshape(1), res, back, *([] if room is None else [room]))


def local(
    layer_in, memory, cotangent, norm_gain, attn_gain, expert_in, expert_out, slot_index, gate_prob
):
    sections = lax.axis_size("section")
    section = lax.axis_index("section")
    decoder = section >= sections // 2
    grid = Grid(lax.axis_size("expert"))
    own_rows, _, width = memory[0].shape
    half = width // 2
    heights = grid.heights(own_rows)
    narrow = any(n % 16 for n in heights)

    first = swapped(memory[0, :, :, :half].reshape(own_rows, width))
    second = memory[0, :, :, half:].reshape(own_rows, width)
    pieces = grid.gather(jnp.where(decoder, second, first))
    current, *first, second, gates = make_queries(
        layer_in[0], attn_gain, gate_prob, slot_index, [pieces[0]]
    )
    first = [swapped(q) for q in first]
    *upstream, cot_second = cut(cotangent[0], [gates])
    upstream = [swapped(c) for c in upstream]
    if narrow:
        pieces = [jnp.concatenate(pieces, axis=0)]

    mixed, weights, queries = attend(
        section, sections, first, second, pieces, upstream
    )
    cots = (upstream, cot_second)
    if narrow:
        whole = [sum(heights)], [jnp.float32]
        (whole,) = gradient(section, sections, queries, *cots, weights, pieces, *whole)
        parts, at = [], 0
        for n, t in zip(heights, grid.types()):
            parts.append(whole[at : at + n].astype(t))
            at += n
    else:
        parts = gradient(section, sections, queries, *cots, weights, pieces, heights, grid.types())
    residual, capacity = settle(
        section, sections, current, to_decoder(mixed), mixed, norm_gain, gates, [parts[0]]
    )
    residual_before = passed_along(current if sections == 2 else residual, "section", 1)
    grads = grid.scatter(parts, own_rows)
    halves = next(grads)
    sums = []

    def plane_sums(own):
        if not sums:
            sums.append(grads.send([own]))
        return [sums[0][0][0]]

    gathered = grid.gather(capacity, halves, plane_sums)
    total_grad = grads.send([])
    computed = expert(
        expert_in[0], expert_out[0], gathered, grid.heights(CAP), grid.types(),
        [residual_before, total_grad],
    )
    room, made = blank(section, capacity, residual)
    results = grid.scatter(computed, CAP, [], gates)
    next(results)
    results.send([made])
    total_grad, laid = lay_out(section, sections, to_decoder(total_grad), total_grad)
    returned = results.send([laid])
    returned_before = passed_along(returned, "section", 1)
    output = finish(section, residual, returned)
    arriving = finish(section, residual_before, returned_before, room)
    return (output[None], arriving[None], total_grad[None])


def solution(mesh):
    placed = (
        P("section", "expert", None),
        P("section", "expert", None, None),
        P("section", "expert", None),
        P("section", None),
        P("section", None),
        P("section", None, "expert"),
        P("section", "expert", None),
        P("section", "expert"),
        P("section", "expert"),
    )
    return jax.shard_map(
        local,
        mesh=mesh,
        in_specs=placed,
        out_specs=(
            P("section", "expert", None),
            P("section", "expert", None),
            P("section", "expert", None, None),
        ),
        check_vma=False,
    )
```

```python
import functools

import jax
import jax.numpy as jnp
from jax import lax
from jax.experimental import pallas as pl
from jax.experimental.pallas import tpu as pltpu
from jax.sharding import PartitionSpec as P

HD = 128
CAP = 8


def passed_along(block, axis, distance):
    devices = range(lax.axis_size(axis))
    route = [(i - distance, i) for i in devices if i - distance in devices]
    return lax.ppermute(block, axis, route)


def swapped(block):
    sections = lax.axis_size("section")
    return lax.ppermute(block, "section", [(i, (i + sections // 2) % sections) for i in range(sections)])


def to_decoder(block):
    apart = lax.axis_size("section") // 2
    return lax.ppermute(block, "section", [(i, i + apart) for i in range(apart)])


def partner(position, distance, size):
    return position ^ distance if size & (size - 1) == 0 else (position + distance) % size


class Grid:
    def __init__(self, size):
        a = 4 if size % 4 == 0 else 1
        c = 2 if (size // a) % 2 == 0 else 1
        self.sizes = (a, size // a // c, c)
        self.size = size

    def shift(self, block, by, back=False):
        sizes = self.sizes
        route = []
        for index in range(self.size):
            at = (index // (sizes[1] * sizes[2]), index // sizes[2] % sizes[1], index % sizes[2])
            to = [partner(p, d, n) for p, d, n in zip(at, by, sizes)]
            route.append((index, (to[0] * sizes[1] + to[1]) * sizes[2] + to[2]))
        if back:
            route = [(target, source) for source, target in route]
        return lax.ppermute(block, "expert", route)

    def offsets(self):
        _, nb, nc = self.sizes
        return [(b, c) for b in range(nb) for c in range(nc)]

    def heights(self, rows):
        na = self.sizes[0]
        half = rows * (na - na // 2)
        listed = []
        for b, c in self.offsets():
            listed += [half, na * rows - half] if b and c else [na * rows]
        return listed

    def types(self):
        listed = []
        for b, c in self.offsets():
            listed += [jnp.bfloat16] * 2 if b and c else [jnp.float32]
        return listed

    def gather(self, block, first=(), second=lambda own: ()):
        na, nb, nc = self.sizes
        rows = block.shape[0]
        own = join([block] + [self.shift(block, (s, 0, 0)) for s in range(1, na)], first)
        half = rows * (na - na // 2)
        pieces = {(0, 0): [own]}
        for b in range(1, nb):
            pieces[b, 0] = [self.shift(own, (0, b, 0))]
        for c in range(1, nc):
            pieces[0, c] = [self.shift(own, (0, 0, c))]
        for b in range(1, nb):
            for c in range(1, nc):
                upper, lower = halves_of(pieces[b, 0][0], pieces[0, c][0], half, second(own))
                pieces[b, c] = [self.shift(upper, (0, 0, c)), self.shift(lower, (0, b, 0))]
        return sum((pieces[k] for k in self.offsets()), [])

    def scatter(self, pieces, rows, after=(), extra=None):
        na, nb, nc = self.sizes
        half = rows * (na - na // 2)
        held, at = {}, 0
        for k in self.offsets():
            count = 2 if k[0] and k[1] else 1
            held[k] = pieces[at : at + count]
            at += count
        arrived = []
        for b in range(1, nb):
            more = [self.shift(held[b, c][0], (0, 0, c), back=True) for c in range(1, nc)]
            arrived.append((held[b, 0][0], more, 0, (0, b, 0)))
        for c in range(1, nc):
            more = [self.shift(held[b, c][1], (0, b, 0), back=True) for b in range(1, nb)]
            arrived.append((held[0, c][0], more, half, (0, 0, c)))
        halves = [add_half(piece, more, start, after) for piece, more, start, _ in arrived]
        arrived = [self.shift(piece, by, back=True) for piece, (*_, by) in zip(halves, arrived)]
        after = yield halves
        blocks = add_blocks(held[0, 0][0], arrived, rows, after)
        more = [self.shift(blocks[s], (s, 0, 0), back=True) for s in reversed(range(1, na))]
        after = yield blocks, more
        yield add_last(blocks[0], more, after, extra)


def compiler_params():
    return pltpu.CompilerParams(vmem_limit_bytes=20 * 2**20)


def in_vmem(count):
    return [pl.BlockSpec(memory_space=pltpu.VMEM)] * count


ANYWHERE = pl.BlockSpec(memory_space=pl.ANY)
LAST = (((1,), (1,)), ((), ()))
PLAIN = (((1,), (0,)), ((), ()))


def dot(left, right, dims=PLAIN):
    return lax.dot_general(left, right, dims, preferred_element_type=jnp.float32)


def local_kernel(kernel, name, outs, args, after=(), flops=0, scalars=0, **more):
    args = list(args)
    in_specs = [pl.BlockSpec(memory_space=pltpu.SMEM)] * scalars + in_vmem(len(args) - scalars)
    count = len(args)
    body = kernel
    if after:
        args += after
        in_specs += [ANYWHERE] * len(after)

        def body(*refs):
            kernel(*refs[:count], *refs[count + len(after) :])

    moved = sum(x.size * x.dtype.itemsize for x in args[:count]) + sum(
        x.size * x.dtype.itemsize for x in outs
    )
    return pl.pallas_call(
        body,
        out_shape=tuple(outs),
        in_specs=in_specs,
        out_specs=tuple(in_vmem(len(outs))),
        compiler_params=compiler_params(),
        cost_estimate=pl.CostEstimate(flops=flops, bytes_accessed=moved, transcendentals=0),
        name=name,
        **more,
    )(*args)


def join(blocks, after=()):
    if blocks[0].shape[0] % 8:
        return jnp.concatenate(blocks, axis=0)

    def kernel(*refs):
        rows = jnp.concatenate([r[...].astype(jnp.float32) for r in refs[:-1]], axis=0)
        refs[-1][...] = rows.astype(jnp.bfloat16)

    one = jax.ShapeDtypeStruct((len(blocks) * blocks[0].shape[0], blocks[0].shape[1]), jnp.bfloat16)
    return local_kernel(kernel, "join", [one], blocks, after)[0]


def halves_of(first, second, half, after):
    if half % 16 or not after:
        return first[:half], second[half:]

    def kernel(first_ref, second_ref, upper_ref, lower_ref):
        upper_ref[...] = first_ref[:half]
        lower_ref[...] = second_ref[half:]

    width = first.shape[1]
    outs = [
        jax.ShapeDtypeStruct((half, width), first.dtype),
        jax.ShapeDtypeStruct((second.shape[0] - half, width), first.dtype),
    ]
    return local_kernel(kernel, "halves", outs, [first, second], after)


def add_half(piece, more, start, after):
    rows = more[0].shape[0]

    def add(whole, terms):
        there = whole[start : start + rows]
        for term in terms:
            there = there + term.astype(jnp.float32)
        parts = [whole[:start], there, whole[start + rows :]]
        return jnp.concatenate([p for p in parts if p.shape[0]], axis=0).astype(jnp.bfloat16)

    if rows % 16:
        return add(piece, more)

    def kernel(piece_ref, *refs):
        refs[-1][...] = add(piece_ref[...], [r[...] for r in refs[:-1]])

    one = jax.ShapeDtypeStruct(piece.shape, jnp.bfloat16)
    return local_kernel(kernel, "add_half", [one], [piece, *more], after)[0]


def add_blocks(piece, more, rows, after):
    count = piece.shape[0] // rows
    types = [jnp.float32] + [jnp.bfloat16] * (count - 1)

    def add(whole, terms):
        for term in terms:
            whole = whole + term.astype(jnp.float32)
        return [whole[s * rows : (s + 1) * rows].astype(t) for s, t in enumerate(types)]

    if rows % 8:
        return add(piece, more)

    def kernel(*refs):
        terms = [r[...] for r in refs[: 1 + len(more)]]
        for ref, block in zip(refs[1 + len(more) :], add(terms[0], terms[1:])):
            ref[...] = block

    outs = [jax.ShapeDtypeStruct((rows, piece.shape[1]), t) for t in types]
    return local_kernel(kernel, "add_blocks", outs, [piece, *more], after)


def add_last(block, more, after, extra=None):
    rows, width = block.shape
    wide = 0 if extra is None else extra.shape[1]

    def kernel(block_ref, *refs):
        total = block_ref[...]
        for ref in refs[: len(more)]:
            total = total + ref[...].astype(jnp.float32)
        refs[-1][:, :width] = total
        if wide:
            refs[-1][:, width:] = jnp.zeros((rows, wide), jnp.float32)
            refs[-1][: extra.shape[0], width:] = refs[len(more)][...]

    one = jax.ShapeDtypeStruct((rows, width + wide), jnp.float32)
    args = [block, *more] + ([extra] if wide else [])
    return local_kernel(kernel, "add_last", [one], args, after)[0]


def head_loop(heads, some_heads):
    few = next(u for u in (20, 10, 5, 4, 2, 1) if heads % u == 0)

    def step(g, carry):
        numbers = [g * few + u for u in range(few)]
        some_heads(numbers, [pl.ds(pl.multiple_of(h * HD, HD), HD) for h in numbers])
        return carry

    lax.fori_loop(0, heads // few, step, 0)


def beside(columns, width):
    return [pl.ds(pl.multiple_of(width + c.start, HD), HD) for c in columns]


def stacked(refs, columns):
    return [jnp.concatenate([r[:, c] for r in refs], axis=0) for c in columns]


def make_queries(x, gain, gate, slots, after):
    tokens, width = x.shape
    half = width // 2

    quarter = half // 2

    def kernel(x_ref, gain_ref, gate_ref, slot_ref, copy_ref, *refs):
        *q_refs, gates_ref = refs
        copy_ref[...] = x_ref[...]
        gates_ref[0:1] = gate_ref[...]
        gates_ref[1:2] = slot_ref[...].astype(jnp.float32)
        x = x_ref[...].astype(jnp.float32)
        inverse = lax.rsqrt(jnp.mean(x * x, axis=-1, keepdims=True) + 1e-06)
        for at, ref in zip((0, quarter, half), q_refs):
            columns = slice(at, at + ref.shape[1])
            x = x_ref[:, columns].astype(jnp.float32)
            ref[...] = (x * inverse * gain_ref[:, columns]).astype(jnp.bfloat16)

    part = jax.ShapeDtypeStruct((tokens, quarter), jnp.bfloat16)
    one = jax.ShapeDtypeStruct((tokens, half), jnp.bfloat16)
    same = jax.ShapeDtypeStruct((tokens, width), x.dtype)
    pair = jax.ShapeDtypeStruct((2, tokens), jnp.float32)
    return local_kernel(
        kernel,
        "queries",
        [same, part, part, one, pair],
        [x, gain, gate, slots],
        after,
    )


def cut(x, after):
    tokens, width = x.shape
    widths = [width // 4, width // 4, width // 2]

    def kernel(x_ref, *refs):
        at = 0
        for ref in refs:
            ref[...] = x_ref[:, at : at + ref.shape[1]]
            at += ref.shape[1]

    outs = [jax.ShapeDtypeStruct((tokens, n), x.dtype) for n in widths]
    return local_kernel(kernel, "cut", outs, [x], after)


def choose(section, sections, first_refs, second_ref, out_ref):
    @pl.when(section[0] >= sections // 2)
    def _():
        out_ref[...] = second_ref[...]

    @pl.when(section[0] < sections // 2)
    def _():
        at = 0
        for ref in first_refs:
            out_ref[:, at : at + ref.shape[1]] = ref[...]
            at += ref.shape[1]


def attend(section, sections, first, second, pieces, after):
    tokens, width = second.shape
    heads = width // HD
    rows = sum(p.shape[0] for p in pieces)
    count = len(pieces)

    def kernel(section, *refs):
        *first_refs, second_ref = refs[: len(first) + 1]
        refs = refs[len(first) + 1 :]
        kv_refs, (mixed_ref, p_ref, q_ref) = refs[:count], refs[count:]
        choose(section, sections, first_refs, second_ref, q_ref)

        def some_heads(numbers, columns):
            keys = stacked(kv_refs, columns)
            values = stacked(kv_refs, beside(columns, width))
            scores = [dot(k, q_ref[:, c], LAST) * HD**-0.5 for k, c in zip(keys, columns)]
            e = [jnp.exp(s - jnp.max(s, axis=0, keepdims=True)) for s in scores]
            w = [x * (1.0 / jnp.sum(x, axis=0, keepdims=True)) for x in e]
            mixed = [dot(x.astype(jnp.bfloat16).T, v) for x, v in zip(w, values)]
            for h, c, x, m in zip(numbers, columns, w, mixed):
                p_ref[h] = x
                mixed_ref[:, c] = m.astype(jnp.bfloat16)

        head_loop(heads, some_heads)

    outs = [
        jax.ShapeDtypeStruct((tokens, width), jnp.bfloat16),
        jax.ShapeDtypeStruct((heads, rows, tokens), jnp.float32),
        jax.ShapeDtypeStruct((tokens, width), jnp.bfloat16),
    ]
    args = [section.reshape(1), *first, second, *pieces]
    return local_kernel(
        kernel, "attend", outs, args, after, flops=4 * tokens * rows * width, scalars=1
    )


def gradient(section, sections, q, first, second, p, pieces, heights, types):
    tokens, width = q.shape
    heads, rows, _ = p.shape
    count = len(pieces)

    def kernel(section, q_ref, *refs):
        *first_refs, second_ref, p_ref = refs[: len(first) + 2]
        refs = refs[len(first) + 2 :]
        kv_refs, out_refs, cot_ref = refs[:count], refs[count:-1], refs[-1]
        choose(section, sections, first_refs, second_ref, cot_ref)

        def some_heads(numbers, columns):
            values = stacked(kv_refs, beside(columns, width))
            q = [q_ref[:, c] for c in columns]
            cot = [cot_ref[:, c] for c in columns]
            w = [p_ref[h] for h in numbers]
            dp = [dot(v, c, LAST) for v, c in zip(values, cot)]
            ds = [
                x * (d - jnp.sum(d * x, axis=0, keepdims=True)) * HD**-0.5 for d, x in zip(dp, w)
            ]
            upper = [x.astype(jnp.bfloat16) for x in ds]
            lower = [(x - u.astype(jnp.float32)).astype(jnp.bfloat16) for x, u in zip(ds, upper)]
            dk = [
                dot(jnp.concatenate([u, v], axis=1), jnp.concatenate([x, x], axis=0))
                for u, v, x in zip(upper, lower, q)
            ]
            dv = [dot(x.astype(jnp.bfloat16), c) for x, c in zip(w, cot)]
            for there, grads in ((columns, dk), (beside(columns, width), dv)):
                for c, g in zip(there, grads):
                    at = 0
                    for ref in out_refs:
                        ref[:, c] = g[at : at + ref.shape[0]].astype(ref.dtype)
                        at += ref.shape[0]

        head_loop(heads, some_heads)

    outs = [jax.ShapeDtypeStruct((n, 2 * width), t) for n, t in zip(heights, types)]
    return local_kernel(
        kernel,
        "gradient",
        outs,
        [section.reshape(1), q, *first, second, p, *pieces],
        flops=10 * tokens * rows * width,
        scalars=1,
        scratch_shapes=[pltpu.VMEM((tokens, width), jnp.bfloat16)],
    )


def settle(section, sections, x, first, second, norm_gain, gates, after):
    tokens, width = first.shape[0], x.shape[1]
    half = width // 2

    def kernel(section, x_ref, first_ref, second_ref, norm_ref, gate_ref, res_ref, cap_ref):
        slots = lax.broadcasted_iota(jnp.int32, (CAP, tokens), 0).astype(jnp.float32)
        onehot = jnp.where(gate_ref[1:2] == slots, 1.0, 0.0).astype(jnp.bfloat16)
        attends = jnp.full((tokens, 1), section[0], jnp.int32) >= sections // 2
        chosen = []
        for at, ref in ((0, first_ref), (half, second_ref)):
            mixed = jnp.where(attends, ref[...].astype(jnp.float32), 0.0)
            res = (x_ref[:tokens, at : at + half].astype(jnp.float32) + mixed).astype(jnp.bfloat16)
            res_ref[:, at : at + half] = res
            chosen.append(dot(onehot, res))
        squares = sum(jnp.sum(c * c, axis=-1, keepdims=True) for c in chosen)
        inverse = lax.rsqrt(squares / width + 1e-06)
        for at, c in zip((0, half), chosen):
            rows = (c * inverse * norm_ref[:, at : at + half]).astype(jnp.bfloat16)
            cap_ref[:, at : at + half] = rows

    outs = [
        jax.ShapeDtypeStruct((tokens, width), jnp.bfloat16),
        jax.ShapeDtypeStruct((CAP, width), jnp.bfloat16),
    ]
    return local_kernel(
        kernel, "settle", outs, [section.reshape(1), x, first, second, norm_gain, gates], after,
        scalars=1,
    )


def expert(w1, w2, pieces, heights, types, after):
    width, units = w1.shape
    rows = sum(heights)
    count = len(pieces)
    steps = next(s for s in (4, 2, 1) if width % (s * 128) == 0)
    step = width // steps

    def kernel(w1_ref, w2_ref, *refs):
        in_refs, out_refs = refs[:count], refs[count:]
        parts = [slice(i * step, (i + 1) * step) for i in range(steps)]
        hidden = jnp.zeros((rows, units), jnp.float32)
        for c in parts:
            hidden = hidden + dot(jnp.concatenate([r[:, c] for r in in_refs], axis=0), w1_ref[c, :])
        hidden = jax.nn.gelu(hidden).astype(jnp.bfloat16)
        for c in parts:
            y = dot(hidden, w2_ref[:, c])
            at = 0
            for ref in out_refs:
                ref[:, c] = y[at : at + ref.shape[0]].astype(ref.dtype)
                at += ref.shape[0]

    outs = [jax.ShapeDtypeStruct((n, width), t) for n, t in zip(heights, types)]
    return local_kernel(
        kernel, "expert", outs, [w1, w2, *pieces], after, flops=4 * rows * width * units
    )


def lay_out(section, sections, first, second):
    rows, width = first.shape
    half = width // 2

    def kernel(section, first_ref, second_ref, out_ref, after_ref):
        decodes = jnp.full((rows, 1), section[0]) >= sections // 2
        after_ref[...] = jnp.zeros_like(after_ref)
        for at, ref in ((0, first_ref), (half, second_ref)):
            for side in (0, 1):
                block = jnp.where(decodes, ref[:, side * half : (side + 1) * half], 0.0)
                out_ref[:, side, at : at + half] = block

    outs = [
        jax.ShapeDtypeStruct((rows, 2, width), jnp.float32),
        jax.ShapeDtypeStruct((8, HD), jnp.float32),
    ]
    return local_kernel(kernel, "lay_out", outs, [section.reshape(1), first, second], scalars=1)


def blank(section, after, like):
    def kernel(section, after_any, out_any, after_ref, zero_ref, sem):
        after_ref[...] = jnp.zeros_like(after_ref)

        @pl.when(section[0] == 0)
        def _():
            zero_ref[...] = jnp.zeros_like(zero_ref)
            copy = pltpu.make_async_copy(zero_ref, out_any, sem)
            copy.start()
            copy.wait()

    return pl.pallas_call(
        kernel,
        out_shape=(
            jax.ShapeDtypeStruct(like.shape, like.dtype),
            jax.ShapeDtypeStruct((8, HD), jnp.float32),
        ),
        in_specs=[pl.BlockSpec(memory_space=pltpu.SMEM), ANYWHERE],
        out_specs=(pl.BlockSpec(memory_space=pltpu.HBM), in_vmem(1)[0]),
        scratch_shapes=[pltpu.VMEM(like.shape, like.dtype), pltpu.SemaphoreType.DMA],
        compiler_params=compiler_params(),
        name="blank",
    )(section.reshape(1), after)


def finish(section, res, back, room=None):
    tokens, width = res.shape
    one = jax.ShapeDtypeStruct((tokens, width), jnp.bfloat16)
    step = next(s for s in (640, 512, 256, 128) if width % s == 0)
    parts = [slice(at, at + step) for at in range(0, width, step)]

    def kernel(section, res_ref, back_ref, *refs):
        out_any, out_ref, sems = refs[-3:]

        def compute():
            gate, slot = back_ref[0:1, width:], back_ref[1:2, width:]
            gate = jnp.broadcast_to(gate, (CAP, tokens)).T[:, 0:1]
            slots = lax.broadcasted_iota(jnp.int32, (CAP, tokens), 0).astype(jnp.float32)
            onehot = jnp.where(slot == slots, 1.0, 0.0).T
            onehot = jnp.concatenate([onehot] * 3, axis=1).astype(jnp.bfloat16)
            copies = []
            for i, columns in enumerate(parts):
                back = back_ref[:, columns]
                high = back.astype(jnp.bfloat16).astype(jnp.float32)
                middle = (back - high).astype(jnp.bfloat16).astype(jnp.float32)
                three = jnp.concatenate([high, middle, back - high - middle], axis=0)
                moved = dot(onehot, three.astype(jnp.bfloat16))
                here = res_ref[:, columns].astype(jnp.float32)
                out_ref[:, columns] = (here + gate * moved).astype(jnp.bfloat16)
                copy = pltpu.make_async_copy(
                    out_ref.at[:, columns], out_any.at[:, columns], sems.at[i]
                )
                copy.start()
                copies.append(copy)
            for copy in copies:
                copy.wait()

        if room is None:
            compute()
        else:
            pl.when(section[0] > 0)(compute)

    aliased = [] if room is None else [pl.BlockSpec(memory_space=pltpu.HBM)]
    return pl.pallas_call(
        kernel,
        out_shape=one,
        in_specs=[pl.BlockSpec(memory_space=pltpu.SMEM), *in_vmem(2), *aliased],
        out_specs=pl.BlockSpec(memory_space=pltpu.HBM),
        scratch_shapes=[
            pltpu.VMEM(one.shape, one.dtype),
            pltpu.SemaphoreType.DMA((len(parts),)),
        ],
        input_output_aliases={} if room is None else {3: 0},
        compiler_params=compiler_params(),
        cost_estimate=pl.CostEstimate(
            flops=50 * tokens * width, bytes_accessed=5 * tokens * width, transcendentals=0
        ),
        name="finish",
    )(section.reshape(1), res, back, *([] if room is None else [room]))


def local(
    layer_in, memory, cotangent, norm_gain, attn_gain, expert_in, expert_out, slot_index, gate_prob
):
    sections = lax.axis_size("section")
    section = lax.axis_index("section")
    decoder = section >= sections // 2
    grid = Grid(lax.axis_size("expert"))
    own_rows, _, width = memory[0].shape
    half = width // 2
    heights = grid.heights(own_rows)
    narrow = any(n % 16 for n in heights)

    first = swapped(memory[0, :, :, :half].reshape(own_rows, width))
    second = memory[0, :, :, half:].reshape(own_rows, width)
    pieces = grid.gather(jnp.where(decoder, second, first))
    current, *first, second, gates = make_queries(
        layer_in[0], attn_gain, gate_prob, slot_index, [pieces[0]]
    )
    first = [swapped(q) for q in first]
    *upstream, cot_second = cut(cotangent[0], [gates])
    upstream = [swapped(c) for c in upstream]
    if narrow:
        pieces = [jnp.concatenate(pieces, axis=0)]

    mixed, weights, queries = attend(
        section, sections, first, second, pieces, upstream
    )
    cots = (upstream, cot_second)
    if narrow:
        whole = [sum(heights)], [jnp.float32]
        (whole,) = gradient(section, sections, queries, *cots, weights, pieces, *whole)
        parts, at = [], 0
        for n, t in zip(heights, grid.types()):
            parts.append(whole[at : at + n].astype(t))
            at += n
    else:
        parts = gradient(section, sections, queries, *cots, weights, pieces, heights, grid.types())
    residual, capacity = settle(
        section, sections, current, to_decoder(mixed), mixed, norm_gain, gates, [parts[0]]
    )
    residual_before = passed_along(current if sections == 2 else residual, "section", 1)
    grads = grid.scatter(parts, own_rows)
    halves = next(grads)
    sums = []

    def plane_sums(own):
        if not sums:
            sums.append(grads.send([own]))
        return [sums[0][0][0]]

    gathered = grid.gather(capacity, halves, plane_sums)
    computed = expert(
        expert_in[0], expert_out[0], gathered, grid.heights(CAP), grid.types(), [residual_before, *sums[0][1][:2]]
    )
    total_grad = grads.send([computed[0]])
    room, made = blank(section, capacity, residual)
    results = grid.scatter(computed, CAP, [total_grad], gates)
    next(results)
    results.send([made])
    total_grad, laid = lay_out(section, sections, to_decoder(total_grad), total_grad)
    returned = results.send([laid])
    returned_before = passed_along(returned, "section", 1)
    output = finish(section, residual, returned)
    arriving = finish(section, residual_before, returned_before, room)
    return (output[None], arriving[None], total_grad[None])


def solution(mesh):
    placed = (
        P("section", "expert", None),
        P("section", "expert", None, None),
        P("section", "expert", None),
        P("section", None),
        P("section", None),
        P("section", None, "expert"),
        P("section", "expert", None),
        P("section", "expert"),
        P("section", "expert"),
    )
    return jax.shard_map(
        local,
        mesh=mesh,
        in_specs=placed,
        out_specs=(
            P("section", "expert", None),
            P("section", "expert", None),
            P("section", "expert", None, None),
        ),
        check_vma=False,
    )
```

```python
import functools

import jax
import jax.numpy as jnp
from jax import lax
from jax.experimental import pallas as pl
from jax.experimental.pallas import tpu as pltpu
from jax.sharding import PartitionSpec as P

HD = 128
CAP = 8


def passed_along(block, axis, distance):
    devices = range(lax.axis_size(axis))
    route = [(i - distance, i) for i in devices if i - distance in devices]
    return lax.ppermute(block, axis, route)


def swapped(block):
    sections = lax.axis_size("section")
    return lax.ppermute(block, "section", [(i, (i + sections // 2) % sections) for i in range(sections)])


def to_decoder(block):
    apart = lax.axis_size("section") // 2
    return lax.ppermute(block, "section", [(i, i + apart) for i in range(apart)])


def partner(position, distance, size):
    return position ^ distance if size & (size - 1) == 0 else (position + distance) % size


class Grid:
    def __init__(self, size):
        a = 4 if size % 4 == 0 else 1
        c = 2 if (size // a) % 2 == 0 else 1
        self.sizes = (a, size // a // c, c)
        self.size = size

    def shift(self, block, by, back=False):
        sizes = self.sizes
        route = []
        for index in range(self.size):
            at = (index // (sizes[1] * sizes[2]), index // sizes[2] % sizes[1], index % sizes[2])
            to = [partner(p, d, n) for p, d, n in zip(at, by, sizes)]
            route.append((index, (to[0] * sizes[1] + to[1]) * sizes[2] + to[2]))
        if back:
            route = [(target, source) for source, target in route]
        return lax.ppermute(block, "expert", route)

    def offsets(self):
        _, nb, nc = self.sizes
        return [(b, c) for b in range(nb) for c in range(nc)]

    def heights(self, rows):
        na = self.sizes[0]
        half = rows * (na - na // 2)
        listed = []
        for b, c in self.offsets():
            listed += [half, na * rows - half] if b and c else [na * rows]
        return listed

    def types(self):
        listed = []
        for b, c in self.offsets():
            listed += [jnp.bfloat16] * 2 if b and c else [jnp.float32]
        return listed

    def gather(self, block, first=(), second=lambda own: ()):
        na, nb, nc = self.sizes
        rows = block.shape[0]
        own = join([block] + [self.shift(block, (s, 0, 0)) for s in range(1, na)], first)
        half = rows * (na - na // 2)
        pieces = {(0, 0): [own]}
        for b in range(1, nb):
            pieces[b, 0] = [self.shift(own, (0, b, 0))]
        for c in range(1, nc):
            pieces[0, c] = [self.shift(own, (0, 0, c))]
        for b in range(1, nb):
            for c in range(1, nc):
                upper, lower = halves_of(pieces[b, 0][0], pieces[0, c][0], half, second(own))
                pieces[b, c] = [self.shift(upper, (0, 0, c)), self.shift(lower, (0, b, 0))]
        return sum((pieces[k] for k in self.offsets()), [])

    def scatter(self, pieces, rows, after=(), extra=None):
        na, nb, nc = self.sizes
        half = rows * (na - na // 2)
        held, at = {}, 0
        for k in self.offsets():
            count = 2 if k[0] and k[1] else 1
            held[k] = pieces[at : at + count]
            at += count
        arrived = []
        for b in range(1, nb):
            more = [self.shift(held[b, c][0], (0, 0, c), back=True) for c in range(1, nc)]
            arrived.append((held[b, 0][0], more, 0, (0, b, 0)))
        for c in range(1, nc):
            more = [self.shift(held[b, c][1], (0, b, 0), back=True) for b in range(1, nb)]
            arrived.append((held[0, c][0], more, half, (0, 0, c)))
        halves = [add_half(piece, more, start, after) for piece, more, start, _ in arrived]
        arrived = [self.shift(piece, by, back=True) for piece, (*_, by) in zip(halves, arrived)]
        after = yield halves
        blocks = add_blocks(held[0, 0][0], arrived, rows, after)
        order = range(1, na) if extra is None else reversed(range(1, na))
        more = [self.shift(blocks[s], (s, 0, 0), back=True) for s in order]
        after = yield blocks, more
        yield add_last(blocks[0], more, after, extra)


def compiler_params():
    return pltpu.CompilerParams(vmem_limit_bytes=20 * 2**20)


def in_vmem(count):
    return [pl.BlockSpec(memory_space=pltpu.VMEM)] * count


ANYWHERE = pl.BlockSpec(memory_space=pl.ANY)
LAST = (((1,), (1,)), ((), ()))
PLAIN = (((1,), (0,)), ((), ()))


def dot(left, right, dims=PLAIN):
    return lax.dot_general(left, right, dims, preferred_element_type=jnp.float32)


def local_kernel(kernel, name, outs, args, after=(), flops=0, scalars=0, **more):
    args = list(args)
    in_specs = [pl.BlockSpec(memory_space=pltpu.SMEM)] * scalars + in_vmem(len(args) - scalars)
    count = len(args)
    body = kernel
    if after:
        args += after
        in_specs += [ANYWHERE] * len(after)

        def body(*refs):
            kernel(*refs[:count], *refs[count + len(after) :])

    moved = sum(x.size * x.dtype.itemsize for x in args[:count]) + sum(
        x.size * x.dtype.itemsize for x in outs
    )
    return pl.pallas_call(
        body,
        out_shape=tuple(outs),
        in_specs=in_specs,
        out_specs=tuple(in_vmem(len(outs))),
        compiler_params=compiler_params(),
        cost_estimate=pl.CostEstimate(flops=flops, bytes_accessed=moved, transcendentals=0),
        name=name,
        **more,
    )(*args)


def join(blocks, after=()):
    if blocks[0].shape[0] % 8:
        return jnp.concatenate(blocks, axis=0)

    def kernel(*refs):
        rows = jnp.concatenate([r[...].astype(jnp.float32) for r in refs[:-1]], axis=0)
        refs[-1][...] = rows.astype(jnp.bfloat16)

    one = jax.ShapeDtypeStruct((len(blocks) * blocks[0].shape[0], blocks[0].shape[1]), jnp.bfloat16)
    return local_kernel(kernel, "join", [one], blocks, after)[0]


def halves_of(first, second, half, after):
    if half % 16 or not after:
        return first[:half], second[half:]

    def kernel(first_ref, second_ref, upper_ref, lower_ref):
        upper_ref[...] = first_ref[:half]
        lower_ref[...] = second_ref[half:]

    width = first.shape[1]
    outs = [
        jax.ShapeDtypeStruct((half, width), first.dtype),
        jax.ShapeDtypeStruct((second.shape[0] - half, width), first.dtype),
    ]
    return local_kernel(kernel, "halves", outs, [first, second], after)


def add_half(piece, more, start, after):
    rows = more[0].shape[0]

    def add(whole, terms):
        there = whole[start : start + rows]
        for term in terms:
            there = there + term.astype(jnp.float32)
        parts = [whole[:start], there, whole[start + rows :]]
        return jnp.concatenate([p for p in parts if p.shape[0]], axis=0).astype(jnp.bfloat16)

    if rows % 16:
        return add(piece, more)

    def kernel(piece_ref, *refs):
        refs[-1][...] = add(piece_ref[...], [r[...] for r in refs[:-1]])

    one = jax.ShapeDtypeStruct(piece.shape, jnp.bfloat16)
    return local_kernel(kernel, "add_half", [one], [piece, *more], after)[0]


def add_blocks(piece, more, rows, after):
    count = piece.shape[0] // rows
    types = [jnp.float32] + [jnp.bfloat16] * (count - 1)

    def add(whole, terms):
        for term in terms:
            whole = whole + term.astype(jnp.float32)
        return [whole[s * rows : (s + 1) * rows].astype(t) for s, t in enumerate(types)]

    if rows % 8:
        return add(piece, more)

    def kernel(*refs):
        terms = [r[...] for r in refs[: 1 + len(more)]]
        for ref, block in zip(refs[1 + len(more) :], add(terms[0], terms[1:])):
            ref[...] = block

    outs = [jax.ShapeDtypeStruct((rows, piece.shape[1]), t) for t in types]
    return local_kernel(kernel, "add_blocks", outs, [piece, *more], after)


def add_last(block, more, after, extra=None):
    rows, width = block.shape
    wide = 0 if extra is None else extra.shape[1]

    def kernel(block_ref, *refs):
        total = block_ref[...]
        for ref in refs[: len(more)]:
            total = total + ref[...].astype(jnp.float32)
        refs[-1][:, :width] = total
        if wide:
            refs[-1][:, width:] = jnp.zeros((rows, wide), jnp.float32)
            refs[-1][: extra.shape[0], width:] = refs[len(more)][...]

    one = jax.ShapeDtypeStruct((rows, width + wide), jnp.float32)
    args = [block, *more] + ([extra] if wide else [])
    return local_kernel(kernel, "add_last", [one], args, after)[0]


def head_loop(heads, some_heads):
    few = next(u for u in (20, 10, 5, 4, 2, 1) if heads % u == 0)

    def step(g, carry):
        numbers = [g * few + u for u in range(few)]
        some_heads(numbers, [pl.ds(pl.multiple_of(h * HD, HD), HD) for h in numbers])
        return carry

    lax.fori_loop(0, heads // few, step, 0)


def beside(columns, width):
    return [pl.ds(pl.multiple_of(width + c.start, HD), HD) for c in columns]


def stacked(refs, columns):
    return [jnp.concatenate([r[:, c] for r in refs], axis=0) for c in columns]


def make_queries(x, gain, gate, slots, after):
    tokens, width = x.shape
    half = width // 2

    quarter = half // 2

    def kernel(x_ref, gain_ref, gate_ref, slot_ref, copy_ref, *refs):
        *q_refs, gates_ref = refs
        copy_ref[...] = x_ref[...]
        gates_ref[0:1] = gate_ref[...]
        gates_ref[1:2] = slot_ref[...].astype(jnp.float32)
        x = x_ref[...].astype(jnp.float32)
        inverse = lax.rsqrt(jnp.mean(x * x, axis=-1, keepdims=True) + 1e-06)
        for at, ref in zip((0, quarter, half), q_refs):
            columns = slice(at, at + ref.shape[1])
            x = x_ref[:, columns].astype(jnp.float32)
            ref[...] = (x * inverse * gain_ref[:, columns]).astype(jnp.bfloat16)

    part = jax.ShapeDtypeStruct((tokens, quarter), jnp.bfloat16)
    one = jax.ShapeDtypeStruct((tokens, half), jnp.bfloat16)
    same = jax.ShapeDtypeStruct((tokens, width), x.dtype)
    pair = jax.ShapeDtypeStruct((2, tokens), jnp.float32)
    return local_kernel(
        kernel,
        "queries",
        [same, part, part, one, pair],
        [x, gain, gate, slots],
        after,
    )


def cut(x, after):
    tokens, width = x.shape
    widths = [width // 4, width // 4, width // 2]

    def kernel(x_ref, *refs):
        at = 0
        for ref in refs:
            ref[...] = x_ref[:, at : at + ref.shape[1]]
            at += ref.shape[1]

    outs = [jax.ShapeDtypeStruct((tokens, n), x.dtype) for n in widths]
    return local_kernel(kernel, "cut", outs, [x], after)


def choose(section, sections, first_refs, second_ref, out_ref):
    @pl.when(section[0] >= sections // 2)
    def _():
        out_ref[...] = second_ref[...]

    @pl.when(section[0] < sections // 2)
    def _():
        at = 0
        for ref in first_refs:
            out_ref[:, at : at + ref.shape[1]] = ref[...]
            at += ref.shape[1]


def attend(section, sections, first, second, pieces, after):
    tokens, width = second.shape
    heads = width // HD
    rows = sum(p.shape[0] for p in pieces)
    count = len(pieces)

    def kernel(section, *refs):
        *first_refs, second_ref = refs[: len(first) + 1]
        refs = refs[len(first) + 1 :]
        kv_refs, (mixed_ref, p_ref, q_ref) = refs[:count], refs[count:]
        choose(section, sections, first_refs, second_ref, q_ref)

        def some_heads(numbers, columns):
            keys = stacked(kv_refs, columns)
            values = stacked(kv_refs, beside(columns, width))
            scores = [dot(k, q_ref[:, c], LAST) * HD**-0.5 for k, c in zip(keys, columns)]
            e = [jnp.exp(s - jnp.max(s, axis=0, keepdims=True)) for s in scores]
            w = [x * (1.0 / jnp.sum(x, axis=0, keepdims=True)) for x in e]
            mixed = [dot(x.astype(jnp.bfloat16).T, v) for x, v in zip(w, values)]
            for h, c, x, m in zip(numbers, columns, w, mixed):
                p_ref[h] = x
                mixed_ref[:, c] = m.astype(jnp.bfloat16)

        head_loop(heads, some_heads)

    outs = [
        jax.ShapeDtypeStruct((tokens, width), jnp.bfloat16),
        jax.ShapeDtypeStruct((heads, rows, tokens), jnp.float32),
        jax.ShapeDtypeStruct((tokens, width), jnp.bfloat16),
    ]
    args = [section.reshape(1), *first, second, *pieces]
    return local_kernel(
        kernel, "attend", outs, args, after, flops=4 * tokens * rows * width, scalars=1
    )


def gradient(section, sections, q, first, second, p, pieces, heights, types):
    tokens, width = q.shape
    heads, rows, _ = p.shape
    count = len(pieces)

    def kernel(section, q_ref, *refs):
        *first_refs, second_ref, p_ref = refs[: len(first) + 2]
        refs = refs[len(first) + 2 :]
        kv_refs, out_refs, cot_ref = refs[:count], refs[count:-1], refs[-1]
        choose(section, sections, first_refs, second_ref, cot_ref)

        def some_heads(numbers, columns):
            values = stacked(kv_refs, beside(columns, width))
            q = [q_ref[:, c] for c in columns]
            cot = [cot_ref[:, c] for c in columns]
            w = [p_ref[h] for h in numbers]
            dp = [dot(v, c, LAST) for v, c in zip(values, cot)]
            ds = [
                x * (d - jnp.sum(d * x, axis=0, keepdims=True)) * HD**-0.5 for d, x in zip(dp, w)
            ]
            upper = [x.astype(jnp.bfloat16) for x in ds]
            lower = [(x - u.astype(jnp.float32)).astype(jnp.bfloat16) for x, u in zip(ds, upper)]
            dk = [
                dot(jnp.concatenate([u, v], axis=1), jnp.concatenate([x, x], axis=0))
                for u, v, x in zip(upper, lower, q)
            ]
            dv = [dot(x.astype(jnp.bfloat16), c) for x, c in zip(w, cot)]
            for there, grads in ((columns, dk), (beside(columns, width), dv)):
                for c, g in zip(there, grads):
                    at = 0
                    for ref in out_refs:
                        ref[:, c] = g[at : at + ref.shape[0]].astype(ref.dtype)
                        at += ref.shape[0]

        head_loop(heads, some_heads)

    outs = [jax.ShapeDtypeStruct((n, 2 * width), t) for n, t in zip(heights, types)]
    return local_kernel(
        kernel,
        "gradient",
        outs,
        [section.reshape(1), q, *first, second, p, *pieces],
        flops=10 * tokens * rows * width,
        scalars=1,
        scratch_shapes=[pltpu.VMEM((tokens, width), jnp.bfloat16)],
    )


def settle(section, sections, x, first, second, norm_gain, gates, after):
    tokens, width = first.shape[0], x.shape[1]
    half = width // 2

    def kernel(section, x_ref, first_ref, second_ref, norm_ref, gate_ref, res_ref, cap_ref):
        slots = lax.broadcasted_iota(jnp.int32, (CAP, tokens), 0).astype(jnp.float32)
        onehot = jnp.where(gate_ref[1:2] == slots, 1.0, 0.0).astype(jnp.bfloat16)
        attends = jnp.full((tokens, 1), section[0], jnp.int32) >= sections // 2
        chosen = []
        for at, ref in ((0, first_ref), (half, second_ref)):
            mixed = jnp.where(attends, ref[...].astype(jnp.float32), 0.0)
            res = (x_ref[:tokens, at : at + half].astype(jnp.float32) + mixed).astype(jnp.bfloat16)
            res_ref[:, at : at + half] = res
            chosen.append(dot(onehot, res))
        squares = sum(jnp.sum(c * c, axis=-1, keepdims=True) for c in chosen)
        inverse = lax.rsqrt(squares / width + 1e-06)
        for at, c in zip((0, half), chosen):
            rows = (c * inverse * norm_ref[:, at : at + half]).astype(jnp.bfloat16)
            cap_ref[:, at : at + half] = rows

    outs = [
        jax.ShapeDtypeStruct((tokens, width), jnp.bfloat16),
        jax.ShapeDtypeStruct((CAP, width), jnp.bfloat16),
    ]
    return local_kernel(
        kernel, "settle", outs, [section.reshape(1), x, first, second, norm_gain, gates], after,
        scalars=1,
    )


def expert(w1, w2, pieces, heights, types, after):
    width, units = w1.shape
    rows = sum(heights)
    count = len(pieces)
    steps = next(s for s in (4, 2, 1) if width % (s * 128) == 0)
    step = width // steps

    def kernel(w1_ref, w2_ref, *refs):
        in_refs, out_refs = refs[:count], refs[count:]
        parts = [slice(i * step, (i + 1) * step) for i in range(steps)]
        hidden = jnp.zeros((rows, units), jnp.float32)
        for c in parts:
            hidden = hidden + dot(jnp.concatenate([r[:, c] for r in in_refs], axis=0), w1_ref[c, :])
        hidden = jax.nn.gelu(hidden).astype(jnp.bfloat16)
        for c in parts:
            y = dot(hidden, w2_ref[:, c])
            at = 0
            for ref in out_refs:
                ref[:, c] = y[at : at + ref.shape[0]].astype(ref.dtype)
                at += ref.shape[0]

    outs = [jax.ShapeDtypeStruct((n, width), t) for n, t in zip(heights, types)]
    return local_kernel(
        kernel, "expert", outs, [w1, w2, *pieces], after, flops=4 * rows * width * units
    )


def lay_out(section, sections, first, second):
    rows, width = first.shape
    half = width // 2

    def kernel(section, first_ref, second_ref, out_ref, after_ref):
        decodes = jnp.full((rows, 1), section[0]) >= sections // 2
        after_ref[...] = jnp.zeros_like(after_ref)
        for at, ref in ((0, first_ref), (half, second_ref)):
            for side in (0, 1):
                block = jnp.where(decodes, ref[:, side * half : (side + 1) * half], 0.0)
                out_ref[:, side, at : at + half] = block

    outs = [
        jax.ShapeDtypeStruct((rows, 2, width), jnp.float32),
        jax.ShapeDtypeStruct((8, HD), jnp.float32),
    ]
    return local_kernel(kernel, "lay_out", outs, [section.reshape(1), first, second], scalars=1)


def blank(section, after, like):
    def kernel(section, after_any, out_any, after_ref, zero_ref, sem):
        after_ref[...] = jnp.zeros_like(after_ref)

        @pl.when(section[0] == 0)
        def _():
            zero_ref[...] = jnp.zeros_like(zero_ref)
            copy = pltpu.make_async_copy(zero_ref, out_any, sem)
            copy.start()
            copy.wait()

    return pl.pallas_call(
        kernel,
        out_shape=(
            jax.ShapeDtypeStruct(like.shape, like.dtype),
            jax.ShapeDtypeStruct((8, HD), jnp.float32),
        ),
        in_specs=[pl.BlockSpec(memory_space=pltpu.SMEM), ANYWHERE],
        out_specs=(pl.BlockSpec(memory_space=pltpu.HBM), in_vmem(1)[0]),
        scratch_shapes=[pltpu.VMEM(like.shape, like.dtype), pltpu.SemaphoreType.DMA],
        compiler_params=compiler_params(),
        name="blank",
    )(section.reshape(1), after)


def finish(section, res, back, room=None):
    tokens, width = res.shape
    one = jax.ShapeDtypeStruct((tokens, width), jnp.bfloat16)
    step = next(s for s in (640, 512, 256, 128) if width % s == 0)
    parts = [slice(at, at + step) for at in range(0, width, step)]

    def kernel(section, res_ref, back_ref, *refs):
        out_any, out_ref, sems = refs[-3:]

        def compute():
            gate, slot = back_ref[0:1, width:], back_ref[1:2, width:]
            gate = jnp.broadcast_to(gate, (CAP, tokens)).T[:, 0:1]
            slots = lax.broadcasted_iota(jnp.int32, (CAP, tokens), 0).astype(jnp.float32)
            onehot = jnp.where(slot == slots, 1.0, 0.0).T
            onehot = jnp.concatenate([onehot] * 3, axis=1).astype(jnp.bfloat16)
            copies = []
            for i, columns in enumerate(parts):
                back = back_ref[:, columns]
                high = back.astype(jnp.bfloat16).astype(jnp.float32)
                middle = (back - high).astype(jnp.bfloat16).astype(jnp.float32)
                three = jnp.concatenate([high, middle, back - high - middle], axis=0)
                moved = dot(onehot, three.astype(jnp.bfloat16))
                here = res_ref[:, columns].astype(jnp.float32)
                out_ref[:, columns] = (here + gate * moved).astype(jnp.bfloat16)
                copy = pltpu.make_async_copy(
                    out_ref.at[:, columns], out_any.at[:, columns], sems.at[i]
                )
                copy.start()
                copies.append(copy)
            for copy in copies:
                copy.wait()

        if room is None:
            compute()
        else:
            pl.when(section[0] > 0)(compute)

    aliased = [] if room is None else [pl.BlockSpec(memory_space=pltpu.HBM)]
    return pl.pallas_call(
        kernel,
        out_shape=one,
        in_specs=[pl.BlockSpec(memory_space=pltpu.SMEM), *in_vmem(2), *aliased],
        out_specs=pl.BlockSpec(memory_space=pltpu.HBM),
        scratch_shapes=[
            pltpu.VMEM(one.shape, one.dtype),
            pltpu.SemaphoreType.DMA((len(parts),)),
        ],
        input_output_aliases={} if room is None else {3: 0},
        compiler_params=compiler_params(),
        cost_estimate=pl.CostEstimate(
            flops=50 * tokens * width, bytes_accessed=5 * tokens * width, transcendentals=0
        ),
        name="finish",
    )(section.reshape(1), res, back, *([] if room is None else [room]))


def local(
    layer_in, memory, cotangent, norm_gain, attn_gain, expert_in, expert_out, slot_index, gate_prob
):
    sections = lax.axis_size("section")
    section = lax.axis_index("section")
    decoder = section >= sections // 2
    grid = Grid(lax.axis_size("expert"))
    own_rows, _, width = memory[0].shape
    half = width // 2
    heights = grid.heights(own_rows)
    narrow = any(n % 16 for n in heights)

    first = swapped(memory[0, :, :, :half].reshape(own_rows, width))
    second = memory[0, :, :, half:].reshape(own_rows, width)
    pieces = grid.gather(jnp.where(decoder, second, first))
    current, *first, second, gates = make_queries(
        layer_in[0], attn_gain, gate_prob, slot_index, [pieces[0]]
    )
    first = [swapped(q) for q in first]
    *upstream, cot_second = cut(cotangent[0], [gates])
    upstream = [swapped(c) for c in upstream]
    if narrow:
        pieces = [jnp.concatenate(pieces, axis=0)]

    mixed, weights, queries = attend(
        section, sections, first, second, pieces, upstream
    )
    cots = (upstream, cot_second)
    if narrow:
        whole = [sum(heights)], [jnp.float32]
        (whole,) = gradient(section, sections, queries, *cots, weights, pieces, *whole)
        parts, at = [], 0
        for n, t in zip(heights, grid.types()):
            parts.append(whole[at : at + n].astype(t))
            at += n
    else:
        parts = gradient(section, sections, queries, *cots, weights, pieces, heights, grid.types())
    residual, capacity = settle(
        section, sections, current, to_decoder(mixed), mixed, norm_gain, gates, [parts[0]]
    )
    residual_before = passed_along(current if sections == 2 else residual, "section", 1)
    grads = grid.scatter(parts, own_rows)
    halves = next(grads)
    sums = []

    def plane_sums(own):
        if not sums:
            sums.append(grads.send([own]))
        return [sums[0][0][0]]

    gathered = grid.gather(capacity, halves, plane_sums)
    computed = expert(
        expert_in[0], expert_out[0], gathered, grid.heights(CAP), grid.types(), [residual_before, *sums[0][1][:2]]
    )
    total_grad = grads.send([computed[0]])
    room, made = blank(section, capacity, residual)
    results = grid.scatter(computed, CAP, [total_grad], gates)
    next(results)
    results.send([made])
    total_grad, laid = lay_out(section, sections, to_decoder(total_grad), total_grad)
    returned = results.send([laid])
    returned_before = passed_along(returned, "section", 1)
    output = finish(section, residual, returned)
    arriving = finish(section, residual_before, returned_before, room)
    return (output[None], arriving[None], total_grad[None])


def solution(mesh):
    placed = (
        P("section", "expert", None),
        P("section", "expert", None, None),
        P("section", "expert", None),
        P("section", None),
        P("section", None),
        P("section", None, "expert"),
        P("section", "expert", None),
        P("section", "expert"),
        P("section", "expert"),
    )
    return jax.shard_map(
        local,
        mesh=mesh,
        in_specs=placed,
        out_specs=(
            P("section", "expert", None),
            P("section", "expert", None),
            P("section", "expert", None, None),
        ),
        check_vma=False,
    )
```

```python
import functools

import jax
import jax.numpy as jnp
from jax import lax
from jax.experimental import pallas as pl
from jax.experimental.pallas import tpu as pltpu
from jax.sharding import PartitionSpec as P

HD = 128
CAP = 8


def passed_along(block, axis, distance):
    devices = range(lax.axis_size(axis))
    route = [(i - distance, i) for i in devices if i - distance in devices]
    return lax.ppermute(block, axis, route)


def swapped(block):
    sections = lax.axis_size("section")
    return lax.ppermute(block, "section", [(i, (i + sections // 2) % sections) for i in range(sections)])


def to_decoder(block):
    apart = lax.axis_size("section") // 2
    return lax.ppermute(block, "section", [(i, i + apart) for i in range(apart)])


def partner(position, distance, size):
    return position ^ distance if size & (size - 1) == 0 else (position + distance) % size


class Grid:
    def __init__(self, size):
        a = 4 if size % 4 == 0 else 1
        c = 2 if (size // a) % 2 == 0 else 1
        self.sizes = (a, size // a // c, c)
        self.size = size

    def shift(self, block, by, back=False):
        sizes = self.sizes
        route = []
        for index in range(self.size):
            at = (index // (sizes[1] * sizes[2]), index // sizes[2] % sizes[1], index % sizes[2])
            to = [partner(p, d, n) for p, d, n in zip(at, by, sizes)]
            route.append((index, (to[0] * sizes[1] + to[1]) * sizes[2] + to[2]))
        if back:
            route = [(target, source) for source, target in route]
        return lax.ppermute(block, "expert", route)

    def offsets(self):
        _, nb, nc = self.sizes
        return [(b, c) for b in range(nb) for c in range(nc)]

    def heights(self, rows):
        na = self.sizes[0]
        half = rows * (na - na // 2)
        listed = []
        for b, c in self.offsets():
            listed += [half, na * rows - half] if b and c else [na * rows]
        return listed

    def types(self):
        listed = []
        for b, c in self.offsets():
            listed += [jnp.bfloat16] * 2 if b and c else [jnp.float32]
        return listed

    def gather(self, block, first=(), second=lambda own: ()):
        na, nb, nc = self.sizes
        rows = block.shape[0]
        own = join([block] + [self.shift(block, (s, 0, 0)) for s in range(1, na)], first)
        half = rows * (na - na // 2)
        pieces = {(0, 0): [own]}
        for b in range(1, nb):
            pieces[b, 0] = [self.shift(own, (0, b, 0))]
        for c in range(1, nc):
            pieces[0, c] = [self.shift(own, (0, 0, c))]
        for b in range(1, nb):
            for c in range(1, nc):
                upper, lower = halves_of(pieces[b, 0][0], pieces[0, c][0], half, second(own))
                pieces[b, c] = [self.shift(upper, (0, 0, c)), self.shift(lower, (0, b, 0))]
        return sum((pieces[k] for k in self.offsets()), [])

    def scatter(self, pieces, rows, after=(), extra=None):
        na, nb, nc = self.sizes
        half = rows * (na - na // 2)
        held, at = {}, 0
        for k in self.offsets():
            count = 2 if k[0] and k[1] else 1
            held[k] = pieces[at : at + count]
            at += count
        arrived = []
        for b in range(1, nb):
            more = [self.shift(held[b, c][0], (0, 0, c), back=True) for c in range(1, nc)]
            arrived.append((held[b, 0][0], more, 0, (0, b, 0)))
        for c in range(1, nc):
            more = [self.shift(held[b, c][1], (0, b, 0), back=True) for b in range(1, nb)]
            arrived.append((held[0, c][0], more, half, (0, 0, c)))
        halves = [add_half(piece, more, start, after) for piece, more, start, _ in arrived]
        arrived = [self.shift(piece, by, back=True) for piece, (*_, by) in zip(halves, arrived)]
        after = yield halves
        blocks = add_blocks(held[0, 0][0], arrived, rows, after)
        order = range(1, na) if extra is None else reversed(range(1, na))
        more = [self.shift(blocks[s], (s, 0, 0), back=True) for s in order]
        after = yield blocks, more
        yield add_last(blocks[0], more, after, extra)


def compiler_params():
    return pltpu.CompilerParams(vmem_limit_bytes=20 * 2**20)


def in_vmem(count):
    return [pl.BlockSpec(memory_space=pltpu.VMEM)] * count


ANYWHERE = pl.BlockSpec(memory_space=pl.ANY)
LAST = (((1,), (1,)), ((), ()))
PLAIN = (((1,), (0,)), ((), ()))


def dot(left, right, dims=PLAIN):
    return lax.dot_general(left, right, dims, preferred_element_type=jnp.float32)


def local_kernel(kernel, name, outs, args, after=(), flops=0, scalars=0, **more):
    args = list(args)
    in_specs = [pl.BlockSpec(memory_space=pltpu.SMEM)] * scalars + in_vmem(len(args) - scalars)
    count = len(args)
    body = kernel
    if after:
        args += after
        in_specs += [ANYWHERE] * len(after)

        def body(*refs):
            kernel(*refs[:count], *refs[count + len(after) :])

    moved = sum(x.size * x.dtype.itemsize for x in args[:count]) + sum(
        x.size * x.dtype.itemsize for x in outs
    )
    return pl.pallas_call(
        body,
        out_shape=tuple(outs),
        in_specs=in_specs,
        out_specs=tuple(in_vmem(len(outs))),
        compiler_params=compiler_params(),
        cost_estimate=pl.CostEstimate(flops=flops, bytes_accessed=moved, transcendentals=0),
        name=name,
        **more,
    )(*args)


def join(blocks, after=()):
    if blocks[0].shape[0] % 8:
        return jnp.concatenate(blocks, axis=0)

    def kernel(*refs):
        rows = jnp.concatenate([r[...].astype(jnp.float32) for r in refs[:-1]], axis=0)
        refs[-1][...] = rows.astype(jnp.bfloat16)

    one = jax.ShapeDtypeStruct((len(blocks) * blocks[0].shape[0], blocks[0].shape[1]), jnp.bfloat16)
    return local_kernel(kernel, "join", [one], blocks, after)[0]


def halves_of(first, second, half, after):
    if half % 16 or not after:
        return first[:half], second[half:]

    def kernel(first_ref, second_ref, upper_ref, lower_ref):
        upper_ref[...] = first_ref[:half]
        lower_ref[...] = second_ref[half:]

    width = first.shape[1]
    outs = [
        jax.ShapeDtypeStruct((half, width), first.dtype),
        jax.ShapeDtypeStruct((second.shape[0] - half, width), first.dtype),
    ]
    return local_kernel(kernel, "halves", outs, [first, second], after)


def add_half(piece, more, start, after):
    rows = more[0].shape[0]

    def add(whole, terms):
        there = whole[start : start + rows]
        for term in terms:
            there = there + term.astype(jnp.float32)
        parts = [whole[:start], there, whole[start + rows :]]
        return jnp.concatenate([p for p in parts if p.shape[0]], axis=0).astype(jnp.bfloat16)

    if rows % 16:
        return add(piece, more)

    def kernel(piece_ref, *refs):
        refs[-1][...] = add(piece_ref[...], [r[...] for r in refs[:-1]])

    one = jax.ShapeDtypeStruct(piece.shape, jnp.bfloat16)
    return local_kernel(kernel, "add_half", [one], [piece, *more], after)[0]


def add_blocks(piece, more, rows, after):
    count = piece.shape[0] // rows
    types = [jnp.float32] + [jnp.bfloat16] * (count - 1)

    def add(whole, terms):
        for term in terms:
            whole = whole + term.astype(jnp.float32)
        return [whole[s * rows : (s + 1) * rows].astype(t) for s, t in enumerate(types)]

    if rows % 8:
        return add(piece, more)

    def kernel(*refs):
        terms = [r[...] for r in refs[: 1 + len(more)]]
        for ref, block in zip(refs[1 + len(more) :], add(terms[0], terms[1:])):
            ref[...] = block

    outs = [jax.ShapeDtypeStruct((rows, piece.shape[1]), t) for t in types]
    return local_kernel(kernel, "add_blocks", outs, [piece, *more], after)


def add_last(block, more, after, extra=None):
    rows, width = block.shape
    wide = 0 if extra is None else extra.shape[1]

    def kernel(block_ref, *refs):
        total = block_ref[...]
        for ref in refs[: len(more)]:
            total = total + ref[...].astype(jnp.float32)
        refs[-1][:, :width] = total
        if wide:
            refs[-1][:, width:] = jnp.zeros((rows, wide), jnp.float32)
            refs[-1][: extra.shape[0], width:] = refs[len(more)][...]

    one = jax.ShapeDtypeStruct((rows, width + wide), jnp.float32)
    args = [block, *more] + ([extra] if wide else [])
    return local_kernel(kernel, "add_last", [one], args, after)[0]


def head_loop(heads, some_heads):
    few = next(u for u in (20, 10, 5, 4, 2, 1) if heads % u == 0)

    def step(g, carry):
        numbers = [g * few + u for u in range(few)]
        some_heads(numbers, [pl.ds(pl.multiple_of(h * HD, HD), HD) for h in numbers])
        return carry

    lax.fori_loop(0, heads // few, step, 0)


def beside(columns, width):
    return [pl.ds(pl.multiple_of(width + c.start, HD), HD) for c in columns]


def stacked(refs, columns):
    return [jnp.concatenate([r[:, c] for r in refs], axis=0) for c in columns]


def make_queries(x, gain, gate, slots, after):
    tokens, width = x.shape
    half = width // 2

    quarter = half // 2

    def kernel(x_ref, gain_ref, gate_ref, slot_ref, copy_ref, *refs):
        *q_refs, gates_ref = refs
        copy_ref[...] = x_ref[...]
        gates_ref[0:1] = gate_ref[...]
        gates_ref[1:2] = slot_ref[...].astype(jnp.float32)
        x = x_ref[...].astype(jnp.float32)
        inverse = lax.rsqrt(jnp.mean(x * x, axis=-1, keepdims=True) + 1e-06)
        for at, ref in zip((0, quarter, half), q_refs):
            columns = slice(at, at + ref.shape[1])
            x = x_ref[:, columns].astype(jnp.float32)
            ref[...] = (x * inverse * gain_ref[:, columns]).astype(jnp.bfloat16)

    part = jax.ShapeDtypeStruct((tokens, quarter), jnp.bfloat16)
    one = jax.ShapeDtypeStruct((tokens, half), jnp.bfloat16)
    same = jax.ShapeDtypeStruct((tokens, width), x.dtype)
    pair = jax.ShapeDtypeStruct((2, tokens), jnp.float32)
    return local_kernel(
        kernel,
        "queries",
        [same, part, part, one, pair],
        [x, gain, gate, slots],
        after,
    )


def cut(x, after):
    tokens, width = x.shape
    widths = [width // 4, width // 4, width // 2]

    def kernel(x_ref, *refs):
        at = 0
        for ref in refs:
            ref[...] = x_ref[:, at : at + ref.shape[1]]
            at += ref.shape[1]

    outs = [jax.ShapeDtypeStruct((tokens, n), x.dtype) for n in widths]
    return local_kernel(kernel, "cut", outs, [x], after)


def choose(section, sections, first_refs, second_ref, out_ref):
    @pl.when(section[0] >= sections // 2)
    def _():
        out_ref[...] = second_ref[...]

    @pl.when(section[0] < sections // 2)
    def _():
        at = 0
        for ref in first_refs:
            out_ref[:, at : at + ref.shape[1]] = ref[...]
            at += ref.shape[1]


def attend(section, sections, first, second, pieces, after):
    tokens, width = second.shape
    heads = width // HD
    rows = sum(p.shape[0] for p in pieces)
    count = len(pieces)

    def kernel(section, *refs):
        *first_refs, second_ref = refs[: len(first) + 1]
        refs = refs[len(first) + 1 :]
        kv_refs, (mixed_ref, p_ref, q_ref) = refs[:count], refs[count:]
        choose(section, sections, first_refs, second_ref, q_ref)

        def some_heads(numbers, columns):
            keys = stacked(kv_refs, columns)
            values = stacked(kv_refs, beside(columns, width))
            scores = [dot(k, q_ref[:, c], LAST) * HD**-0.5 for k, c in zip(keys, columns)]
            e = [jnp.exp(s - jnp.max(s, axis=0, keepdims=True)) for s in scores]
            w = [x * (1.0 / jnp.sum(x, axis=0, keepdims=True)) for x in e]
            mixed = [dot(x.astype(jnp.bfloat16).T, v) for x, v in zip(w, values)]
            for h, c, x, m in zip(numbers, columns, w, mixed):
                p_ref[h] = x
                mixed_ref[:, c] = m.astype(jnp.bfloat16)

        head_loop(heads, some_heads)

    outs = [
        jax.ShapeDtypeStruct((tokens, width), jnp.bfloat16),
        jax.ShapeDtypeStruct((heads, rows, tokens), jnp.float32),
        jax.ShapeDtypeStruct((tokens, width), jnp.bfloat16),
    ]
    args = [section.reshape(1), *first, second, *pieces]
    return local_kernel(
        kernel, "attend", outs, args, after, flops=4 * tokens * rows * width, scalars=1
    )


def gradient(section, sections, q, first, second, p, pieces, heights, types):
    tokens, width = q.shape
    heads, rows, _ = p.shape
    count = len(pieces)

    def kernel(section, q_ref, *refs):
        *first_refs, second_ref, p_ref = refs[: len(first) + 2]
        refs = refs[len(first) + 2 :]
        kv_refs, out_refs, cot_ref = refs[:count], refs[count:-1], refs[-1]
        choose(section, sections, first_refs, second_ref, cot_ref)

        def some_heads(numbers, columns):
            values = stacked(kv_refs, beside(columns, width))
            q = [q_ref[:, c] for c in columns]
            cot = [cot_ref[:, c] for c in columns]
            w = [p_ref[h] for h in numbers]
            dp = [dot(v, c, LAST) for v, c in zip(values, cot)]
            ds = [
                x * (d - jnp.sum(d * x, axis=0, keepdims=True)) * HD**-0.5 for d, x in zip(dp, w)
            ]
            upper = [x.astype(jnp.bfloat16) for x in ds]
            lower = [(x - u.astype(jnp.float32)).astype(jnp.bfloat16) for x, u in zip(ds, upper)]
            dk = [
                dot(jnp.concatenate([u, v], axis=1), jnp.concatenate([x, x], axis=0))
                for u, v, x in zip(upper, lower, q)
            ]
            dv = [dot(x.astype(jnp.bfloat16), c) for x, c in zip(w, cot)]
            for there, grads in ((columns, dk), (beside(columns, width), dv)):
                for c, g in zip(there, grads):
                    at = 0
                    for ref in out_refs:
                        ref[:, c] = g[at : at + ref.shape[0]].astype(ref.dtype)
                        at += ref.shape[0]

        head_loop(heads, some_heads)

    outs = [jax.ShapeDtypeStruct((n, 2 * width), t) for n, t in zip(heights, types)]
    return local_kernel(
        kernel,
        "gradient",
        outs,
        [section.reshape(1), q, *first, second, p, *pieces],
        flops=10 * tokens * rows * width,
        scalars=1,
        scratch_shapes=[pltpu.VMEM((tokens, width), jnp.bfloat16)],
    )


def settle(section, sections, x, first, second, norm_gain, gates, after):
    tokens, width = first.shape[0], x.shape[1]
    half = width // 2

    def kernel(section, x_ref, first_ref, second_ref, norm_ref, gate_ref, res_ref, cap_ref):
        slots = lax.broadcasted_iota(jnp.int32, (CAP, tokens), 0).astype(jnp.float32)
        onehot = jnp.where(gate_ref[1:2] == slots, 1.0, 0.0).astype(jnp.bfloat16)
        attends = jnp.full((tokens, 1), section[0], jnp.int32) >= sections // 2
        chosen = []
        for at, ref in ((0, first_ref), (half, second_ref)):
            mixed = jnp.where(attends, ref[...].astype(jnp.float32), 0.0)
            res = (x_ref[:tokens, at : at + half].astype(jnp.float32) + mixed).astype(jnp.bfloat16)
            res_ref[:, at : at + half] = res
            chosen.append(dot(onehot, res))
        squares = sum(jnp.sum(c * c, axis=-1, keepdims=True) for c in chosen)
        inverse = lax.rsqrt(squares / width + 1e-06)
        for at, c in zip((0, half), chosen):
            rows = (c * inverse * norm_ref[:, at : at + half]).astype(jnp.bfloat16)
            cap_ref[:, at : at + half] = rows

    outs = [
        jax.ShapeDtypeStruct((tokens, width), jnp.bfloat16),
        jax.ShapeDtypeStruct((CAP, width), jnp.bfloat16),
    ]
    return local_kernel(
        kernel, "settle", outs, [section.reshape(1), x, first, second, norm_gain, gates], after,
        scalars=1,
    )


def expert(w1, w2, pieces, heights, types, after):
    width, units = w1.shape
    rows = sum(heights)
    count = len(pieces)
    steps = next(s for s in (4, 2, 1) if width % (s * 128) == 0)
    step = width // steps

    def kernel(w1_ref, w2_ref, *refs):
        in_refs, out_refs = refs[:count], refs[count:]
        parts = [slice(i * step, (i + 1) * step) for i in range(steps)]
        hidden = jnp.zeros((rows, units), jnp.float32)
        for c in parts:
            hidden = hidden + dot(jnp.concatenate([r[:, c] for r in in_refs], axis=0), w1_ref[c, :])
        hidden = jax.nn.gelu(hidden).astype(jnp.bfloat16)
        for c in parts:
            y = dot(hidden, w2_ref[:, c])
            at = 0
            for ref in out_refs:
                ref[:, c] = y[at : at + ref.shape[0]].astype(ref.dtype)
                at += ref.shape[0]

    outs = [jax.ShapeDtypeStruct((n, width), t) for n, t in zip(heights, types)]
    return local_kernel(
        kernel, "expert", outs, [w1, w2, *pieces], after, flops=4 * rows * width * units
    )


def lay_out(section, sections, first, second):
    rows, width = first.shape
    half = width // 2

    def kernel(section, first_ref, second_ref, out_ref, after_ref):
        decodes = jnp.full((rows, 1), section[0]) >= sections // 2
        after_ref[...] = jnp.zeros_like(after_ref)
        for at, ref in ((0, first_ref), (half, second_ref)):
            for side in (0, 1):
                block = jnp.where(decodes, ref[:, side * half : (side + 1) * half], 0.0)
                out_ref[:, side, at : at + half] = block

    outs = [
        jax.ShapeDtypeStruct((rows, 2, width), jnp.float32),
        jax.ShapeDtypeStruct((8, HD), jnp.float32),
    ]
    return local_kernel(kernel, "lay_out", outs, [section.reshape(1), first, second], scalars=1)


def blank(section, after, like):
    def kernel(section, after_any, out_any, after_ref, zero_ref, sem):
        after_ref[...] = jnp.zeros_like(after_ref)

        @pl.when(section[0] == 0)
        def _():
            zero_ref[...] = jnp.zeros_like(zero_ref)
            copy = pltpu.make_async_copy(zero_ref, out_any, sem)
            copy.start()
            copy.wait()

    return pl.pallas_call(
        kernel,
        out_shape=(
            jax.ShapeDtypeStruct(like.shape, like.dtype),
            jax.ShapeDtypeStruct((8, HD), jnp.float32),
        ),
        in_specs=[pl.BlockSpec(memory_space=pltpu.SMEM), ANYWHERE],
        out_specs=(pl.BlockSpec(memory_space=pltpu.HBM), in_vmem(1)[0]),
        scratch_shapes=[pltpu.VMEM(like.shape, like.dtype), pltpu.SemaphoreType.DMA],
        compiler_params=compiler_params(),
        name="blank",
    )(section.reshape(1), after)


def finish(section, res, back, room=None):
    tokens, width = res.shape
    one = jax.ShapeDtypeStruct((tokens, width), jnp.bfloat16)
    step = next(s for s in (640, 512, 256, 128) if width % s == 0)
    parts = [slice(at, at + step) for at in range(0, width, step)]

    def kernel(section, res_ref, back_ref, *refs):
        out_any, out_ref, sems = refs[-3:]

        def compute():
            gate, slot = back_ref[0:1, width:], back_ref[1:2, width:]
            slots = lax.broadcasted_iota(jnp.int32, (CAP, tokens), 0).astype(jnp.float32)
            match = jnp.where(slot == slots, 1.0, 0.0)
            gate = jnp.sum(match * gate, axis=1, keepdims=True)
            onehot = jnp.concatenate([match.T] * 3, axis=1).astype(jnp.bfloat16)
            copies = []
            for i, columns in enumerate(parts):
                back = back_ref[:, columns] * gate
                high = back.astype(jnp.bfloat16).astype(jnp.float32)
                middle = (back - high).astype(jnp.bfloat16).astype(jnp.float32)
                three = jnp.concatenate([high, middle, back - high - middle], axis=0)
                moved = dot(onehot, three.astype(jnp.bfloat16))
                here = res_ref[:, columns].astype(jnp.float32)
                out_ref[:, columns] = (here + moved).astype(jnp.bfloat16)
                copy = pltpu.make_async_copy(
                    out_ref.at[:, columns], out_any.at[:, columns], sems.at[i]
                )
                copy.start()
                copies.append(copy)
            for copy in copies:
                copy.wait()

        if room is None:
            compute()
        else:
            pl.when(section[0] > 0)(compute)

    aliased = [] if room is None else [pl.BlockSpec(memory_space=pltpu.HBM)]
    return pl.pallas_call(
        kernel,
        out_shape=one,
        in_specs=[pl.BlockSpec(memory_space=pltpu.SMEM), *in_vmem(2), *aliased],
        out_specs=pl.BlockSpec(memory_space=pltpu.HBM),
        scratch_shapes=[
            pltpu.VMEM(one.shape, one.dtype),
            pltpu.SemaphoreType.DMA((len(parts),)),
        ],
        input_output_aliases={} if room is None else {3: 0},
        compiler_params=compiler_params(),
        cost_estimate=pl.CostEstimate(
            flops=50 * tokens * width, bytes_accessed=5 * tokens * width, transcendentals=0
        ),
        name="finish",
    )(section.reshape(1), res, back, *([] if room is None else [room]))


def local(
    layer_in, memory, cotangent, norm_gain, attn_gain, expert_in, expert_out, slot_index, gate_prob
):
    sections = lax.axis_size("section")
    section = lax.axis_index("section")
    decoder = section >= sections // 2
    grid = Grid(lax.axis_size("expert"))
    own_rows, _, width = memory[0].shape
    half = width // 2
    heights = grid.heights(own_rows)
    narrow = any(n % 16 for n in heights)

    first = swapped(memory[0, :, :, :half].reshape(own_rows, width))
    second = memory[0, :, :, half:].reshape(own_rows, width)
    pieces = grid.gather(jnp.where(decoder, second, first))
    current, *first, second, gates = make_queries(
        layer_in[0], attn_gain, gate_prob, slot_index, [pieces[0]]
    )
    first = [swapped(q) for q in first]
    *upstream, cot_second = cut(cotangent[0], [gates])
    upstream = [swapped(c) for c in upstream]
    if narrow:
        pieces = [jnp.concatenate(pieces, axis=0)]

    mixed, weights, queries = attend(
        section, sections, first, second, pieces, upstream
    )
    cots = (upstream, cot_second)
    if narrow:
        whole = [sum(heights)], [jnp.float32]
        (whole,) = gradient(section, sections, queries, *cots, weights, pieces, *whole)
        parts, at = [], 0
        for n, t in zip(heights, grid.types()):
            parts.append(whole[at : at + n].astype(t))
            at += n
    else:
        parts = gradient(section, sections, queries, *cots, weights, pieces, heights, grid.types())
    residual, capacity = settle(
        section, sections, current, to_decoder(mixed), mixed, norm_gain, gates, [parts[0]]
    )
    residual_before = passed_along(current if sections == 2 else residual, "section", 1)
    grads = grid.scatter(parts, own_rows)
    halves = next(grads)
    sums = []

    def plane_sums(own):
        if not sums:
            sums.append(grads.send([own]))
        return [sums[0][0][0]]

    gathered = grid.gather(capacity, halves, plane_sums)
    computed = expert(
        expert_in[0], expert_out[0], gathered, grid.heights(CAP), grid.types(), [residual_before, *sums[0][1][:2]]
    )
    total_grad = grads.send([computed[0]])
    room, made = blank(section, capacity, residual)
    results = grid.scatter(computed, CAP, [total_grad], gates)
    next(results)
    results.send([made])
    total_grad, laid = lay_out(section, sections, to_decoder(total_grad), total_grad)
    returned = results.send([laid])
    returned_before = passed_along(returned, "section", 1)
    output = finish(section, residual, returned)
    arriving = finish(section, residual_before, returned_before, room)
    return (output[None], arriving[None], total_grad[None])


def solution(mesh):
    placed = (
        P("section", "expert", None),
        P("section", "expert", None, None),
        P("section", "expert", None),
        P("section", None),
        P("section", None),
        P("section", None, "expert"),
        P("section", "expert", None),
        P("section", "expert"),
        P("section", "expert"),
    )
    return jax.shard_map(
        local,
        mesh=mesh,
        in_specs=placed,
        out_specs=(
            P("section", "expert", None),
            P("section", "expert", None),
            P("section", "expert", None, None),
        ),
        check_vma=False,
    )
```
